32 devices in a mesh: dp: 16 (over z, y, x), rep: 2 (over core).
Axes of the slice: x: 2, y: 2, z: 4, core: 2. Of those that a mesh axis runs over, the one named last changes fastest.
Arguments:
- start_deter: bfloat16 [3072, 512], P(('dp', 'rep')), may hold values from -3 to 3
- frame_mask: int32 [3072], P(('dp', 'rep')), may hold values 0 or 1
- counts: int32 [32], P(('dp', 'rep')), may hold values from 0 to 96, as said below
- route: int32 [3072], P(('dp', 'rep')), may hold values from 0 to 767, as said below
- weights_flat: bfloat16 [4194304], P('dp'), may hold values from -3 to 3
- act_embed: bfloat16 [18, 512], replicated, may hold values from -2.5 to 2.5
- gru_gain: bfloat16 [1536], replicated, may hold values from 0.5 to 1.5
- gru_bias: bfloat16 [1536], replicated, may hold values from -1.5 to 1.5
- actor_head: bfloat16 [512, 18], replicated, may hold values from -0.75 to 0.75
- critic_head: bfloat16 [512], replicated, may hold values from -0.25 to 0.25
- latent_idx: int32 [1536, 16, 32], P(('dp', 'rep')), may hold values from 0 to 31
- action_idx: int32 [1536, 16], P(('dp', 'rep')), may hold values from 0 to 17
- rewards: float32 [1536, 16], P(('dp', 'rep')), may hold values from -12 to 12
Outputs:
- loss: float32 [], replicated
- start_grad: float32 [3072, 512], P(('dp', 'rep'))
- weights_grad: float32 [4194304], P('dp')
- embed_grad: float32 [18, 512], replicated
- gain_grad: float32 [1536], replicated
- bias_grad: float32 [1536], replicated
- actor_head_grad: float32 [512, 18], replicated
- critic_head_grad: float32 [512], replicated
The draws below stay inside these ranges and needn't reach their ends.
Inputs may be any that keep to these rules, and one draw needn't show every extreme that they name: Within each index of rep, the counts of the 16 devices sum to 768, and some device holds 96. `route`: for slots below the device's count, the used slots of one rep index fill every position of every destination exactly once, and at most 12 slots of one device go to one destination, reached by some device; entries of other slots are arbitrary.
All inputs are finite; a program needn't handle non-finite values. No bound on the sum of `frame_mask` on one device may be relied on, other than what follows from the above.
Results may differ from the reference program's by a relative error of at most 0.0075.
Values may be sent and summed in bfloat16 or wider, within the bound.
A program may use at most 192 MiB of HBM per device.

```python
import jax
import jax.numpy as jnp
from jax import lax

DET = 512
LATENTS = 32
CLASSES = 32
UNITS = 512
ACTIONS = 18
HORIZON = 16
SLOT = 96
CAP = 48
PAIR = 12
STOCH = 1024
FRAMES = 3072
STARTS = 1536
PARAMS = 4194304
N_DP = 16
N_REP = 2


def shared_plan(key):
    key_one, key_two, key_three, key_four = jax.random.split(key, 4)
    half = N_DP // 2
    deltas = jax.random.randint(key_one, (N_REP, half), 0, SLOT - CAP + 1)
    deltas = deltas.at[:, 0].set(SLOT - CAP)
    paired = jnp.stack([CAP + deltas, CAP - deltas], axis=-1).reshape(N_REP, N_DP).astype(jnp.int32)
    place_perm = jax.vmap(lambda sub_key: jax.random.permutation(sub_key, N_DP))(jax.random.split(key_two, N_REP))
    group_rows = jnp.arange(N_REP)[:, None]
    counts_grid = jnp.zeros((N_REP, N_DP), jnp.int32).at[group_rows, place_perm].set(paired)
    order_perm = jax.vmap(lambda sub_key: jax.random.permutation(sub_key, N_DP))(jax.random.split(key_three, N_REP))
    ordered = counts_grid[group_rows, order_perm]
    before = jnp.cumsum(ordered, axis=1) - ordered
    offsets = jnp.zeros((N_REP, N_DP), jnp.int32).at[group_rows, order_perm].set(before)
    filler = jax.random.randint(key_four, (N_DP, N_REP, SLOT), 0, N_DP * CAP)
    return (counts_grid.T, offsets.T, filler)


def draw_counts(key, part):
    counts_grid, offsets, filler = shared_plan(key)
    return counts_grid.reshape(-1).astype(jnp.int32)


def draw_route(key, part):
    counts_grid, offsets, filler = shared_plan(key)
    slot_ids = jnp.arange(SLOT, dtype=jnp.int32)
    ranks = offsets[:, :, None] + slot_ids[None, None, :]
    target = ranks // PAIR % N_DP
    position = ranks // (PAIR * N_DP) * PAIR + ranks % PAIR
    values = jnp.where(slot_ids[None, None, :] < counts_grid[:, :, None], target * CAP + position, filler)
    return values.reshape(-1).astype(jnp.int32)


def draw_rewards(key, part):
    key = jax.random.fold_in(key, 7)
    shape = (N_DP, N_REP * CAP, HORIZON)
    ramp = 1.0 + 2.0 * jnp.arange(N_DP, dtype=jnp.float32) / max(N_DP - 1, 1)
    base = jnp.clip(jax.random.normal(key, shape, jnp.float32), -4.0, 4.0)
    return (base * ramp[:, None, None]).reshape(STARTS, HORIZON).astype(jnp.float32)


def draw_weights_flat(key, part):
    key = jax.random.fold_in(key, 11)
    pieces = [(STOCH * DET, LATENTS), (6 * DET * DET, 2 * DET), ((DET + STOCH) * UNITS, DET + STOCH), (UNITS * UNITS, UNITS), ((DET + STOCH) * UNITS, DET + STOCH), (UNITS * UNITS, UNITS)]
    scales = jnp.concatenate([jnp.full((piece_size,), fan_in ** (-0.5), jnp.float32) for piece_size, fan_in in pieces])
    base = jnp.clip(jax.random.normal(key, (PARAMS,), jnp.float32), -4.0, 4.0)
    return (base * scales).astype(jnp.bfloat16)


def touch_ends(entries, key, least, high):
    place = [jax.random.randint(jax.random.fold_in(key, axis), (), 0, length) for axis, length in enumerate(entries.shape)]
    widest = entries.shape.index(max(entries.shape))
    next_to = place[:widest] + [(place[widest] + 1) % entries.shape[widest]] + place[widest + 1:]
    return entries.at[tuple(place)].set(least).at[tuple(next_to)].set(high)


def levels(key, extent, cuts, smallest, high):
    def one(dim, blocks):
        heights = jax.random.uniform(jax.random.fold_in(jax.random.fold_in(key, 6), dim), (blocks,), jnp.float32, smallest / len(cuts), high / len(cuts))
        return jnp.repeat(jnp.exp(heights), extent[dim] // blocks).reshape((-1,) + (1,) * (len(extent) - dim - 1))

    level = one(*cuts[0])
    for cut in cuts[1:]:
        level = level * one(*cut)
    return level


def gaussian(stream_key, shape, width, reach, cuts=(), held_as=jnp.bfloat16):
    loudness = levels(stream_key, shape, cuts, -0.22, 0.18) if cuts else 1.0
    values = jax.random.normal(stream_key, shape, jnp.float32) * width * loudness
    return jnp.minimum(jnp.maximum(values, -reach), reach).astype(held_as)


def setup_inputs(seed: int = 0) -> dict:
    streams_of = jax.random.split(jax.random.key(seed), 14)
    start_deter = gaussian(streams_of[0], (FRAMES, DET), 0.5, 3.0, ((0, 32),))
    frame_mask = touch_ends((jax.random.randint(streams_of[1], (FRAMES,), 0, 4) < 3).astype(jnp.int32), jax.random.fold_in(streams_of[1], 1), 0, 1)
    counts = draw_counts(jax.random.fold_in(streams_of[13], 71), 0)
    route = draw_route(jax.random.fold_in(streams_of[13], 71), 0)
    weights_flat = draw_weights_flat(jax.random.fold_in(streams_of[13], 71), 0)
    act_embed = gaussian(streams_of[5], (ACTIONS, DET), 0.5, 2.5)
    gru_gain = jnp.clip(1.0 + 0.1 * jax.random.normal(streams_of[6], (3 * DET,), jnp.float32), 0.5, 1.5).astype(jnp.bfloat16)
    gru_bias = gaussian(streams_of[7], (3 * DET,), 0.3, 1.5)
    actor_head = gaussian(streams_of[8], (UNITS, ACTIONS), (UNITS // 8) ** -0.5, 0.75)
    critic_head = gaussian(streams_of[9], (UNITS,), UNITS ** -0.5, 0.25)
    latent_idx = touch_ends(jax.random.randint(streams_of[10], (STARTS, HORIZON, LATENTS), 0, CLASSES), jax.random.fold_in(streams_of[10], 1), 0, CLASSES - 1).astype(jnp.int32)
    action_idx = touch_ends(jax.random.randint(streams_of[11], (STARTS, HORIZON), 0, ACTIONS), jax.random.fold_in(streams_of[11], 1), 0, ACTIONS - 1).astype(jnp.int32)
    rewards = draw_rewards(jax.random.fold_in(streams_of[13], 71), 0)
    return dict(start_deter=start_deter, frame_mask=frame_mask, counts=counts, route=route, weights_flat=weights_flat, act_embed=act_embed, gru_gain=gru_gain, gru_bias=gru_bias, actor_head=actor_head, critic_head=critic_head, latent_idx=latent_idx, action_idx=action_idx, rewards=rewards)


discount = 0.99
entropy_weight = 0.1
norm_eps = 1e-05

@jax.custom_vjp
def low(v):
    return lax.optimization_barrier(v.astype(jnp.bfloat16)).astype(jnp.float32)

@jax.custom_vjp
def low_back(v):
    return v

def low_keep(v):
    return (low(v), None)

def low_pass(kept, grad):
    return (grad,)

def back_keep(v):
    return (v, None)

def back_low(kept, grad):
    return (low(grad),)
low.defvjp(low_keep, low_pass)
low_back.defvjp(back_keep, back_low)

def mat_mul(left, right):
    return jnp.dot(left, right, precision=lax.Precision.HIGHEST)

def unpack(flat):
    shapes = [(STOCH, DET), (2 * DET, 3 * DET), (DET + STOCH, UNITS), (UNITS, UNITS), (DET + STOCH, UNITS), (UNITS, UNITS)]
    pieces = []
    offset = 0
    for piece_shape in shapes:
        piece_size = piece_shape[0] * piece_shape[1]
        pieces.append(flat[offset:offset + piece_size].reshape(piece_shape))
        offset = offset + piece_size
    return tuple(pieces)

def gru_update(gru_raw, state, gain, bias):
    ln_mean = lax.optimization_barrier(jnp.mean(gru_raw, axis=-1, keepdims=True))
    centred = gru_raw - ln_mean
    inv_std = lax.rsqrt(lax.optimization_barrier(jnp.mean(centred * centred, axis=-1, keepdims=True)) + norm_eps)
    parts = centred * inv_std * gain + bias
    reset = jax.nn.sigmoid(parts[..., :DET])
    candidate = jnp.tanh(reset * parts[..., DET:2 * DET])
    update = jax.nn.sigmoid(parts[..., 2 * DET:] - 1.0)
    return update * candidate + (1.0 - update) * state

def mlp_head(features, first, second, head):
    hidden_one = low_back(mat_mul(features, first))
    active_one = low(jax.nn.elu(hidden_one))
    hidden_two = low_back(mat_mul(active_one, second))
    active_two = low(jax.nn.elu(hidden_two))
    return low_back(mat_mul(active_two, head))

def block_loss(params, start_h, latent_ids, action_ids, advantage, start_mask):
    win_z, w_gru, actor_one, actor_two, critic_one, critic_two, act_embed, gain, bias, actor_head, critic_head = params
    block = start_h.shape[0]
    latent_hot = jax.nn.one_hot(latent_ids, CLASSES, dtype=jnp.float32).reshape(block, HORIZON, STOCH)
    latent_hot = jnp.swapaxes(latent_hot, 0, 1)
    action_hot = jnp.swapaxes(jax.nn.one_hot(action_ids, ACTIONS, dtype=jnp.float32), 0, 1)

    def dyn_step(state, inputs):
        latent_now, action_now = inputs
        state_low = low(state)
        pre_act = low_back(mat_mul(latent_now, win_z) + mat_mul(action_now, act_embed))
        input_low = low(jax.nn.elu(pre_act))
        gru_raw = low_back(mat_mul(jnp.concatenate([input_low, state_low], -1), w_gru))
        return (gru_update(gru_raw, state, gain, bias), state_low)
    last_state, state_lows = lax.scan(dyn_step, start_h, (latent_hot[:-1], action_hot[:-1]))
    all_states = jnp.concatenate([state_lows, low(last_state)[None]], 0)
    rows = HORIZON * block
    features = jnp.concatenate([all_states, latent_hot], -1).reshape(rows, DET + STOCH)
    logits = mlp_head(features, actor_one, actor_two, actor_head)
    values = mlp_head(features, critic_one, critic_two, critic_head)
    adv_rows = jnp.swapaxes(advantage, 0, 1).reshape(rows)
    mask_rows = jnp.broadcast_to(start_mask[None, :], (HORIZON, block)).reshape(rows)
    action_rows = action_hot.reshape(rows, ACTIONS)
    log_probs = jax.nn.log_softmax(logits, axis=-1)
    chosen = lax.optimization_barrier(jnp.sum(log_probs * action_rows, axis=-1))
    entropy = -lax.optimization_barrier(jnp.sum(jnp.exp(log_probs) * log_probs, axis=-1))
    terms = -adv_rows * chosen - entropy_weight * entropy + 0.5 * (values - adv_rows) ** 2
    return jnp.sum(mask_rows * terms) / HORIZON

def reference(start_deter, frame_mask, counts, route, weights_flat, act_embed, gru_gain, gru_bias, actor_head, critic_head, latent_idx, action_idx, rewards):
    frame_ids = jnp.arange(FRAMES, dtype=jnp.int32)
    slot_ids = frame_ids % SLOT
    group_ids = frame_ids // SLOT % N_REP
    used = slot_ids < counts[frame_ids // SLOT]
    target = jnp.where(used, (route // CAP * N_REP + group_ids) * CAP + route % CAP, STARTS).astype(jnp.int32)
    start_mask = jnp.zeros((STARTS,), jnp.float32).at[target].set(frame_mask.astype(jnp.float32), mode='drop')
    running = jnp.zeros((STARTS,), jnp.float32)
    columns = []
    for step_index in range(HORIZON - 1, -1, -1):
        running = rewards[:, step_index] + discount * running
        columns.insert(0, running)
    returns = jnp.stack(columns, axis=1)
    weight_mask = start_mask[:, None]
    number = HORIZON * jnp.sum(start_mask)
    centre = jnp.sum(weight_mask * returns) / number
    spread = jnp.sqrt(jnp.sum(weight_mask * returns * returns) / number - centre * centre + norm_eps)
    advantage = (returns - centre) / spread
    block = CAP * N_REP
    blocks = STARTS // block

    def total(frames_h, flat, embed, gain, bias, a_head, c_head):
        start_h = jnp.zeros((STARTS, DET), jnp.float32).at[target].set(frames_h, mode='drop')
        params = unpack(flat) + (embed, gain, bias, a_head, c_head)

        def one_block(inputs):
            return block_loss(params, *inputs)
        losses = lax.map(jax.checkpoint(one_block), (start_h.reshape(blocks, block, DET), latent_idx.reshape(blocks, block, HORIZON, LATENTS), action_idx.reshape(blocks, block, HORIZON), advantage.reshape(blocks, block, HORIZON), start_mask.reshape(blocks, block)))
        return jnp.sum(losses)
    loss, pull = jax.vjp(total, start_deter.astype(jnp.float32), weights_flat.astype(jnp.float32), act_embed.astype(jnp.float32), gru_gain.astype(jnp.float32), gru_bias.astype(jnp.float32), actor_head.astype(jnp.float32), critic_head.astype(jnp.float32))
    grads = pull(jnp.ones_like(loss))
    return (loss, grads[0], grads[1], grads[2], grads[3], grads[4], grads[5], grads[6])
```

```python
import functools
from types import SimpleNamespace

import jax
import jax.numpy as jnp
from jax import lax
from jax.experimental import pallas as pl
from jax.experimental.pallas import tpu as pltpu
from jax.sharding import PartitionSpec as P

DET = 512
CLASSES = 32
LATENTS = 32
ACTIONS = 18
STOCH = 1024
GATES = 1536
WIDE = 256
META = 128
BLOCK = 192
TALL = 384
LAG_A, LAG_B, LAG_Z = 2, 4, 1

discount = 0.99
entropy_weight = 0.1
norm_eps = 1e-05

F32 = jnp.float32
BF16 = jnp.bfloat16
MESH = pl.DeviceIdType.MESH

ROW_WIN, ROW_GRU, ROW_A1, ROW_A2, ROW_C1, ROW_C2 = 0, 1024, 4096, 5632, 6144, 7680
SM_EMBED, SM_GAIN, SM_BIAS, SM_ACTOR, SM_CRITIC, SM_LOSS = 0, 48, 54, 64, 112, 114


def dot(left, right):
    return jnp.dot(left, right, preferred_element_type=F32)


def dot_t(left, right):
    return lax.dot_general(left, right, (((0,), (0,)), ((), ())), preferred_element_type=F32)


def dot_nt(left, right):
    return lax.dot_general(left, right, (((1,), (1,)), ((), ())), preferred_element_type=F32)


def elu(value):
    near = value + 0.5 * value * value
    below = jnp.where(value > -0.00390625, near, jnp.exp(jnp.minimum(value, 0.0)) - 1.0)
    return jnp.where(value > 0, value, below)


def elu_grad(value):
    return jnp.where(value > 0, 1.0, jnp.exp(jnp.minimum(value, 0.0)))


def iota(shape, dim):
    return lax.broadcasted_iota(jnp.int32, shape, dim)


def mult(value, step):
    return pl.multiple_of(value, step)


class Plan:
    def __init__(self, devices, slots, cap, horizon, flat_rows):
        self.n = devices
        self.line = devices // 4
        self.half = self.line // 2
        self.rows = flat_rows // devices
        self.slots = slots
        self.cap = cap
        self.horizon = horizon
        self.all_rows = cap * horizon
        self.step_rows = cap * (horizon - 1)
        self.lane = -(-max(2, 2 * slots // devices) // 16) * 16
        self.parts = max(1, min(4, self.rows // 2 // 32))
        self.part_rows = self.rows // 2 // self.parts
        self.items = self.half * self.parts
        self.bits = self.line.bit_length() - 1
        self.small = 8 * devices


def kernel_body(plan, names, *refs):
    r = SimpleNamespace(**dict(zip(names, refs)))
    n, line, half, rows = plan.n, plan.line, plan.half, plan.rows
    cap, horizon, parts, prow = plan.cap, plan.horizon, plan.parts, plan.part_rows
    total, steps_rows, lane = plan.all_rows, plan.step_rows, plan.lane
    items, bits = plan.items, plan.bits
    me = lax.axis_index("dp")
    core = lax.axis_index("rep")
    z = me // 4
    a_step = 1 + core
    b_step = 2 - core
    a_bit = (me // a_step) % 2
    b_bit = (me // b_step) % 2
    a_dev = me + a_step * (1 - 2 * a_bit)
    b_dev = me + b_step * (1 - 2 * b_bit)
    q = me % 4
    q_a = a_dev % 4
    q_b = b_dev % 4
    q_ab = 3 - q
    sibling = 1 - core

    def remote(src, dst, send, recv, dev, on_core=None):
        return pltpu.make_async_remote_copy(
            src_ref=src,
            dst_ref=dst,
            send_sem=send,
            recv_sem=recv,
            device_id=(dev, core if on_core is None else on_core),
            device_id_type=MESH,
        )

    barrier = pltpu.get_barrier_semaphore()

    def greet(k, carry):
        pl.semaphore_signal(barrier, inc=1, device_id=((me + k) % n, core), device_id_type=MESH)
        return carry

    lax.fori_loop(1, n, greet, 0)
    pl.semaphore_signal(barrier, inc=1, device_id=(me, sibling), device_id_type=MESH)

    full = r.full
    own_rows = pl.ds(mult(me * rows + core * (rows // 2), 16), rows // 2)
    r.narrow[...] = r.weights[pl.ds(mult(core * rows * 2, 16), rows * 2)].astype(F32)
    for c in range(4):
        full[own_rows, 128 * c : 128 * (c + 1)] = r.narrow[pl.ds(c, rows // 2, stride=4), :].astype(BF16)

    route = r.route[...].astype(F32)
    slots = plan.slots
    used_row = (iota((1, slots), 1) < r.counts[...]).astype(F32)
    target_row = jnp.floor((route + 0.5) * (1.0 / cap))
    within_row = route - cap * target_row
    eye = iota((slots, slots), 0) == iota((slots, slots), 1)
    target_col = jnp.sum(jnp.where(eye, target_row, 0.0), axis=1, keepdims=True)
    used_col = jnp.sum(jnp.where(eye, used_row, 0.0), axis=1, keepdims=True)
    earlier = iota((slots, slots), 0) < iota((slots, slots), 1)
    same = jnp.where(earlier & (target_col == target_row), used_col, 0.0)
    rank_row = jnp.sum(same, axis=0, keepdims=True)
    column_row = jnp.where(used_row > 0, target_row * lane + rank_row, -1.0)
    lanes = n * lane
    tall = min(lanes, 256)

    def each(low, high, body):
        def step(k, carry):
            body(k)
            return carry

        lax.fori_loop(low, high, step, 0)

    def to_lanes(k):
        block = pl.ds(mult(k * tall, 16), tall)
        chosen_slot = column_row == (iota((tall, slots), 0) + k * tall).astype(F32)
        picked = jnp.where(chosen_slot, 1.0, 0.0).astype(BF16)
        r.to_lane[block] = picked
        place = jnp.sum(jnp.where(chosen_slot, within_row + 1.0, 0.0), axis=1, keepdims=True)
        marked = jnp.sum(
            jnp.where(chosen_slot, r.frame_mask[...].astype(F32), 0.0), axis=1, keepdims=True
        )
        meta_lane = iota((tall, META), 1)
        meta = jnp.where(meta_lane == 0, place, jnp.where(meta_lane == 1, marked, 0.0))
        r.sent[block, :DET] = dot(picked, r.start_deter[...]).astype(BF16)
        r.sent[block, DET:] = meta.astype(BF16)

    each(0, lanes // tall, to_lanes)

    pl.semaphore_wait(barrier, n)

    def lane_rows(k):
        return pl.ds(mult(k * lane, 16), lane)

    def exchange(width, sends, recvs):
        src, dst = r.sent, r.got

        def copy(k, to, into):
            return remote(
                src.at[lane_rows(to), 0:width], dst.at[lane_rows(into), 0:width], sends.at[k], recvs.at[k], to
            )

        def begin():
            dst[lane_rows(me), 0:width] = src[lane_rows(me), 0:width]
            each(1, n, lambda k: copy(k, (me + k) % n, me).start())

        def finish():
            each(1, n, lambda k: copy(k, me, (me + n - k) % n).wait_recv())

        def drain():
            each(1, n, lambda k: copy(k, (me + k) % n, me).wait_send())

        return begin, finish, drain

    out_begin, out_finish, out_drain = exchange(DET + META, r.ex_send, r.ex_recv)
    def bit_of(value, b):
        return (value // 2**b) % 2

    def across(b):
        return me + 4 * 2**b * (1 - 2 * bit_of(z, b))

    def item_at(i):
        group = i // items
        inner = i % items
        order = inner // parts
        place = z % half
        for b in range(bits - 1):
            place = place + bit_of(order, b) * 2**b * (1 - 2 * bit_of(z, b))
        return group, order, group * half + place, inner % parts

    def full_at(shard, piece, part):
        return full.at[pl.ds(mult(shard * rows + part * (rows // 2) + piece * prow, 16), prow)]

    def gather_copy(shard, piece, send, dev):
        view = full_at(shard, piece, core)
        return remote(view, view, send, r.ag_recv.at[shard, piece], dev)

    def share_copy(shard, piece, send, part=None):
        view = full_at(shard, piece, core if part is None else part)
        return remote(view, view, send, r.sh_recv.at[shard, piece], me, sibling)

    def far_copy(piece):
        return gather_copy(me, piece, r.far_send.at[piece], across(bits - 1))

    def plane_sends(zi, piece):
        mine = zi * 4 + q
        other = zi * 4 + q_a
        return (
            gather_copy(mine, piece, r.a_send.at[zi, piece], a_dev),
            gather_copy(mine, piece, r.b_send.at[zi, piece, 0], b_dev),
            gather_copy(other, piece, r.b_send.at[zi, piece, 1], b_dev),
        )

    def line_sends(order, zi, piece):
        return [
            (order < 2**b, gather_copy(zi * 4 + q, piece, r.line_send.at[zi, piece, b], across(b)))
            for b in range(bits - 1)
        ]

    def gather_line(i):
        _, order, zi, piece = item_at(i)

        @pl.when(zi != z)
        def _():
            gather_copy(zi * 4 + q, piece, r.a_send.at[zi, piece], me).wait_recv()

        for need, copy in line_sends(order, zi, piece):
            pl.when(need)(copy.start)
        to_a, to_b, _ = plane_sends(zi, piece)
        to_a.start()
        to_b.start()
        share_copy(zi * 4 + q, piece, r.sh_send.at[zi, piece, 0]).start()

    def gather_a(i):
        _, _, zi, piece = item_at(i)
        gather_copy(zi * 4 + q_a, piece, r.a_send.at[zi, piece], me).wait_recv()
        plane_sends(zi, piece)[2].start()
        share_copy(zi * 4 + q_a, piece, r.sh_send.at[zi, piece, 1]).start()

    def gather_b(i):
        _, _, zi, piece = item_at(i)
        for k, where in ((2, q_b), (3, q_ab)):
            gather_copy(zi * 4 + where, piece, r.a_send.at[zi, piece], me).wait_recv()
            share_copy(zi * 4 + where, piece, r.sh_send.at[zi, piece, k]).start()

    def gather_shared(i):
        _, _, zi, piece = item_at(i)
        for k, where in ((0, q), (1, q_a), (2, q_b), (3, q_ab)):
            share_copy(zi * 4 + where, piece, r.sh_send.at[zi, piece, k], sibling).wait_recv()

    def gather_drain(i):
        _, order, zi, piece = item_at(i)
        for need, copy in line_sends(order, zi, piece):
            pl.when(need)(copy.wait_send)
        for copy in plane_sends(zi, piece):
            copy.wait_send()
        for k, where in ((0, q), (1, q_a), (2, q_b), (3, q_ab)):
            share_copy(zi * 4 + where, piece, r.sh_send.at[zi, piece, k]).wait_send()

    lag_a, lag_b = LAG_A, LAG_B
    all_items = 2 * items
    ticks = all_items + lag_b
    first_ticks = items + lag_b

    def gather_tick(k):
        pl.when(k < all_items)(lambda: gather_line(k))
        pl.when((k >= lag_a) & (k < all_items + lag_a))(lambda: gather_a(k - lag_a))
        pl.when((k >= lag_b) & (k < all_items + lag_b))(lambda: gather_b(k - lag_b))

    each(0, parts, lambda piece: far_copy(piece).start())
    early = min(2, first_ticks)
    each(0, early, gather_tick)
    out_begin()

    hot, hot_t, act_hot = r.hot, r.hot_t, r.act_hot
    for t in range(horizon):
        r.latent_row[:, t * cap : (t + 1) * cap] = r.latent[t].astype(F32)
        r.action_row[:, t * cap : (t + 1) * cap] = r.action[t : t + 1].astype(F32)
    latent_row = r.latent_row[...].astype(BF16)
    spread_rows = (iota((LATENTS, STOCH), 1) // CLASSES == iota((LATENTS, STOCH), 0)).astype(F32).astype(BF16)
    class_row = (iota((1, STOCH), 1) % CLASSES).astype(F32)
    latent_col = latent_row.T
    for k in range(total // 128):
        seen = dot(latent_col[128 * k : 128 * (k + 1)], spread_rows)
        hot[128 * k : 128 * (k + 1)] = jnp.where(seen == class_row, 1.0, 0.0).astype(BF16)

    def hot_t_block(k):
        block = pl.ds(mult(k * 128, 128), 128)
        first = k * 128
        spread = ((iota((128, LATENTS), 0) + first) // CLASSES == iota((128, LATENTS), 1)).astype(F32).astype(BF16)
        seen = dot(spread, latent_row)
        class_col = ((iota((128, 1), 0) + first) % CLASSES).astype(F32)
        hot_t[block] = jnp.where(seen == class_col, 1.0, 0.0).astype(BF16)

    each(0, STOCH // 128, hot_t_block)
    act_hot[...] = jnp.where(r.action_row[...] == iota((128, total), 0).astype(F32), 1.0, 0.0).T.astype(BF16)

    r.embed_pad[...] = jnp.zeros((32, DET), BF16)
    r.embed_pad[0:ACTIONS] = r.act_embed[...]
    r.head_pad[...] = jnp.zeros((128, DET), BF16)
    r.head_pad[0:ACTIONS] = r.actor_head[...]
    r.small[...] = jnp.zeros(r.small.shape, F32)

    each(early, first_ticks, gather_tick)

    out_finish()
    r.start[...] = jnp.zeros((128, DET + META), F32)

    def from_lanes(k):
        block = pl.ds(mult(k * tall, 16), tall)
        got = r.got[block]
        put = jnp.where(got[:, DET : DET + 1].astype(F32) == (iota((tall, 128), 1) + 1).astype(F32), 1.0, 0.0).astype(BF16)
        r.placing[block] = put
        r.start[...] += dot_t(put, got)

    each(0, lanes // tall, from_lanes)
    start = r.start
    states_ref = r.states
    states_ref[0:cap] = start[0:cap, 0:DET]
    mask = start[0:cap, DET + 1 : DET + 2]
    eye = iota((cap, cap), 0) == iota((cap, cap), 1)
    mask_row = jnp.sum(jnp.where(eye, mask, 0.0), axis=0, keepdims=True)
    adv = r.adv
    running = jnp.zeros((1, cap), F32)
    sum_one = jnp.zeros((1, cap), F32)
    sum_two = jnp.zeros((1, cap), F32)
    for t in range(horizon - 1, -1, -1):
        running = r.rewards[t : t + 1] + discount * running
        sum_one = sum_one + mask_row * running
        sum_two = sum_two + mask_row * running * running
        r.returns[:, t * cap : (t + 1) * cap] = running
        r.weight_row[:, t * cap : (t + 1) * cap] = mask_row * (1.0 / horizon)
    tile_lane = iota((8, 128), 1)

    def total_of(value):
        return jnp.sum(value, axis=1, keepdims=True)

    sums = jnp.where(
        tile_lane == 0,
        total_of(sum_one),
        jnp.where(tile_lane == 1, total_of(sum_two), jnp.where(tile_lane == 2, horizon * total_of(mask_row), 0.0)),
    )
    moments, pair = r.moments, r.pair
    pair[0] = sums
    swap = remote(pair.at[0], pair.at[1], r.pair_sem.at[0], r.pair_sem.at[1], me, sibling)
    swap.start()
    each(0, items, gather_shared)
    swap.wait()
    moments[me] = pair[0] + pair[1]

    def moments_copy(k):
        peer = (me + k) % n
        return remote(moments.at[me], moments.at[me], r.mo_send.at[k], r.mo_recv.at[k], peer)

    def moments_landing(k):
        peer = (me + n - k) % n
        return remote(moments.at[peer], moments.at[peer], r.mo_send.at[k], r.mo_recv.at[k], peer)

    each(1, n, lambda k: moments_copy(k).start())

    shuffle = r.shuffle
    row_i = iota((TALL, TALL), 0)
    shuffle[...] = jnp.where(
        iota((TALL, TALL), 1) == 3 * (row_i % 128) + row_i // 128, 1.0, 0.0
    ).astype(BF16)
    w_gru = r.w_gru
    for j in range(8):
        block = full[ROW_GRU + TALL * j : ROW_GRU + TALL * (j + 1)]
        sorted_rows = dot(shuffle[...], block).astype(BF16)
        for k in range(3):
            w_gru[128 * j : 128 * (j + 1), DET * k : DET * (k + 1)] = sorted_rows[128 * k : 128 * (k + 1)]
    each(0, items, gather_drain)
    each(0, parts, lambda piece: pl.when(z < half)(far_copy(piece).wait_send))
    w_back = full.at[ROW_GRU : ROW_GRU + GATES]
    for j in range(4):
        for k in range(3):
            w_back[DET * k : DET * (k + 1), 128 * j : 128 * (j + 1)] = w_gru[
                DET + 128 * j : DET + 128 * (j + 1), DET * k : DET * (k + 1)
            ].T

    pre, inputs, raw = r.pre, r.inputs, r.raw
    low, work = r.low, r.work
    a_one_at, a_two_at, g_one, g_two = 0, 2 * DET, 4 * DET, 6 * DET
    p_low = GATES
    inputs[steps_rows:total] = jnp.zeros((total - steps_rows, DET), BF16)
    pre_block = 5 * cap

    def pre_step(k):
        block = pl.ds(mult(k * pre_block, 16), pre_block)
        value = dot(hot[block], full[ROW_WIN : ROW_WIN + STOCH])
        value = value + dot(act_hot[block][:, 0:32], r.embed_pad[...])
        pre[block] = value
        active = elu(value).astype(BF16)
        inputs[block] = active
        raw[block] = dot(active, w_gru[0:DET])
        gather_tick(first_ticks + k)

    pre_blocks = (horizon - 1) // 5
    each(0, pre_blocks, pre_step)

    def as_row(ref):
        value = ref[...].astype(F32)
        return jnp.concatenate([value[k : k + 1] for k in range(ref.shape[0])], axis=-1)

    gain = as_row(r.gain)
    bias = as_row(r.bias)
    update_ref, inv_ref = r.update, r.inv

    def forward_step(t):
        block = pl.ds(mult(t * cap, 16), cap)
        state = states_ref[block]
        state_low = state.astype(BF16)
        low[block] = state_low
        gru_raw = raw[block] + dot(state_low, w_gru[DET:])
        centred = gru_raw - jnp.mean(gru_raw, axis=-1, keepdims=True)
        inv_std = lax.rsqrt(jnp.mean(centred * centred, axis=-1, keepdims=True) + norm_eps)
        normed = centred * inv_std
        raw[block] = normed
        inv_ref[block] = jnp.broadcast_to(inv_std, (cap, 128))
        mixed = normed * gain + bias
        reset = jax.nn.sigmoid(mixed[:, :DET])
        candidate = jnp.tanh(reset * mixed[:, DET : 2 * DET])
        update = jax.nn.sigmoid(mixed[:, 2 * DET :] - 1.0)
        update_ref[block] = update
        states_ref[pl.ds(mult(t * cap + cap, 16), cap)] = update * candidate + (1.0 - update) * state
        pl.when(t % 3 == 2)(lambda: gather_tick(first_ticks + pre_blocks + t // 3))

    each(0, horizon - 1, forward_step)
    done_ticks = first_ticks + pre_blocks + (horizon - 1) // 3
    each(done_ticks, max(ticks, done_ticks), gather_tick)
    low[steps_rows:total] = states_ref[steps_rows:total].astype(BF16)
    each(items, 2 * items, gather_shared)
    each(items, 2 * items, gather_drain)
    each(0, parts, lambda piece: pl.when(z >= half)(far_copy(piece).wait_send))

    each(1, n, lambda k: moments_landing(k).wait_recv())
    sums = moments[0]
    for k in range(1, n):
        sums = sums + moments[k]
    centre = sums[0:1, 0:1] / sums[0:1, 2:3]
    spread = jnp.sqrt(sums[0:1, 1:2] / sums[0:1, 2:3] - centre * centre + norm_eps)
    per_row = jnp.concatenate(
        [(r.returns[...] - centre) / spread, r.weight_row[...], jnp.zeros((126, total), F32)], axis=0
    ).T
    adv[...] = per_row

    grads = r.grads

    def keep_grads(first, value):
        for c in range(4):
            grads[c, pl.ds(first, value.shape[0])] = value[:, 128 * c : 128 * (c + 1)]

    def load_grads(block):
        return jnp.concatenate([grads[c, block] for c in range(4)], axis=-1)

    def grad_rows(local, part, piece):
        return pl.ds(mult(local * rows + part * (rows // 2) + piece * prow, 16), prow)

    def store_grads(block, value):
        for c in range(4):
            grads[c, block] = value[:, 128 * c : 128 * (c + 1)]

    pair_in, b_in, a_in, z_in = r.pair_in, r.b_in, r.a_in, r.z_in

    class Reducer:
        def __init__(self, group):
            self.group = group
            self.turn = half // 2 if group == 0 else 0

        def target(self, i):
            return (i // parts + self.turn) % half, i % parts

        def sem(self, array, *at):
            return array.at[(self.group,) + at]

        def out_rows(self, t, offset, piece, count):
            return pl.ds(mult(ROW_A1 + t * 4 * rows + offset + piece * count * prow, 16), count * prow)

        def in_rows(self, t, piece, count):
            return pl.ds(mult((t * parts + piece) * count * prow, 16), count * prow)

        def pair_copy(self, t, piece):
            return remote(
                full.at[self.out_rows(t, 0, piece, 4)],
                pair_in.at[self.in_rows(t, piece, 4)],
                self.sem(r.pair_s, t, piece),
                self.sem(r.pair_r, t, piece),
                me,
                sibling,
            )

        def b_copy(self, t, piece):
            return remote(
                full.at[self.out_rows(t, 2 * rows, piece, 2)],
                b_in.at[self.group, self.in_rows(t, piece, 2)],
                self.sem(r.b_s, t, piece),
                self.sem(r.b_r, t, piece),
                b_dev,
            )

        def a_copy(self, t, piece):
            return remote(
                full.at[self.out_rows(t, 3 * rows, piece, 1)],
                a_in.at[self.group, self.in_rows(t, piece, 1)],
                self.sem(r.a_s, t, piece),
                self.sem(r.a_r, t, piece),
                a_dev,
            )

        def z_slot(self, b, t):
            return sum(half // 2 ** (k + 1) for k in range(b)) + t // 2 ** (b + 1)

        def z_copy(self, b, t, piece):
            slot = self.z_slot(b, t)
            return remote(
                full.at[self.out_rows(t, 3 * rows + rows // 2, piece, 1)],
                z_in.at[self.group, self.in_rows(slot, piece, 1)],
                self.sem(r.z_s, t, piece),
                self.sem(r.z_r, slot, piece),
                across(b),
            )

        def holds(self, b, t):
            return (z - t - self.group * half) % 2**b == 0

        def differs(self, b, t):
            return bit_of(z, b) != bit_of(t + self.group * half, b)

        def fin_rows(self, piece, part):
            return pl.ds(mult((part * (rows // 2) + piece * prow) * 4, 16), prow * 4)

        def fin_copy(self, piece, part=None):
            block = self.fin_rows(piece, core if part is None else part)
            return remote(
                r.weights_grad.at[block], r.weights_grad.at[block], r.fin_s.at[piece], r.fin_r.at[piece], me, sibling
            )

        def load(self, t, piece, a):
            if self.group == 0:
                return load_grads(grad_rows(t * 4 + a * a_step + b_bit * b_step, core, piece))
            return r.kept[(t * parts + piece) * 2 + a]

        def store(self, t, piece, a, value):
            if self.group == 0:
                store_grads(grad_rows(t * 4 + a * a_step + b_bit * b_step, core, piece), value)
            else:
                r.kept[(t * parts + piece) * 2 + a] = value

        def to_pair(self, i):
            t, piece = self.target(i)
            for k in range(4):
                block = pl.ds(mult(ROW_A1 + t * 4 * rows + (piece * 4 + k) * prow, 16), prow)
                full[block] = load_grads(grad_rows(t * 4 + k, sibling, piece)).astype(BF16)
            self.pair_copy(t, piece).start()

        def to_b(self, i):
            t, piece = self.target(i)
            self.pair_copy(t, piece).wait_recv()

            def both_cores(where):
                spot = pl.ds(mult(((t * parts + piece) * 4 + where) * prow, 16), prow)
                return load_grads(grad_rows(t * 4 + where, core, piece)) + pair_in[spot].astype(F32)

            for a in range(2):
                block = pl.ds(mult(ROW_A1 + t * 4 * rows + 2 * rows + (piece * 2 + a) * prow, 16), prow)
                full[block] = both_cores(a * a_step + (1 - b_bit) * b_step).astype(BF16)
            self.b_copy(t, piece).start()
            for a in range(2):
                self.store(t, piece, a, both_cores(a * a_step + b_bit * b_step))

        def b_part(self, t, piece, a):
            spot = pl.ds(mult(((t * parts + piece) * 2 + a) * prow, 16), prow)
            return b_in[self.group, spot].astype(F32)

        def to_a(self, i):
            t, piece = self.target(i)
            self.b_copy(t, piece).wait_recv()
            other = 1 - a_bit
            full[self.out_rows(t, 3 * rows, piece, 1)] = (
                self.load(t, piece, other) + self.b_part(t, piece, other)
            ).astype(BF16)
            self.a_copy(t, piece).start()
            self.store(t, piece, a_bit, self.load(t, piece, a_bit) + self.b_part(t, piece, a_bit))

        def to_plane(self, b, i):
            t, piece = self.target(i)

            @pl.when(self.holds(b, t))
            def _():
                if b == 0:
                    self.a_copy(t, piece).wait_recv()
                    came = a_in[self.group, self.in_rows(t, piece, 1)]
                else:
                    self.z_copy(b - 1, t, piece).wait_recv()
                    came = z_in[self.group, self.in_rows(self.z_slot(b - 1, t), piece, 1)]
                value = self.load(t, piece, a_bit) + came.astype(F32)
                if b == bits:
                    first = mult((core * (rows // 2) + piece * prow) * 4, 16)
                    for c in range(4):
                        r.weights_grad[pl.ds(first + c, prow, stride=4), :] = value[:, 128 * c : 128 * (c + 1)]
                    self.fin_copy(piece).start()
                else:

                    @pl.when(self.differs(b, t))
                    def _():
                        full[self.out_rows(t, 3 * rows + rows // 2, piece, 1)] = value.astype(BF16)
                        self.z_copy(b, t, piece).start()

                    pl.when(~self.differs(b, t))(lambda: self.store(t, piece, a_bit, value))

        def drain_early(self, i):
            t, piece = self.target(i)
            self.pair_copy(t, piece).wait_send()
            self.b_copy(t, piece).wait_send()

        def drain(self, i):
            t, piece = self.target(i)
            self.a_copy(t, piece).wait_send()
            for b in range(bits):
                pl.when(self.holds(b, t) & self.differs(b, t))(self.z_copy(b, t, piece).wait_send)

            @pl.when(self.holds(bits, t))
            def _():
                self.fin_copy(piece).wait_send()
                self.fin_copy(piece, sibling).wait_recv()

        def tick(self, k):
            pl.when((k >= 0) & (k < items))(lambda: self.to_a(k))
            for b in range(bits + 1):
                j = k - LAG_Z * (b + 1)
                pl.when((j >= 0) & (j < items))(lambda b=b, j=j: self.to_plane(b, j))

    rs_ticks = items + LAG_Z * (bits + 1)
    heads_rs, gru_rs = Reducer(1), Reducer(0)
    net_items = items // 2

    out_grads, state_grads = r.out_grads, r.state_grads
    r.loss_acc[...] = jnp.zeros((BLOCK, 128), F32)
    critic_row = as_row(r.critic_head)
    lane_id = iota((BLOCK, 128), 1)

    def net_rows(side):
        return (ROW_A1, ROW_A2) if side == 0 else (ROW_C1, ROW_C2)

    def net_cols(base, side):
        return slice(base + side * DET, base + (side + 1) * DET)

    def net_step(k, side):
        first, second = net_rows(side)
        block = pl.ds(mult(k * BLOCK, 64), BLOCK)
        one = dot(low[block], full[first : first + DET]) + dot(hot[block], full[first + DET : first + DET + STOCH])
        one_low = elu(one).astype(BF16)
        work[block, net_cols(a_one_at, side)] = one_low
        two = dot(one_low, full[second : second + DET])
        two_low = elu(two).astype(BF16)
        work[block, net_cols(a_two_at, side)] = two_low
        advantage = adv[block][:, 0:1]
        weight = adv[block][:, 1:2]
        if side == 0:
            real = lane_id < ACTIONS
            logits = jnp.where(real, dot_nt(two_low, r.head_pad[...]), -1e30)
            shifted = logits - jnp.max(logits, axis=-1, keepdims=True)
            powers = jnp.where(real, jnp.exp(shifted), 0.0)
            norm = jnp.sum(powers, axis=-1, keepdims=True)
            log_probs = jnp.where(real, shifted - jnp.log(norm), 0.0)
            probs = powers / norm
            taken = act_hot[block].astype(F32)
            chosen = jnp.sum(taken * log_probs, axis=-1, keepdims=True)
            entropy = -jnp.sum(probs * log_probs, axis=-1, keepdims=True)
            r.loss_acc[...] += weight * (-advantage * chosen - entropy_weight * entropy)
            grad_logits = weight * (
                -advantage * (taken - probs) + entropy_weight * probs * (log_probs + entropy)
            )
            both = grad_logits.astype(BF16)
            out_grads[block] = both
            back = dot(both, r.head_pad[...])
        else:
            value = jnp.sum(two_low.astype(F32) * critic_row, axis=-1, keepdims=True)
            gap = value - advantage
            r.loss_acc[...] += weight * (0.5 * gap * gap)
            value_low = (weight * gap).astype(BF16).astype(F32)
            out_grads[block] = jnp.where(lane_id == ACTIONS, value_low, out_grads[block].astype(F32)).astype(BF16)
            back = value_low * critic_row
        back_low = (back * elu_grad(two)).astype(BF16)
        work[block, net_cols(g_two, side)] = back_low
        low_one = (dot_nt(back_low, full[second : second + DET]) * elu_grad(one)).astype(BF16)
        work[block, net_cols(g_one, side)] = low_one
        state_part = dot_nt(low_one, full[first : first + DET])
        if side == 0:
            state_grads[block] = state_part
        else:
            state_grads[block] += state_part

    def net_grads(side):
        base = side * 2048
        for j in range(2):
            part = slice(j * WIDE, (j + 1) * WIDE)
            keep_grads(base + j * WIDE, dot_t(low[:, part], work[:, net_cols(g_one, side)]))
            at = a_one_at + side * DET + j * WIDE
            keep_grads(base + GATES + j * WIDE, dot_t(work[:, at : at + WIDE], work[:, net_cols(g_two, side)]))

        def latent_part(k):
            part = pl.ds(mult(k * WIDE, WIDE), WIDE)
            keep_grads(mult(base + DET + k * WIDE, WIDE), dot(hot_t[part], work[:, net_cols(g_one, side)]))

        each(0, STOCH // WIDE, latent_part)

    blocks = total // BLOCK
    each(0, blocks, lambda k: net_step(k, 0))
    net_grads(0)
    each(0, net_items, heads_rs.to_pair)
    net_step(0, 1)
    each(0, net_items, heads_rs.to_b)
    each(1, blocks, lambda k: net_step(k, 1))
    net_grads(1)
    each(net_items, items, heads_rs.to_pair)

    small = r.small
    head_grad = dot_t(out_grads[...], work[:, a_two_at : a_two_at + 2 * DET])
    small[SM_ACTOR : SM_ACTOR + 24] = head_grad[0:24, 0:WIDE]
    small[SM_ACTOR + 24 : SM_ACTOR + 48] = head_grad[0:24, WIDE:DET]
    small[SM_CRITIC : SM_CRITIC + 1] = head_grad[ACTIONS : ACTIONS + 1, DET : DET + WIDE]
    small[SM_CRITIC + 1 : SM_CRITIC + 2] = head_grad[ACTIONS : ACTIONS + 1, DET + WIDE :]
    small[SM_LOSS : SM_LOSS + 1, 0:128] = jnp.sum(r.loss_acc[...], axis=0, keepdims=True)

    scan_b = 2

    def heads_b(index):
        share = -(-net_items // scan_b)
        low_item = net_items + index * share
        each(low_item, jnp.minimum(low_item + share, items), heads_rs.to_b)

    gain_acc, bias_acc = r.gain_acc, r.bias_acc
    gain_acc[...] = jnp.zeros((8, GATES), F32)
    bias_acc[...] = jnp.zeros((8, GATES), F32)
    carry_ref = r.carry
    carry_ref[...] = state_grads[steps_rows:total]
    work[steps_rows:total, 0 : 4 * DET] = jnp.zeros((total - steps_rows, 4 * DET), BF16)
    gain_mid, bias_mid = gain[:, DET : 2 * DET], bias[:, DET : 2 * DET]

    def fold(value):
        out = value[0:8]
        for k in range(1, cap // 8):
            out = out + value[8 * k : 8 * (k + 1)]
        return out

    def backward_step(index):
        t = horizon - 2 - index
        block = pl.ds(mult(t * cap, 16), cap)
        carry = carry_ref[...]
        normed = raw[block]
        inv_std = inv_ref[block][:, 0:1]
        reset = jax.nn.sigmoid(normed[:, :DET] * gain[:, :DET] + bias[:, :DET])
        update = update_ref[block]
        state = states_ref[block]
        middle = normed[:, DET : 2 * DET] * gain_mid + bias_mid
        candidate = jnp.tanh(reset * middle)
        inner = carry * update * (1.0 - candidate * candidate)
        part = jnp.concatenate(
            [
                inner * middle * reset * (1.0 - reset),
                inner * reset,
                carry * (candidate - state) * update * (1.0 - update),
            ],
            axis=-1,
        )
        gain_acc[...] += fold(part * normed)
        bias_acc[...] += fold(part)
        normed_grad = part * gain
        raw_grad = inv_std * (
            normed_grad
            - jnp.mean(normed_grad, axis=-1, keepdims=True)
            - normed * jnp.mean(normed_grad * normed, axis=-1, keepdims=True)
        )
        grad_low = raw_grad.astype(BF16)
        work[block, 0:GATES] = grad_low
        carry_ref[...] = carry * (1.0 - update) + dot(grad_low, w_back[...]) + state_grads[block]
        pl.when(index < scan_b)(lambda: heads_b(index))
        pl.when((index >= scan_b) & (index % 2 == 0))(lambda: heads_rs.tick((index - scan_b) // 2))

    each(0, horizon - 1, backward_step)

    back_begin, back_finish, back_drain = exchange(DET, r.bk_send, r.bk_recv)
    out_drain()
    start_grads = carry_ref[...].astype(BF16)

    def back_lanes(k):
        block = pl.ds(mult(k * tall, 16), tall)
        r.sent[block, :DET] = dot(r.placing[block][:, 0:cap], start_grads).astype(BF16)

    each(0, lanes // tall, back_lanes)
    back_begin()

    each(0, items, heads_rs.drain_early)
    pl.semaphore_signal(r.credit, inc=1, device_id=(me, sibling), device_id_type=MESH)
    scan_ticks = (horizon - 1 - scan_b + 1) // 2
    tail_ticks = max(rs_ticks - scan_ticks, 0)

    def gru_part(j):
        source = inputs if j < 2 else low
        part = slice((j % 2) * WIDE, (j % 2 + 1) * WIDE)
        for k in range(3):
            value = dot_t(source[:, part], work[:, DET * k : DET * (k + 1)])
            for c in range(4):
                grads[c, pl.ds(ROW_GRU + k + 768 * j, WIDE, stride=3), :] = value[:, 128 * c : 128 * (c + 1)]

    def heads_ticks(low_share, high_share):
        each(
            scan_ticks + tail_ticks * low_share // 4,
            scan_ticks + tail_ticks * high_share // 4,
            heads_rs.tick,
        )

    for j in (3, 2, 1):
        gru_part(j)
    pl.semaphore_wait(r.credit, 1)
    each(0, net_items, gru_rs.to_pair)

    def pre_back(k):
        block = pl.ds(mult(k * pre_block, 16), pre_block)
        value = dot_nt(work[block, 0:GATES], w_gru[0:DET])
        work[block, p_low : p_low + DET] = (value * elu_grad(pre[block])).astype(BF16)

    each(0, pre_blocks, pre_back)
    each(0, net_items, gru_rs.to_b)
    heads_ticks(0, 1)
    gru_part(0)

    def win_part(k):
        part = pl.ds(mult(k * WIDE, WIDE), WIDE)
        keep_grads(mult(k * WIDE, WIDE), dot(hot_t[part], work[:, p_low : p_low + DET]))

    each(0, STOCH // WIDE, win_part)
    each(net_items, items, gru_rs.to_pair)
    heads_ticks(1, 2)
    each(net_items, items, gru_rs.to_b)
    embed_grad = dot_t(act_hot[...], work[:, p_low : p_low + DET])
    small[SM_EMBED : SM_EMBED + 24] = embed_grad[0:24, 0:WIDE]
    small[SM_EMBED + 24 : SM_EMBED + 48] = embed_grad[0:24, WIDE:DET]
    gain_sum = jnp.sum(gain_acc[...], axis=0, keepdims=True)
    bias_sum = jnp.sum(bias_acc[...], axis=0, keepdims=True)
    for k in range(GATES // WIDE):
        small[SM_GAIN + k : SM_GAIN + k + 1] = gain_sum[:, k * WIDE : (k + 1) * WIDE]
        small[SM_BIAS + k : SM_BIAS + k + 1] = bias_sum[:, k * WIDE : (k + 1) * WIDE]

    small_in, scattered = r.small_in, r.scattered
    summed = small_in
    swap_small = remote(small, small_in, r.pair_sem.at[2], r.pair_sem.at[3], me, sibling)
    swap_small.start()
    heads_ticks(2, 4)
    each(0, items, heads_rs.drain)
    each(0, 2, gru_rs.tick)
    swap_small.wait()
    small_sum = small
    small_sum[...] = small[...] + small_in[...]

    def eight(k):
        return pl.ds(mult(k * 8, 8), 8)

    def scatter_copy(k):
        peer = (me + k) % n
        return remote(small_sum.at[eight(peer)], scattered.at[me], r.sc_send.at[k], r.sc_recv.at[k], peer)

    def scatter_landing(k):
        peer = (me + n - k) % n
        return remote(small_sum.at[eight(me)], scattered.at[peer], r.sc_send.at[k], r.sc_recv.at[k], peer)

    def summed_copy(k):
        peer = (me + k) % n
        return remote(summed.at[eight(me)], summed.at[eight(me)], r.sm_send.at[k], r.sm_recv.at[k], peer)

    def summed_landing(k):
        peer = (me + n - k) % n
        return remote(summed.at[eight(peer)], summed.at[eight(peer)], r.sm_send.at[k], r.sm_recv.at[k], peer)

    scattered[me] = small_sum[eight(me)]
    each(1, n, lambda k: scatter_copy(k).start())
    each(2, 4, gru_rs.tick)
    each(1, n, lambda k: scatter_landing(k).wait_recv())
    block_sum = scattered[0]
    for k in range(1, n):
        block_sum = block_sum + scattered[k]
    summed[eight(me)] = block_sum
    each(1, n, lambda k: summed_copy(k).start())
    each(4, rs_ticks, gru_rs.tick)

    back_finish()
    r.start_grad[...] = jnp.zeros((slots, DET), F32)

    def frames(k):
        block = pl.ds(mult(k * tall, 16), tall)
        r.start_grad[...] += dot_t(r.to_lane[block], r.got[block][:, 0:DET])

    each(0, lanes // tall, frames)
    each(1, n, lambda k: summed_landing(k).wait_recv())
    r.loss[...] = summed[SM_LOSS : SM_LOSS + 1, 0:1]
    r.embed_grad[:, 0:WIDE] = summed[SM_EMBED : SM_EMBED + ACTIONS]
    r.embed_grad[:, WIDE:DET] = summed[SM_EMBED + 24 : SM_EMBED + 24 + ACTIONS]
    for k in range(GATES // WIDE):
        for h in range(2):
            lanes_of = slice(h * 128, (h + 1) * 128)
            r.gain_grad[2 * k + h : 2 * k + h + 1] = summed[SM_GAIN + k : SM_GAIN + k + 1, lanes_of]
            r.bias_grad[2 * k + h : 2 * k + h + 1] = summed[SM_BIAS + k : SM_BIAS + k + 1, lanes_of]
    for k in range(2):
        for h in range(2):
            lanes_of = slice(h * 128, (h + 1) * 128)
            r.critic_grad[2 * k + h : 2 * k + h + 1] = summed[SM_CRITIC + k : SM_CRITIC + k + 1, lanes_of]
    r.actor_grad[:, 0:WIDE] = summed[SM_ACTOR : SM_ACTOR + ACTIONS]
    r.actor_grad[:, WIDE:DET] = summed[SM_ACTOR + 24 : SM_ACTOR + 24 + ACTIONS]
    each(0, items, gru_rs.drain_early)
    each(0, items, gru_rs.drain)

    back_drain()
    each(1, n, lambda k: moments_copy(k).wait_send())
    each(1, n, lambda k: scatter_copy(k).wait_send())
    each(1, n, lambda k: summed_copy(k).wait_send())


def on_device(
    start_deter,
    frame_mask,
    counts,
    route,
    weights_flat,
    act_embed,
    gru_gain,
    gru_bias,
    actor_head,
    critic_head,
    latent_idx,
    action_idx,
    rewards,
):
    n = lax.axis_size("dp")
    slots = start_deter.shape[0]
    cap, horizon = action_idx.shape
    shard = weights_flat.shape[0]
    plan = Plan(n, slots, cap, horizon, shard * n // DET)
    total, steps_rows, lanes = plan.all_rows, plan.step_rows, n * plan.lane
    line, half, parts, prow, items = plan.line, plan.half, plan.parts, plan.part_rows, plan.items
    inputs = dict(
        start_deter=start_deter,
        frame_mask=frame_mask.reshape(1, slots),
        counts=counts.reshape(1, 1),
        route=route.reshape(1, slots),
        weights=weights_flat.reshape(plan.rows * 4, 128),
        act_embed=act_embed,
        gain=gru_gain.reshape(GATES // 128, 128),
        bias=gru_bias.reshape(GATES // 128, 128),
        actor_head=actor_head.T,
        critic_head=critic_head.reshape(DET // 128, 128),
        latent=jnp.transpose(latent_idx, (1, 2, 0)),
        action=action_idx.T,
        rewards=rewards.T,
    )
    outputs = dict(
        loss=(1, 1),
        start_grad=(slots, DET),
        weights_grad=(plan.rows * 4, 128),
        embed_grad=(ACTIONS, DET),
        gain_grad=(GATES // 128, 128),
        bias_grad=(GATES // 128, 128),
        actor_grad=(ACTIONS, DET),
        critic_grad=(DET // 128, 128),
    )
    group_rows = half * 4 * plan.rows
    half_rows = group_rows // 2
    scratch = dict(
        narrow=((plan.rows * 2, 128), F32),
        latent_row=((LATENTS, total), F32),
        action_row=((1, total), F32),
        returns=((1, total), F32),
        weight_row=((1, total), F32),
        kept=((2 * items, prow, DET), F32),
        full=((n * plan.rows, DET), BF16),
        start=((128, DET + META), F32),
        to_lane=((lanes, slots), BF16),
        sent=((lanes, DET + META), BF16),
        got=((lanes, DET + META), BF16),
        placing=((lanes, 128), BF16),
        hot=((total, STOCH), BF16),
        hot_t=((STOCH, total), BF16),
        act_hot=((total, 128), BF16),
        embed_pad=((32, DET), BF16),
        head_pad=((128, DET), BF16),
        small=((plan.small, WIDE), F32),
        small_in=((plan.small, WIDE), F32),
        scattered=((n, 8, WIDE), F32),
        states=((total, DET), F32),
        adv=((total, 128), F32),
        pair=((2, 8, 128), F32),
        moments=((n, 8, 128), F32),
        shuffle=((TALL, TALL), BF16),
        w_gru=((STOCH, GATES), BF16),
        pre=((steps_rows, DET), F32),
        inputs=((total, DET), BF16),
        work=((total, 8 * DET), BF16),
        raw=((steps_rows, GATES), F32),
        low=((total, DET), BF16),
        update=((steps_rows, DET), F32),
        inv=((steps_rows, 128), F32),
        out_grads=((total, 128), BF16),
        state_grads=((total, DET), F32),
        loss_acc=((BLOCK, 128), F32),
        grads=((4, group_rows, 128), F32),
        pair_in=((half_rows, DET), BF16),
        b_in=((2, half_rows // 2, DET), BF16),
        a_in=((2, half_rows // 4, DET), BF16),
        z_in=((2, half_rows // 4, DET), BF16),
        gain_acc=((8, GATES), F32),
        bias_acc=((8, GATES), F32),
        carry=((cap, DET), F32),
    )
    semaphores = dict(
        ex_send=(n,),
        ex_recv=(n,),
        bk_send=(n,),
        bk_recv=(n,),
        mo_send=(n,),
        mo_recv=(n,),
        sc_send=(n,),
        sc_recv=(n,),
        sm_send=(n,),
        sm_recv=(n,),
        pair_sem=(4,),
        ag_recv=(n, parts),
        sh_recv=(n, parts),
        far_send=(parts,),
        line_send=(line, parts, max(plan.bits - 1, 1)),
        a_send=(line, parts),
        b_send=(line, parts, 2),
        sh_send=(line, parts, 4),
        pair_s=(2, half, parts),
        pair_r=(2, half, parts),
        b_s=(2, half, parts),
        b_r=(2, half, parts),
        a_s=(2, half, parts),
        a_r=(2, half, parts),
        z_s=(2, half, parts),
        z_r=(2, half, parts),
        fin_s=(parts,),
        fin_r=(parts,),
    )
    names = list(inputs) + list(outputs) + list(scratch) + list(semaphores) + list(dict(credit=0))
    vmem = pl.BlockSpec(memory_space=pltpu.VMEM)
    found = pl.pallas_call(
        functools.partial(kernel_body, plan, names),
        out_shape=[jax.ShapeDtypeStruct(shape, F32) for shape in outputs.values()],
        in_specs=[vmem] * len(inputs),
        out_specs=[vmem] * len(outputs),
        scratch_shapes=[pltpu.VMEM(shape, dtype) for shape, dtype in scratch.values()]
        + [pltpu.SemaphoreType.DMA(shape) for shape in semaphores.values()]
        + [pltpu.SemaphoreType.REGULAR],
        compiler_params=pltpu.CompilerParams(
            collective_id=0, has_side_effects=True, vmem_limit_bytes=127 * 2**19
        ),
    )(*inputs.values())
    loss, start_grad, weights_grad, embed_grad, gain_grad, bias_grad, actor_grad, critic_grad = found
    return (
        loss.reshape(()),
        start_grad,
        weights_grad.reshape(shard),
        embed_grad,
        gain_grad.reshape(GATES),
        bias_grad.reshape(GATES),
        actor_grad.T,
        critic_grad.reshape(DET),
    )


def solution(mesh):
    return jax.shard_map(
        on_device,
        mesh=mesh,
        in_specs=(
            P(("dp", "rep"), None),
            P(("dp", "rep")),
            P(("dp", "rep")),
            P(("dp", "rep")),
            P("dp"),
            P(),
            P(),
            P(),
            P(),
            P(),
            P(("dp", "rep"), None, None),
            P(("dp", "rep"), None),
            P(("dp", "rep"), None),
        ),
        out_specs=(P(), P(("dp", "rep"), None), P("dp"), P(), P(), P(), P(), P()),
        check_vma=False,
    )
```

```python
import functools
from types import SimpleNamespace

import jax
import jax.numpy as jnp
from jax import lax
from jax.experimental import pallas as pl
from jax.experimental.pallas import tpu as pltpu
from jax.sharding import PartitionSpec as P

DET = 512
CLASSES = 32
LATENTS = 32
ACTIONS = 18
STOCH = 1024
GATES = 1536
WIDE = 256
META = 128
BLOCK = 192
TALL = 384
LAG_A, LAG_B, LAG_Z = 2, 4, 2
SMALL_TICKS = 4
START_TICKS = 3

discount = 0.99
entropy_weight = 0.1
norm_eps = 1e-05

F32 = jnp.float32
BF16 = jnp.bfloat16
MESH = pl.DeviceIdType.MESH

ROW_WIN, ROW_GRU, ROW_A1, ROW_A2, ROW_C1, ROW_C2 = 0, 1024, 4096, 5632, 6144, 7680
SM_EMBED, SM_GAIN, SM_BIAS, SM_ACTOR, SM_CRITIC, SM_LOSS = 0, 48, 54, 64, 112, 114


def dot(left, right):
    return jnp.dot(left, right, preferred_element_type=F32)


def dot_t(left, right):
    return lax.dot_general(left, right, (((0,), (0,)), ((), ())), preferred_element_type=F32)


def dot_nt(left, right):
    return lax.dot_general(left, right, (((1,), (1,)), ((), ())), preferred_element_type=F32)


def elu(value):
    near = value + 0.5 * value * value
    below = jnp.where(value > -0.00390625, near, jnp.exp(jnp.minimum(value, 0.0)) - 1.0)
    return jnp.where(value > 0, value, below)


def elu_grad(value):
    return jnp.where(value > 0, 1.0, jnp.exp(jnp.minimum(value, 0.0)))


def iota(shape, dim):
    return lax.broadcasted_iota(jnp.int32, shape, dim)


def mult(value, step):
    return pl.multiple_of(value, step)


class Plan:
    def __init__(self, devices, slots, cap, horizon, flat_rows):
        self.n = devices
        self.line = devices // 4
        self.half = self.line // 2
        self.rows = flat_rows // devices
        self.slots = slots
        self.cap = cap
        self.horizon = horizon
        self.all_rows = cap * horizon
        self.step_rows = cap * (horizon - 1)
        self.lane = -(-max(2, 2 * slots // devices) // 16) * 16
        self.parts = max(1, min(4, self.rows // 2 // 32))
        self.part_rows = self.rows // 2 // self.parts
        self.items = self.half * self.parts
        self.bits = self.line.bit_length() - 1
        self.small = 8 * devices


def kernel_body(plan, names, *refs):
    r = SimpleNamespace(**dict(zip(names, refs)))
    n, line, half, rows = plan.n, plan.line, plan.half, plan.rows
    cap, horizon, parts, prow = plan.cap, plan.horizon, plan.parts, plan.part_rows
    total, steps_rows, lane = plan.all_rows, plan.step_rows, plan.lane
    items, bits = plan.items, plan.bits
    me = lax.axis_index("dp")
    core = lax.axis_index("rep")
    z = me // 4
    a_step = 1 + core
    b_step = 2 - core
    a_bit = (me // a_step) % 2
    b_bit = (me // b_step) % 2
    a_dev = me + a_step * (1 - 2 * a_bit)
    b_dev = me + b_step * (1 - 2 * b_bit)
    q = me % 4
    q_a = a_dev % 4
    q_b = b_dev % 4
    q_ab = 3 - q
    sibling = 1 - core

    def remote(src, dst, send, recv, dev, on_core=None):
        return pltpu.make_async_remote_copy(
            src_ref=src,
            dst_ref=dst,
            send_sem=send,
            recv_sem=recv,
            device_id=(dev, core if on_core is None else on_core),
            device_id_type=MESH,
        )

    barrier = pltpu.get_barrier_semaphore()

    def greet(k, carry):
        pl.semaphore_signal(barrier, inc=1, device_id=((me + k) % n, core), device_id_type=MESH)
        return carry

    lax.fori_loop(1, n, greet, 0)
    pl.semaphore_signal(barrier, inc=1, device_id=(me, sibling), device_id_type=MESH)

    full = r.full
    own_rows = pl.ds(mult(me * rows + core * (rows // 2), 16), rows // 2)
    r.narrow[...] = r.weights[pl.ds(mult(core * rows * 2, 16), rows * 2)].astype(F32)
    for c in range(4):
        full[own_rows, 128 * c : 128 * (c + 1)] = r.narrow[pl.ds(c, rows // 2, stride=4), :].astype(BF16)

    route = r.route[...].astype(F32)
    slots = plan.slots
    used_row = (iota((1, slots), 1) < r.counts[...]).astype(F32)
    target_row = jnp.floor((route + 0.5) * (1.0 / cap))
    within_row = route - cap * target_row
    eye = iota((slots, slots), 0) == iota((slots, slots), 1)
    target_col = jnp.sum(jnp.where(eye, target_row, 0.0), axis=1, keepdims=True)
    used_col = jnp.sum(jnp.where(eye, used_row, 0.0), axis=1, keepdims=True)
    earlier = iota((slots, slots), 0) < iota((slots, slots), 1)
    same = jnp.where(earlier & (target_col == target_row), used_col, 0.0)
    rank_row = jnp.sum(same, axis=0, keepdims=True)
    column_row = jnp.where(used_row > 0, target_row * lane + rank_row, -1.0)
    lanes = n * lane
    tall = min(lanes, 256)

    def each(low, high, body):
        def step(k, carry):
            body(k)
            return carry

        lax.fori_loop(low, high, step, 0)

    def to_lanes(k):
        block = pl.ds(mult(k * tall, 16), tall)
        chosen_slot = column_row == (iota((tall, slots), 0) + k * tall).astype(F32)
        picked = jnp.where(chosen_slot, 1.0, 0.0).astype(BF16)
        r.to_lane[block] = picked
        place = jnp.sum(jnp.where(chosen_slot, within_row + 1.0, 0.0), axis=1, keepdims=True)
        marked = jnp.sum(
            jnp.where(chosen_slot, r.frame_mask[...].astype(F32), 0.0), axis=1, keepdims=True
        )
        meta_lane = iota((tall, META), 1)
        meta = jnp.where(meta_lane == 0, place, jnp.where(meta_lane == 1, marked, 0.0))
        r.sent[block, :DET] = dot(picked, r.start_deter[...]).astype(BF16)
        r.sent[block, DET:] = meta.astype(BF16)

    each(0, lanes // tall, to_lanes)

    pl.semaphore_wait(barrier, n)

    def lane_rows(k):
        return pl.ds(mult(k * lane, 16), lane)

    def exchange(width, sends, recvs):
        src, dst = r.sent, r.got

        def copy(k, to, into):
            return remote(
                src.at[lane_rows(to), 0:width], dst.at[lane_rows(into), 0:width], sends.at[k], recvs.at[k], to
            )

        def begin():
            dst[lane_rows(me), 0:width] = src[lane_rows(me), 0:width]
            each(1, n, lambda k: copy(k, (me + k) % n, me).start())

        def finish():
            each(1, n, lambda k: copy(k, me, (me + n - k) % n).wait_recv())

        def drain():
            each(1, n, lambda k: copy(k, (me + k) % n, me).wait_send())

        return begin, finish, drain

    out_begin, out_finish, out_drain = exchange(DET + META, r.ex_send, r.ex_recv)
    def bit_of(value, b):
        return (value // 2**b) % 2

    def across(b):
        return me + 4 * 2**b * (1 - 2 * bit_of(z, b))

    def item_at(i):
        spot = i // parts
        late = jnp.where(z < half, spot, jnp.where(spot == 0, half, spot - 1 + spot // (half + 1)))
        group = late // half
        order = late % half
        place = z % half
        for b in range(bits - 1):
            place = place + bit_of(order, b) * 2**b * (1 - 2 * bit_of(z, b))
        return order, group * half + place, i % parts

    def full_at(shard, piece, part):
        return full.at[pl.ds(mult(shard * rows + part * (rows // 2) + piece * prow, 16), prow)]

    def gather_copy(shard, piece, send, dev):
        view = full_at(shard, piece, core)
        return remote(view, view, send, r.ag_recv.at[shard, piece], dev)

    def share_copy(shard, piece, send, part=None):
        view = full_at(shard, piece, core if part is None else part)
        return remote(view, view, send, r.sh_recv.at[shard, piece], me, sibling)

    def far_copy(piece):
        return gather_copy(me, piece, r.far_send.at[piece], across(bits - 1))

    def plane_sends(zi, piece):
        mine = zi * 4 + q
        other = zi * 4 + q_a
        return (
            gather_copy(mine, piece, r.a_send.at[zi, piece], a_dev),
            gather_copy(mine, piece, r.b_send.at[zi, piece, 0], b_dev),
            gather_copy(other, piece, r.b_send.at[zi, piece, 1], b_dev),
        )

    def line_sends(order, zi, piece):
        return [
            (order < 2**b, gather_copy(zi * 4 + q, piece, r.line_send.at[zi, piece, b], across(b)))
            for b in range(bits - 1)
        ]

    def gather_line(i):
        order, zi, piece = item_at(i)

        @pl.when(zi != z)
        def _():
            gather_copy(zi * 4 + q, piece, r.a_send.at[zi, piece], me).wait_recv()

        for need, copy in line_sends(order, zi, piece):
            pl.when(need)(copy.start)
        to_a, to_b, _ = plane_sends(zi, piece)
        to_a.start()
        to_b.start()
        share_copy(zi * 4 + q, piece, r.sh_send.at[zi, piece, 0]).start()

    def gather_a(i):
        _, zi, piece = item_at(i)
        gather_copy(zi * 4 + q_a, piece, r.a_send.at[zi, piece], me).wait_recv()
        plane_sends(zi, piece)[2].start()
        share_copy(zi * 4 + q_a, piece, r.sh_send.at[zi, piece, 1]).start()

    def gather_b(i):
        _, zi, piece = item_at(i)
        for k, where in ((2, q_b), (3, q_ab)):
            gather_copy(zi * 4 + where, piece, r.a_send.at[zi, piece], me).wait_recv()
            share_copy(zi * 4 + where, piece, r.sh_send.at[zi, piece, k]).start()

    def gather_shared(i):
        zi, piece = i // parts, i % parts
        for k, where in ((0, q), (1, q_a), (2, q_b), (3, q_ab)):
            share_copy(zi * 4 + where, piece, r.sh_send.at[zi, piece, k], sibling).wait_recv()

    def gather_drain(i):
        zi, piece = i // parts, i % parts
        place, order = zi % half, 0
        for b in range(bits - 1):
            order = order + 2**b * ((bit_of(place, b) + bit_of(z, b)) % 2)
        for need, copy in line_sends(order, zi, piece):
            pl.when(need)(copy.wait_send)
        for copy in plane_sends(zi, piece):
            copy.wait_send()
        for k, where in ((0, q), (1, q_a), (2, q_b), (3, q_ab)):
            share_copy(zi * 4 + where, piece, r.sh_send.at[zi, piece, k]).wait_send()

    lag_a, lag_b = LAG_A, LAG_B
    all_items = 2 * items
    ticks = all_items + lag_b
    first_ticks = items + lag_b + jnp.where(z < half, 0, parts)

    def gather_tick(k):
        pl.when(k < all_items)(lambda: gather_line(k))
        pl.when((k >= lag_a) & (k < all_items + lag_a))(lambda: gather_a(k - lag_a))
        pl.when((k >= lag_b) & (k < all_items + lag_b))(lambda: gather_b(k - lag_b))

    each(0, parts, lambda piece: far_copy(piece).start())
    early = min(2, START_TICKS, items)
    each(0, early, gather_tick)

    hot, hot_t, act_hot = r.hot, r.hot_t, r.act_hot
    for t in range(horizon):
        r.latent_row[:, t * cap : (t + 1) * cap] = r.latent[t].astype(F32)
        r.action_row[:, t * cap : (t + 1) * cap] = r.action[t : t + 1].astype(F32)
    latent_row = r.latent_row[...].astype(BF16)
    spread_rows = (iota((LATENTS, STOCH), 1) // CLASSES == iota((LATENTS, STOCH), 0)).astype(F32).astype(BF16)
    class_row = (iota((1, STOCH), 1) % CLASSES).astype(F32)
    latent_col = latent_row.T
    for k in range(total // 128):
        seen = dot(latent_col[128 * k : 128 * (k + 1)], spread_rows)
        hot[128 * k : 128 * (k + 1)] = jnp.where(seen == class_row, 1.0, 0.0).astype(BF16)

    def hot_t_block(k):
        block = pl.ds(mult(k * 128, 128), 128)
        first = k * 128
        spread = ((iota((128, LATENTS), 0) + first) // CLASSES == iota((128, LATENTS), 1)).astype(F32).astype(BF16)
        seen = dot(spread, latent_row)
        class_col = ((iota((128, 1), 0) + first) % CLASSES).astype(F32)
        hot_t[block] = jnp.where(seen == class_col, 1.0, 0.0).astype(BF16)

    each(0, STOCH // 128, hot_t_block)
    act_hot[...] = jnp.where(r.action_row[...] == iota((128, total), 0).astype(F32), 1.0, 0.0).T.astype(BF16)

    r.embed_pad[...] = jnp.zeros((32, DET), BF16)
    r.embed_pad[0:ACTIONS] = r.act_embed[...]
    r.head_pad[...] = jnp.zeros((128, DET), BF16)
    r.head_pad[0:ACTIONS] = r.actor_head[...]
    r.small[...] = jnp.zeros(r.small.shape, F32)

    middle_ticks = min(START_TICKS, items + lag_b)
    each(early, middle_ticks, gather_tick)
    out_begin()
    each(middle_ticks, first_ticks, gather_tick)

    each(0, items, gather_shared)

    shuffle = r.shuffle
    row_i = iota((TALL, TALL), 0)
    shuffle[...] = jnp.where(
        iota((TALL, TALL), 1) == 3 * (row_i % 128) + row_i // 128, 1.0, 0.0
    ).astype(BF16)
    w_gru = r.w_gru
    for j in range(8):
        block = full[ROW_GRU + TALL * j : ROW_GRU + TALL * (j + 1)]
        sorted_rows = dot(shuffle[...], block).astype(BF16)
        for k in range(3):
            w_gru[128 * j : 128 * (j + 1), DET * k : DET * (k + 1)] = sorted_rows[128 * k : 128 * (k + 1)]
    each(0, items, gather_drain)
    each(0, parts, lambda piece: pl.when(z < half)(far_copy(piece).wait_send))
    w_back = full.at[ROW_GRU : ROW_GRU + GATES]
    pre, inputs, raw = r.pre, r.inputs, r.raw
    low, work = r.low, r.work
    a_one_at, a_two_at, g_one, g_two = 0, 2 * DET, 4 * DET, 6 * DET
    p_low = GATES
    inputs[steps_rows:total] = jnp.zeros((total - steps_rows, DET), BF16)
    pre_block = 5 * cap

    def pre_step(k):
        block = pl.ds(mult(k * pre_block, 16), pre_block)
        value = dot(hot[block], full[ROW_WIN : ROW_WIN + STOCH])
        value = value + dot(act_hot[block][:, 0:32], r.embed_pad[...])
        pre[block] = value
        active = elu(value).astype(BF16)
        inputs[block] = active
        raw[block] = dot(active, w_gru[0:DET])
        gather_tick(first_ticks + k)

    pre_blocks = (horizon - 1) // 5
    each(0, pre_blocks, pre_step)

    out_finish()
    r.start[...] = jnp.zeros((128, DET + META), F32)

    def from_lanes(k):
        block = pl.ds(mult(k * tall, 16), tall)
        got = r.got[block]
        put = jnp.where(got[:, DET : DET + 1].astype(F32) == (iota((tall, 128), 1) + 1).astype(F32), 1.0, 0.0).astype(BF16)
        r.placing[block] = put
        r.start[...] += dot_t(put, got)

    each(0, lanes // tall, from_lanes)
    start = r.start
    states_ref = r.states
    states_ref[0:cap] = start[0:cap, 0:DET]
    mask = start[0:cap, DET + 1 : DET + 2]
    eye = iota((cap, cap), 0) == iota((cap, cap), 1)
    mask_row = jnp.sum(jnp.where(eye, mask, 0.0), axis=0, keepdims=True)
    adv = r.adv
    running = jnp.zeros((1, cap), F32)
    sum_one = jnp.zeros((1, cap), F32)
    sum_two = jnp.zeros((1, cap), F32)
    for t in range(horizon - 1, -1, -1):
        running = r.rewards[t : t + 1] + discount * running
        sum_one = sum_one + mask_row * running
        sum_two = sum_two + mask_row * running * running
        r.returns[:, t * cap : (t + 1) * cap] = running
        r.weight_row[:, t * cap : (t + 1) * cap] = mask_row * (1.0 / horizon)
    tile_lane = iota((8, 128), 1)

    def total_of(value):
        return jnp.sum(value, axis=1, keepdims=True)

    sums = jnp.where(
        tile_lane == 0,
        total_of(sum_one),
        jnp.where(tile_lane == 1, total_of(sum_two), jnp.where(tile_lane == 2, horizon * total_of(mask_row), 0.0)),
    )
    moments, pair = r.moments, r.pair
    pair[0] = sums
    swap = remote(pair.at[0], pair.at[1], r.pair_sem.at[0], r.pair_sem.at[1], me, sibling)
    swap.start()
    swap.wait()
    moments[me] = pair[0] + pair[1]

    def moments_copy(k):
        peer = (me + k) % n
        return remote(moments.at[me], moments.at[me], r.mo_send.at[k], r.mo_recv.at[k], peer)

    def moments_landing(k):
        peer = (me + n - k) % n
        return remote(moments.at[peer], moments.at[peer], r.mo_send.at[k], r.mo_recv.at[k], peer)

    each(1, n, lambda k: moments_copy(k).start())

    def as_row(ref):
        value = ref[...].astype(F32)
        return jnp.concatenate([value[k : k + 1] for k in range(ref.shape[0])], axis=-1)

    gain = as_row(r.gain)
    bias = as_row(r.bias)
    update_ref, inv_ref = r.update, r.inv

    def forward_step(t):
        block = pl.ds(mult(t * cap, 16), cap)
        state = states_ref[block]
        state_low = state.astype(BF16)
        low[block] = state_low
        gru_raw = raw[block] + dot(state_low, w_gru[DET:])
        centred = gru_raw - jnp.mean(gru_raw, axis=-1, keepdims=True)
        inv_std = lax.rsqrt(jnp.mean(centred * centred, axis=-1, keepdims=True) + norm_eps)
        normed = centred * inv_std
        raw[block] = normed
        inv_ref[block] = jnp.broadcast_to(inv_std, (cap, 128))
        mixed = normed * gain + bias
        reset = jax.nn.sigmoid(mixed[:, :DET])
        candidate = jnp.tanh(reset * mixed[:, DET : 2 * DET])
        update = jax.nn.sigmoid(mixed[:, 2 * DET :] - 1.0)
        update_ref[block] = update
        states_ref[pl.ds(mult(t * cap + cap, 16), cap)] = update * candidate + (1.0 - update) * state
        j, k = t % 12 // 3, t % 3
        w_back[pl.ds(mult(DET * k, DET), DET), pl.ds(mult(128 * j, 128), 128)] = w_gru[
            pl.ds(mult(DET + 128 * j, 128), 128), pl.ds(mult(DET * k, DET), DET)
        ].T
        pl.when(t % 3 == 2)(lambda: gather_tick(first_ticks + pre_blocks + t // 3))

    each(0, horizon - 1, forward_step)
    done_ticks = first_ticks + pre_blocks + (horizon - 1) // 3
    each(done_ticks, jnp.maximum(ticks, done_ticks), gather_tick)
    low[steps_rows:total] = states_ref[steps_rows:total].astype(BF16)
    each(items, 2 * items, gather_shared)
    each(items, 2 * items, gather_drain)
    each(0, parts, lambda piece: pl.when(z >= half)(far_copy(piece).wait_send))

    each(1, n, lambda k: moments_landing(k).wait_recv())
    sums = moments[0]
    for k in range(1, n):
        sums = sums + moments[k]
    centre = sums[0:1, 0:1] / sums[0:1, 2:3]
    spread = jnp.sqrt(sums[0:1, 1:2] / sums[0:1, 2:3] - centre * centre + norm_eps)
    per_row = jnp.concatenate(
        [(r.returns[...] - centre) / spread, r.weight_row[...], jnp.zeros((126, total), F32)], axis=0
    ).T
    adv[...] = per_row

    grads = r.grads

    def keep_grads(first, value):
        for c in range(4):
            grads[c, pl.ds(first, value.shape[0])] = value[:, 128 * c : 128 * (c + 1)]

    def load_grads(block):
        return jnp.concatenate([grads[c, block] for c in range(4)], axis=-1)

    def grad_rows(local, part, piece):
        return pl.ds(mult(local * rows + part * (rows // 2) + piece * prow, 16), prow)

    def store_grads(block, value):
        for c in range(4):
            grads[c, block] = value[:, 128 * c : 128 * (c + 1)]

    pair_in, b_in, a_in, z_in = r.pair_in, r.b_in, r.a_in, r.z_in

    class Reducer:
        def __init__(self, group):
            self.group = group
            self.turn = half // 2 if group == 0 else 0

        def target(self, i):
            return (i // parts + self.turn) % half, i % parts

        def sem(self, array, *at):
            return array.at[(self.group,) + at]

        def out_rows(self, t, offset, piece, count):
            return pl.ds(mult(ROW_A1 + t * 4 * rows + offset + piece * count * prow, 16), count * prow)

        def in_rows(self, t, piece, count):
            return pl.ds(mult((t * parts + piece) * count * prow, 16), count * prow)

        def pair_copy(self, t, piece):
            return remote(
                full.at[self.out_rows(t, 0, piece, 4)],
                pair_in.at[self.in_rows(t, piece, 4)],
                self.sem(r.pair_s, t, piece),
                self.sem(r.pair_r, t, piece),
                me,
                sibling,
            )

        def b_copy(self, t, piece):
            return remote(
                full.at[self.out_rows(t, 2 * rows, piece, 2)],
                b_in.at[self.group, self.in_rows(t, piece, 2)],
                self.sem(r.b_s, t, piece),
                self.sem(r.b_r, t, piece),
                b_dev,
            )

        def a_copy(self, t, piece):
            return remote(
                full.at[self.out_rows(t, 3 * rows, piece, 1)],
                a_in.at[self.group, self.in_rows(t, piece, 1)],
                self.sem(r.a_s, t, piece),
                self.sem(r.a_r, t, piece),
                a_dev,
            )

        def z_slot(self, b, t):
            return sum(half // 2 ** (k + 1) for k in range(b)) + t // 2 ** (b + 1)

        def z_copy(self, b, t, piece):
            slot = self.z_slot(b, t)
            return remote(
                full.at[self.out_rows(t, 3 * rows + rows // 2, piece, 1)],
                z_in.at[self.group, self.in_rows(slot, piece, 1)],
                self.sem(r.z_s, t, piece),
                self.sem(r.z_r, slot, piece),
                across(b),
            )

        def holds(self, b, t):
            return (z - t - self.group * half) % 2**b == 0

        def differs(self, b, t):
            return bit_of(z, b) != bit_of(t + self.group * half, b)

        def fin_rows(self, piece, part):
            return pl.ds(mult((part * (rows // 2) + piece * prow) * 4, 16), prow * 4)

        def fin_copy(self, piece, part=None):
            block = self.fin_rows(piece, core if part is None else part)
            return remote(
                r.weights_grad.at[block], r.weights_grad.at[block], r.fin_s.at[piece], r.fin_r.at[piece], me, sibling
            )

        def load(self, t, piece, a):
            if self.group == 0:
                return load_grads(grad_rows(t * 4 + a * a_step + b_bit * b_step, core, piece))
            return r.kept[(t * parts + piece) * 2 + a]

        def store(self, t, piece, a, value):
            if self.group == 0:
                store_grads(grad_rows(t * 4 + a * a_step + b_bit * b_step, core, piece), value)
            else:
                r.kept[(t * parts + piece) * 2 + a] = value

        def to_pair(self, i):
            t, piece = self.target(i)
            for k in range(4):
                block = pl.ds(mult(ROW_A1 + t * 4 * rows + (piece * 4 + k) * prow, 16), prow)
                full[block] = load_grads(grad_rows(t * 4 + k, sibling, piece)).astype(BF16)
            self.pair_copy(t, piece).start()

        def to_b(self, i):
            t, piece = self.target(i)
            self.pair_copy(t, piece).wait_recv()

            def both_cores(where):
                spot = pl.ds(mult(((t * parts + piece) * 4 + where) * prow, 16), prow)
                return load_grads(grad_rows(t * 4 + where, core, piece)) + pair_in[spot].astype(F32)

            for a in range(2):
                block = pl.ds(mult(ROW_A1 + t * 4 * rows + 2 * rows + (piece * 2 + a) * prow, 16), prow)
                full[block] = both_cores(a * a_step + (1 - b_bit) * b_step).astype(BF16)
            self.b_copy(t, piece).start()
            for a in range(2):
                self.store(t, piece, a, both_cores(a * a_step + b_bit * b_step))

        def b_part(self, t, piece, a):
            spot = pl.ds(mult(((t * parts + piece) * 2 + a) * prow, 16), prow)
            return b_in[self.group, spot].astype(F32)

        def to_a(self, i):
            t, piece = self.target(i)
            self.b_copy(t, piece).wait_recv()
            other = 1 - a_bit
            if self.group == 0:
                heads_rs.a_copy(t, piece).wait_send()
            full[self.out_rows(t, 3 * rows, piece, 1)] = (
                self.load(t, piece, other) + self.b_part(t, piece, other)
            ).astype(BF16)
            self.a_copy(t, piece).start()
            self.store(t, piece, a_bit, self.load(t, piece, a_bit) + self.b_part(t, piece, a_bit))

        def to_plane(self, b, i):
            t, piece = self.target(i)

            @pl.when(self.holds(b, t))
            def _():
                if b == 0:
                    self.a_copy(t, piece).wait_recv()
                    came = a_in[self.group, self.in_rows(t, piece, 1)]
                else:
                    self.z_copy(b - 1, t, piece).wait_recv()
                    came = z_in[self.group, self.in_rows(self.z_slot(b - 1, t), piece, 1)]
                value = self.load(t, piece, a_bit) + came.astype(F32)
                if b == bits:
                    first = mult((core * (rows // 2) + piece * prow) * 4, 16)
                    for c in range(4):
                        r.weights_grad[pl.ds(first + c, prow, stride=4), :] = value[:, 128 * c : 128 * (c + 1)]
                    self.fin_copy(piece).start()
                else:

                    @pl.when(self.differs(b, t))
                    def _():
                        if self.group == 0:
                            heads_rs.plane_gone(t, piece)
                        full[self.out_rows(t, 3 * rows + rows // 2, piece, 1)] = value.astype(BF16)
                        self.z_copy(b, t, piece).start()

                    pl.when(~self.differs(b, t))(lambda: self.store(t, piece, a_bit, value))

        def drain_early(self, i):
            t, piece = self.target(i)
            self.pair_copy(t, piece).wait_send()
            self.b_copy(t, piece).wait_send()

        def plane_gone(self, t, piece):
            for b in range(bits):
                pl.when(self.holds(b, t) & self.differs(b, t))(self.z_copy(b, t, piece).wait_send)

        def drain(self, i):
            t, piece = self.target(i)
            if self.group == 0:
                self.a_copy(t, piece).wait_send()
                self.plane_gone(t, piece)
            else:
                for b in range(bits):
                    waited = False
                    for c in range(bits):
                        waited = waited | (gru_rs.holds(c, t) & gru_rs.differs(c, t))
                    pl.when(self.holds(b, t) & self.differs(b, t) & ~waited)(self.z_copy(b, t, piece).wait_send)

            @pl.when(self.holds(bits, t))
            def _():
                self.fin_copy(piece).wait_send()
                self.fin_copy(piece, sibling).wait_recv()

    heads_rs, gru_rs = Reducer(1), Reducer(0)
    net_items = items // 2

    def of_item(k, stage):
        pl.when((k >= 0) & (k < items))(lambda: stage(heads_rs, k))
        pl.when((k >= items) & (k < 2 * items))(lambda: stage(gru_rs, k - items))

    def rs_tick(k):
        of_item(k, lambda rs, i: rs.to_a(i))
        for b in range(bits + 1):
            of_item(k - LAG_Z * (b + 1), lambda rs, i, b=b: rs.to_plane(b, i))

    rs_ticks = 2 * items + LAG_Z * (bits + 1)

    out_grads, state_grads = r.out_grads, r.state_grads
    r.loss_acc[...] = jnp.zeros((BLOCK, 128), F32)
    critic_row = as_row(r.critic_head)
    lane_id = iota((BLOCK, 128), 1)

    def net_rows(side):
        return (ROW_A1, ROW_A2) if side == 0 else (ROW_C1, ROW_C2)

    def net_cols(base, side):
        return slice(base + side * DET, base + (side + 1) * DET)

    def net_step(k, side):
        first, second = net_rows(side)
        block = pl.ds(mult(k * BLOCK, 64), BLOCK)
        one = dot(low[block], full[first : first + DET]) + dot(hot[block], full[first + DET : first + DET + STOCH])
        one_low = elu(one).astype(BF16)
        work[block, net_cols(a_one_at, side)] = one_low
        two = dot(one_low, full[second : second + DET])
        two_low = elu(two).astype(BF16)
        work[block, net_cols(a_two_at, side)] = two_low
        advantage = adv[block][:, 0:1]
        weight = adv[block][:, 1:2]
        if side == 0:
            real = lane_id < ACTIONS
            logits = jnp.where(real, dot_nt(two_low, r.head_pad[...]), -1e30)
            shifted = logits - jnp.max(logits, axis=-1, keepdims=True)
            powers = jnp.where(real, jnp.exp(shifted), 0.0)
            norm = jnp.sum(powers, axis=-1, keepdims=True)
            log_probs = jnp.where(real, shifted - jnp.log(norm), 0.0)
            probs = powers / norm
            taken = act_hot[block].astype(F32)
            chosen = jnp.sum(taken * log_probs, axis=-1, keepdims=True)
            entropy = -jnp.sum(probs * log_probs, axis=-1, keepdims=True)
            r.loss_acc[...] += weight * (-advantage * chosen - entropy_weight * entropy)
            grad_logits = weight * (
                -advantage * (taken - probs) + entropy_weight * probs * (log_probs + entropy)
            )
            both = grad_logits.astype(BF16)
            out_grads[block] = both
            back = dot(both, r.head_pad[...])
        else:
            value = jnp.sum(two_low.astype(F32) * critic_row, axis=-1, keepdims=True)
            gap = value - advantage
            r.loss_acc[...] += weight * (0.5 * gap * gap)
            value_low = (weight * gap).astype(BF16).astype(F32)
            out_grads[block] = jnp.where(lane_id == ACTIONS, value_low, out_grads[block].astype(F32)).astype(BF16)
            back = value_low * critic_row
        back_low = (back * elu_grad(two)).astype(BF16)
        work[block, net_cols(g_two, side)] = back_low
        low_one = (dot_nt(back_low, full[second : second + DET]) * elu_grad(one)).astype(BF16)
        work[block, net_cols(g_one, side)] = low_one
        state_part = dot_nt(low_one, full[first : first + DET])
        if side == 0:
            state_grads[block] = state_part
        else:
            state_grads[block] += state_part

    def net_grads(side):
        base = side * 2048
        for j in range(2):
            part = slice(j * WIDE, (j + 1) * WIDE)
            keep_grads(base + j * WIDE, dot_t(low[:, part], work[:, net_cols(g_one, side)]))
            at = a_one_at + side * DET + j * WIDE
            keep_grads(base + GATES + j * WIDE, dot_t(work[:, at : at + WIDE], work[:, net_cols(g_two, side)]))

        def latent_part(k):
            part = pl.ds(mult(k * WIDE, WIDE), WIDE)
            keep_grads(mult(base + DET + k * WIDE, WIDE), dot(hot_t[part], work[:, net_cols(g_one, side)]))

        each(0, STOCH // WIDE, latent_part)

    blocks = total // BLOCK
    each(0, blocks, lambda k: net_step(k, 0))
    net_grads(0)
    each(0, net_items, heads_rs.to_pair)
    net_step(0, 1)
    each(0, net_items, heads_rs.to_b)
    each(1, blocks, lambda k: net_step(k, 1))
    each(0, net_items // 2, rs_tick)
    net_grads(1)
    each(net_items, items, heads_rs.to_pair)
    each(net_items // 2, net_items, rs_tick)

    small = r.small
    head_grad = dot_t(out_grads[...], work[:, a_two_at : a_two_at + 2 * DET])
    small[SM_ACTOR : SM_ACTOR + 24] = head_grad[0:24, 0:WIDE]
    small[SM_ACTOR + 24 : SM_ACTOR + 48] = head_grad[0:24, WIDE:DET]
    small[SM_CRITIC : SM_CRITIC + 1] = head_grad[ACTIONS : ACTIONS + 1, DET : DET + WIDE]
    small[SM_CRITIC + 1 : SM_CRITIC + 2] = head_grad[ACTIONS : ACTIONS + 1, DET + WIDE :]
    small[SM_LOSS : SM_LOSS + 1, 0:128] = jnp.sum(r.loss_acc[...], axis=0, keepdims=True)

    scan_b = 2

    def heads_b(index):
        share = -(-net_items // scan_b)
        low_item = net_items + index * share
        each(low_item, jnp.minimum(low_item + share, items), heads_rs.to_b)

    scan_ticks = net_items + (horizon - 1) // 3 - 1

    gain_acc, bias_acc = r.gain_acc, r.bias_acc
    gain_acc[...] = jnp.zeros((8, GATES), F32)
    bias_acc[...] = jnp.zeros((8, GATES), F32)
    carry_ref = r.carry
    carry_ref[...] = state_grads[steps_rows:total]
    work[steps_rows:total, 0 : 4 * DET] = jnp.zeros((total - steps_rows, 4 * DET), BF16)
    gain_mid, bias_mid = gain[:, DET : 2 * DET], bias[:, DET : 2 * DET]

    def fold(value):
        out = value[0:8]
        for k in range(1, cap // 8):
            out = out + value[8 * k : 8 * (k + 1)]
        return out

    def backward_step(index):
        t = horizon - 2 - index
        block = pl.ds(mult(t * cap, 16), cap)
        carry = carry_ref[...]
        normed = raw[block]
        inv_std = inv_ref[block][:, 0:1]
        reset = jax.nn.sigmoid(normed[:, :DET] * gain[:, :DET] + bias[:, :DET])
        update = update_ref[block]
        state = states_ref[block]
        middle = normed[:, DET : 2 * DET] * gain_mid + bias_mid
        candidate = jnp.tanh(reset * middle)
        inner = carry * update * (1.0 - candidate * candidate)
        part = jnp.concatenate(
            [
                inner * middle * reset * (1.0 - reset),
                inner * reset,
                carry * (candidate - state) * update * (1.0 - update),
            ],
            axis=-1,
        )
        gain_acc[...] += fold(part * normed)
        bias_acc[...] += fold(part)
        normed_grad = part * gain
        raw_grad = inv_std * (
            normed_grad
            - jnp.mean(normed_grad, axis=-1, keepdims=True)
            - normed * jnp.mean(normed_grad * normed, axis=-1, keepdims=True)
        )
        grad_low = raw_grad.astype(BF16)
        work[block, 0:GATES] = grad_low
        carry_ref[...] = carry * (1.0 - update) + dot(grad_low, w_back[...]) + state_grads[block]
        pl.when(index < scan_b)(lambda: heads_b(index))
        pl.when((index >= scan_b) & (index % 3 == 1))(lambda: rs_tick(net_items + index // 3 - 1))

    each(0, horizon - 1, backward_step)

    back_begin, back_finish, back_drain = exchange(DET, r.bk_send, r.bk_recv)
    out_drain()
    start_grads = carry_ref[...].astype(BF16)

    def back_lanes(k):
        block = pl.ds(mult(k * tall, 16), tall)
        r.sent[block, :DET] = dot(r.placing[block][:, 0:cap], start_grads).astype(BF16)

    each(0, lanes // tall, back_lanes)
    back_begin()

    each(0, items, heads_rs.drain_early)
    pl.semaphore_signal(r.credit, inc=1, device_id=(me, sibling), device_id_type=MESH)
    def gru_part(j):
        source = inputs if j < 2 else low
        part = slice((j % 2) * WIDE, (j % 2 + 1) * WIDE)
        for k in range(3):
            value = dot_t(source[:, part], work[:, DET * k : DET * (k + 1)])
            for c in range(4):
                grads[c, pl.ds(ROW_GRU + k + 768 * j, WIDE, stride=3), :] = value[:, 128 * c : 128 * (c + 1)]

    for j in (3, 2, 1):
        gru_part(j)
    pl.semaphore_wait(r.credit, 1)
    each(0, net_items, gru_rs.to_pair)

    def pre_back(k):
        block = pl.ds(mult(k * pre_block, 16), pre_block)
        value = dot_nt(work[block, 0:GATES], w_gru[0:DET])
        work[block, p_low : p_low + DET] = (value * elu_grad(pre[block])).astype(BF16)

    each(0, pre_blocks, pre_back)
    ready = min(scan_ticks, items)
    each(ready, items, rs_tick)
    ready = max(ready, items)
    each(0, net_items, gru_rs.to_b)
    gru_part(0)

    def win_part(k):
        part = pl.ds(mult(k * WIDE, WIDE), WIDE)
        keep_grads(mult(k * WIDE, WIDE), dot(hot_t[part], work[:, p_low : p_low + DET]))

    each(0, STOCH // WIDE, win_part)
    each(net_items, items, gru_rs.to_pair)
    step_ticks = max(net_items // 4, 1)
    each(ready, ready + step_ticks, rs_tick)
    each(net_items, items, gru_rs.to_b)
    each(ready + step_ticks, ready + 2 * step_ticks, rs_tick)
    ready += 2 * step_ticks
    embed_grad = dot_t(act_hot[...], work[:, p_low : p_low + DET])
    small[SM_EMBED : SM_EMBED + 24] = embed_grad[0:24, 0:WIDE]
    small[SM_EMBED + 24 : SM_EMBED + 48] = embed_grad[0:24, WIDE:DET]
    gain_sum = jnp.sum(gain_acc[...], axis=0, keepdims=True)
    bias_sum = jnp.sum(bias_acc[...], axis=0, keepdims=True)
    for k in range(GATES // WIDE):
        small[SM_GAIN + k : SM_GAIN + k + 1] = gain_sum[:, k * WIDE : (k + 1) * WIDE]
        small[SM_BIAS + k : SM_BIAS + k + 1] = bias_sum[:, k * WIDE : (k + 1) * WIDE]

    small_in, scattered = r.small_in, r.scattered
    summed = small_in
    swap_small = remote(small, small_in, r.pair_sem.at[2], r.pair_sem.at[3], me, sibling)
    swap_small.start()
    each(ready, ready + step_ticks, rs_tick)
    swap_small.wait()
    small_sum = small
    small_sum[...] = small[...] + small_in[...]

    def eight(k):
        return pl.ds(mult(k * 8, 8), 8)

    def scatter_copy(k):
        peer = (me + k) % n
        return remote(small_sum.at[eight(peer)], scattered.at[me], r.sc_send.at[k], r.sc_recv.at[k], peer)

    def scatter_landing(k):
        peer = (me + n - k) % n
        return remote(small_sum.at[eight(me)], scattered.at[peer], r.sc_send.at[k], r.sc_recv.at[k], peer)

    def summed_copy(k):
        peer = (me + k) % n
        return remote(summed.at[eight(me)], summed.at[eight(me)], r.sm_send.at[k], r.sm_recv.at[k], peer)

    def summed_landing(k):
        peer = (me + n - k) % n
        return remote(summed.at[eight(peer)], summed.at[eight(peer)], r.sm_send.at[k], r.sm_recv.at[k], peer)

    scattered[me] = small_sum[eight(me)]
    each(1, n, lambda k: scatter_copy(k).start())
    landing = max(ready + step_ticks, rs_ticks - SMALL_TICKS)
    each(ready + step_ticks, landing, rs_tick)
    each(1, n, lambda k: scatter_landing(k).wait_recv())
    block_sum = scattered[0]
    for k in range(1, n):
        block_sum = block_sum + scattered[k]
    summed[eight(me)] = block_sum
    each(1, n, lambda k: summed_copy(k).start())
    each(landing, rs_ticks, rs_tick)
    each(0, items, heads_rs.drain)

    back_finish()
    r.start_grad[...] = jnp.zeros((slots, DET), F32)

    def frames(k):
        block = pl.ds(mult(k * tall, 16), tall)
        r.start_grad[...] += dot_t(r.to_lane[block], r.got[block][:, 0:DET])

    each(0, lanes // tall, frames)
    each(1, n, lambda k: summed_landing(k).wait_recv())
    r.loss[...] = summed[SM_LOSS : SM_LOSS + 1, 0:1]
    r.embed_grad[:, 0:WIDE] = summed[SM_EMBED : SM_EMBED + ACTIONS]
    r.embed_grad[:, WIDE:DET] = summed[SM_EMBED + 24 : SM_EMBED + 24 + ACTIONS]
    for k in range(GATES // WIDE):
        for h in range(2):
            lanes_of = slice(h * 128, (h + 1) * 128)
            r.gain_grad[2 * k + h : 2 * k + h + 1] = summed[SM_GAIN + k : SM_GAIN + k + 1, lanes_of]
            r.bias_grad[2 * k + h : 2 * k + h + 1] = summed[SM_BIAS + k : SM_BIAS + k + 1, lanes_of]
    for k in range(2):
        for h in range(2):
            lanes_of = slice(h * 128, (h + 1) * 128)
            r.critic_grad[2 * k + h : 2 * k + h + 1] = summed[SM_CRITIC + k : SM_CRITIC + k + 1, lanes_of]
    r.actor_grad[:, 0:WIDE] = summed[SM_ACTOR : SM_ACTOR + ACTIONS]
    r.actor_grad[:, WIDE:DET] = summed[SM_ACTOR + 24 : SM_ACTOR + 24 + ACTIONS]
    each(0, items, gru_rs.drain_early)
    each(0, items, gru_rs.drain)

    back_drain()
    each(1, n, lambda k: moments_copy(k).wait_send())
    each(1, n, lambda k: scatter_copy(k).wait_send())
    each(1, n, lambda k: summed_copy(k).wait_send())


def hand_over(*refs):
    count = len(refs) // 2
    for k in range(count):
        refs[count + k][...] = refs[k][...]


def on_device(
    start_deter,
    frame_mask,
    counts,
    route,
    weights_flat,
    act_embed,
    gru_gain,
    gru_bias,
    actor_head,
    critic_head,
    latent_idx,
    action_idx,
    rewards,
):
    n = lax.axis_size("dp")
    slots = start_deter.shape[0]
    cap, horizon = action_idx.shape
    shard = weights_flat.shape[0]
    plan = Plan(n, slots, cap, horizon, shard * n // DET)
    total, steps_rows, lanes = plan.all_rows, plan.step_rows, n * plan.lane
    line, half, parts, prow, items = plan.line, plan.half, plan.parts, plan.part_rows, plan.items
    inputs = dict(
        start_deter=start_deter,
        frame_mask=frame_mask.reshape(1, slots),
        counts=counts.reshape(1, 1),
        route=route.reshape(1, slots),
        weights=weights_flat.reshape(plan.rows * 4, 128),
        act_embed=act_embed,
        gain=gru_gain.reshape(GATES // 128, 128),
        bias=gru_bias.reshape(GATES // 128, 128),
        actor_head=actor_head.T,
        critic_head=critic_head.reshape(DET // 128, 128),
        latent=jnp.transpose(latent_idx, (1, 2, 0)),
        action=action_idx.T,
        rewards=rewards.T,
    )
    outputs = dict(
        loss=(1, 1),
        start_grad=(slots, DET),
        weights_grad=(plan.rows * 4, 128),
        embed_grad=(ACTIONS, DET),
        gain_grad=(GATES // 128, 128),
        bias_grad=(GATES // 128, 128),
        actor_grad=(ACTIONS, DET),
        critic_grad=(DET // 128, 128),
    )
    group_rows = half * 4 * plan.rows
    half_rows = group_rows // 2
    scratch = dict(
        narrow=((plan.rows * 2, 128), F32),
        latent_row=((LATENTS, total), F32),
        action_row=((1, total), F32),
        returns=((1, total), F32),
        weight_row=((1, total), F32),
        kept=((2 * items, prow, DET), F32),
        full=((n * plan.rows, DET), BF16),
        start=((128, DET + META), F32),
        to_lane=((lanes, slots), BF16),
        sent=((lanes, DET + META), BF16),
        got=((lanes, DET + META), BF16),
        placing=((lanes, 128), BF16),
        hot=((total, STOCH), BF16),
        hot_t=((STOCH, total), BF16),
        act_hot=((total, 128), BF16),
        embed_pad=((32, DET), BF16),
        head_pad=((128, DET), BF16),
        small=((plan.small, WIDE), F32),
        small_in=((plan.small, WIDE), F32),
        scattered=((n, 8, WIDE), F32),
        states=((total, DET), F32),
        adv=((total, 128), F32),
        pair=((2, 8, 128), F32),
        moments=((n, 8, 128), F32),
        shuffle=((TALL, TALL), BF16),
        w_gru=((STOCH, GATES), BF16),
        pre=((steps_rows, DET), F32),
        inputs=((total, DET), BF16),
        work=((total, 8 * DET), BF16),
        raw=((steps_rows, GATES), F32),
        low=((total, DET), BF16),
        update=((steps_rows, DET), F32),
        inv=((steps_rows, 128), F32),
        out_grads=((total, 128), BF16),
        state_grads=((total, DET), F32),
        loss_acc=((BLOCK, 128), F32),
        grads=((4, group_rows, 128), F32),
        pair_in=((half_rows, DET), BF16),
        b_in=((2, half_rows // 2, DET), BF16),
        a_in=((2, half_rows // 4, DET), BF16),
        z_in=((2, half_rows // 4, DET), BF16),
        gain_acc=((8, GATES), F32),
        bias_acc=((8, GATES), F32),
        carry=((cap, DET), F32),
    )
    semaphores = dict(
        ex_send=(n,),
        ex_recv=(n,),
        bk_send=(n,),
        bk_recv=(n,),
        mo_send=(n,),
        mo_recv=(n,),
        sc_send=(n,),
        sc_recv=(n,),
        sm_send=(n,),
        sm_recv=(n,),
        pair_sem=(4,),
        ag_recv=(n, parts),
        sh_recv=(n, parts),
        far_send=(parts,),
        line_send=(line, parts, max(plan.bits - 1, 1)),
        a_send=(line, parts),
        b_send=(line, parts, 2),
        sh_send=(line, parts, 4),
        pair_s=(2, half, parts),
        pair_r=(2, half, parts),
        b_s=(2, half, parts),
        b_r=(2, half, parts),
        a_s=(2, half, parts),
        a_r=(2, half, parts),
        z_s=(2, half, parts),
        z_r=(2, half, parts),
        fin_s=(parts,),
        fin_r=(parts,),
    )
    names = list(inputs) + list(outputs) + list(scratch) + list(semaphores) + list(dict(credit=0))
    vmem = pl.BlockSpec(memory_space=pltpu.VMEM)
    found = pl.pallas_call(
        functools.partial(kernel_body, plan, names),
        out_shape=[jax.ShapeDtypeStruct(shape, F32) for shape in outputs.values()],
        in_specs=[vmem] * len(inputs),
        out_specs=[vmem] * len(outputs),
        scratch_shapes=[pltpu.VMEM(shape, dtype) for shape, dtype in scratch.values()]
        + [pltpu.SemaphoreType.DMA(shape) for shape in semaphores.values()]
        + [pltpu.SemaphoreType.REGULAR],
        compiler_params=pltpu.CompilerParams(
            collective_id=0, has_side_effects=True, vmem_limit_bytes=127 * 2**19
        ),
    )(*inputs.values())
    found = pl.pallas_call(
        hand_over,
        out_shape=[jax.ShapeDtypeStruct(shape, F32) for shape in outputs.values()],
        in_specs=[vmem] * len(outputs),
        out_specs=[vmem] * len(outputs),
    )(*found)
    loss, start_grad, weights_grad, embed_grad, gain_grad, bias_grad, actor_grad, critic_grad = found
    return (
        loss.reshape(()),
        start_grad,
        weights_grad.reshape(shard),
        embed_grad,
        gain_grad.reshape(GATES),
        bias_grad.reshape(GATES),
        actor_grad.T,
        critic_grad.reshape(DET),
    )


def solution(mesh):
    return jax.shard_map(
        on_device,
        mesh=mesh,
        in_specs=(
            P(("dp", "rep"), None),
            P(("dp", "rep")),
            P(("dp", "rep")),
            P(("dp", "rep")),
            P("dp"),
            P(),
            P(),
            P(),
            P(),
            P(),
            P(("dp", "rep"), None, None),
            P(("dp", "rep"), None),
            P(("dp", "rep"), None),
        ),
        out_specs=(P(), P(("dp", "rep"), None), P("dp"), P(), P(), P(), P(), P()),
        check_vma=False,
    )
```

```python
import functools
from types import SimpleNamespace

import jax
import jax.numpy as jnp
from jax import lax
from jax.experimental import pallas as pl
from jax.experimental.pallas import tpu as pltpu
from jax.sharding import PartitionSpec as P

DET = 512
CLASSES = 32
LATENTS = 32
ACTIONS = 18
STOCH = 1024
GATES = 1536
WIDE = 256
META = 128
TALL = 384
LAG_A, LAG_B, LAG_Z = 2, 4, 2
GATHER_PARTS = 4
AHEAD = 4
SCATTER_TICKS, SPREAD_TICKS = 11, 4
START_TICKS = 3

discount = 0.99
entropy_weight = 0.1
norm_eps = 1e-05

F32 = jnp.float32
BF16 = jnp.bfloat16
MESH = pl.DeviceIdType.MESH

ROW_WIN, ROW_GRU, ROW_A1, ROW_A2, ROW_C1, ROW_C2 = 0, 1024, 4096, 5632, 6144, 7680
SM_EMBED, SM_GAIN, SM_BIAS, SM_ACTOR, SM_CRITIC, SM_LOSS = 0, 48, 54, 64, 112, 114


def dot(left, right):
    return jnp.dot(left, right, preferred_element_type=F32)


def dot_t(left, right):
    return lax.dot_general(left, right, (((0,), (0,)), ((), ())), preferred_element_type=F32)


def dot_nt(left, right):
    return lax.dot_general(left, right, (((1,), (1,)), ((), ())), preferred_element_type=F32)


def elu(value):
    near = value + 0.5 * value * value
    below = jnp.where(value > -0.00390625, near, jnp.exp(jnp.minimum(value, 0.0)) - 1.0)
    return jnp.where(value > 0, value, below)


def elu_grad(value):
    return jnp.where(value > 0, 1.0, jnp.exp(jnp.minimum(value, 0.0)))


def iota(shape, dim):
    return lax.broadcasted_iota(jnp.int32, shape, dim)


def mult(value, step):
    return pl.multiple_of(value, step)


class Plan:
    def __init__(self, devices, slots, cap, horizon, flat_rows):
        self.n = devices
        self.line = devices // 4
        self.half = self.line // 2
        self.rows = flat_rows // devices
        self.slots = slots
        self.cap = cap
        self.horizon = horizon
        self.all_rows = cap * horizon
        self.step_rows = cap * (horizon - 1)
        self.lane = -(-max(2, 2 * slots // devices) // 16) * 16
        self.parts = max(1, min(4, self.rows // 2 // 32))
        self.part_rows = self.rows // 2 // self.parts
        self.items = self.half * self.parts
        self.cuts = max(1, min(GATHER_PARTS, self.rows // 2 // 16))
        self.bits = self.line.bit_length() - 1
        self.small = 8 * devices
        self.block = 256 if self.line <= 4 else 192


def kernel_body(plan, names, *refs):
    r = SimpleNamespace(**dict(zip(names, refs)))
    n, line, half, rows = plan.n, plan.line, plan.half, plan.rows
    cap, horizon, parts, prow = plan.cap, plan.horizon, plan.parts, plan.part_rows
    total, steps_rows, lane = plan.all_rows, plan.step_rows, plan.lane
    items, bits = plan.items, plan.bits
    me = lax.axis_index("dp")
    core = lax.axis_index("rep")
    z = me // 4
    a_step = 1 + core
    b_step = 2 - core
    a_bit = (me // a_step) % 2
    b_bit = (me // b_step) % 2
    a_dev = me + a_step * (1 - 2 * a_bit)
    b_dev = me + b_step * (1 - 2 * b_bit)
    q = me % 4
    q_a = a_dev % 4
    q_b = b_dev % 4
    q_ab = 3 - q
    sibling = 1 - core

    def remote(src, dst, send, recv, dev, on_core=None):
        return pltpu.make_async_remote_copy(
            src_ref=src,
            dst_ref=dst,
            send_sem=send,
            recv_sem=recv,
            device_id=(dev, core if on_core is None else on_core),
            device_id_type=MESH,
        )

    barrier = pltpu.get_barrier_semaphore()

    def greet(k, carry):
        pl.semaphore_signal(barrier, inc=1, device_id=((me + k) % n, core), device_id_type=MESH)
        return carry

    lax.fori_loop(1, n, greet, 0)
    pl.semaphore_signal(barrier, inc=1, device_id=(me, sibling), device_id_type=MESH)

    full = r.full
    own_rows = pl.ds(mult(me * rows + core * (rows // 2), 16), rows // 2)
    r.narrow[...] = r.weights[pl.ds(mult(core * rows * 2, 16), rows * 2)].astype(F32)
    for c in range(4):
        full[own_rows, 128 * c : 128 * (c + 1)] = r.narrow[pl.ds(c, rows // 2, stride=4), :].astype(BF16)

    route = r.route[...].astype(F32)
    slots = plan.slots
    used_row = (iota((1, slots), 1) < r.counts[...]).astype(F32)
    target_row = jnp.floor((route + 0.5) * (1.0 / cap))
    within_row = route - cap * target_row
    eye = iota((slots, slots), 0) == iota((slots, slots), 1)
    target_col = jnp.sum(jnp.where(eye, target_row, 0.0), axis=1, keepdims=True)
    used_col = jnp.sum(jnp.where(eye, used_row, 0.0), axis=1, keepdims=True)
    earlier = iota((slots, slots), 0) < iota((slots, slots), 1)
    same = jnp.where(earlier & (target_col == target_row), used_col, 0.0)
    rank_row = jnp.sum(same, axis=0, keepdims=True)
    column_row = jnp.where(used_row > 0, target_row * lane + rank_row, -1.0)
    lanes = n * lane
    tall = min(lanes, 256)

    def each(low, high, body):
        def step(k, carry):
            body(k)
            return carry

        lax.fori_loop(low, high, step, 0)

    def to_lanes(k):
        block = pl.ds(mult(k * tall, 16), tall)
        chosen_slot = column_row == (iota((tall, slots), 0) + k * tall).astype(F32)
        picked = jnp.where(chosen_slot, 1.0, 0.0).astype(BF16)
        r.to_lane[block] = picked
        place = jnp.sum(jnp.where(chosen_slot, within_row + 1.0, 0.0), axis=1, keepdims=True)
        marked = jnp.sum(
            jnp.where(chosen_slot, r.frame_mask[...].astype(F32), 0.0), axis=1, keepdims=True
        )
        meta_lane = iota((tall, META), 1)
        meta = jnp.where(meta_lane == 0, place, jnp.where(meta_lane == 1, marked, 0.0))
        r.sent[block, :DET] = dot(picked, r.start_deter[...]).astype(BF16)
        r.sent[block, DET:] = meta.astype(BF16)

    each(0, lanes // tall, to_lanes)

    pl.semaphore_wait(barrier, n)

    def lane_rows(k):
        return pl.ds(mult(k * lane, 16), lane)

    def exchange(width, sends, recvs):
        src, dst = r.sent, r.got

        def copy(k, to, into):
            return remote(
                src.at[lane_rows(to), 0:width], dst.at[lane_rows(into), 0:width], sends.at[k], recvs.at[k], to
            )

        def begin():
            dst[lane_rows(me), 0:width] = src[lane_rows(me), 0:width]
            each(1, n, lambda k: copy(k, (me + k) % n, me).start())

        def finish():
            each(1, n, lambda k: copy(k, me, (me + n - k) % n).wait_recv())

        def drain():
            each(1, n, lambda k: copy(k, (me + k) % n, me).wait_send())

        return begin, finish, drain

    out_begin, out_finish, out_drain = exchange(DET + META, r.ex_send, r.ex_recv)
    cuts = plan.cuts
    chunks = half * cuts
    crow = rows // 2 // cuts
    def bit_of(value, b):
        return (value // 2**b) % 2

    def across(b):
        return me + 4 * 2**b * (1 - 2 * bit_of(z, b))

    ahead = min(AHEAD, cuts)

    def item_at(i):
        i = jnp.where(z < half, i, jnp.where(i < ahead, chunks + i, jnp.where(i < ahead + chunks, i - ahead, i)))
        late = i // cuts
        group = late // half
        order = late % half
        place = z % half
        for b in range(bits - 1):
            place = place + bit_of(order, b) * 2**b * (1 - 2 * bit_of(z, b))
        return order, group * half + place, i % cuts

    def full_at(shard, piece, part):
        return full.at[pl.ds(mult(shard * rows + part * (rows // 2) + piece * crow, 16), crow)]

    def gather_copy(shard, piece, send, dev):
        view = full_at(shard, piece, core)
        return remote(view, view, send, r.ag_recv.at[shard, piece], dev)

    def share_copy(shard, piece, send, part=None):
        view = full_at(shard, piece, core if part is None else part)
        return remote(view, view, send, r.sh_recv.at[shard, piece], me, sibling)

    def far_copy(piece):
        return gather_copy(me, piece, r.far_send.at[piece], across(bits - 1))

    def plane_sends(zi, piece):
        mine = zi * 4 + q
        other = zi * 4 + q_a
        return (
            gather_copy(mine, piece, r.a_send.at[zi, piece], a_dev),
            gather_copy(mine, piece, r.b_send.at[zi, piece, 0], b_dev),
            gather_copy(other, piece, r.b_send.at[zi, piece, 1], b_dev),
        )

    def line_sends(order, zi, piece):
        return [
            (order < 2**b, gather_copy(zi * 4 + q, piece, r.line_send.at[zi, piece, b], across(b)))
            for b in range(bits - 1)
        ]

    def gather_line(i):
        order, zi, piece = item_at(i)

        @pl.when(zi != z)
        def _():
            gather_copy(zi * 4 + q, piece, r.a_send.at[zi, piece], me).wait_recv()

        for need, copy in line_sends(order, zi, piece):
            pl.when(need)(copy.start)
        to_a, to_b, _ = plane_sends(zi, piece)
        to_a.start()
        to_b.start()
        share_copy(zi * 4 + q, piece, r.sh_send.at[zi, piece, 0]).start()

    def gather_a(i):
        _, zi, piece = item_at(i)
        gather_copy(zi * 4 + q_a, piece, r.a_send.at[zi, piece], me).wait_recv()
        plane_sends(zi, piece)[2].start()
        share_copy(zi * 4 + q_a, piece, r.sh_send.at[zi, piece, 1]).start()

    def gather_b(i):
        _, zi, piece = item_at(i)
        for k, where in ((2, q_b), (3, q_ab)):
            gather_copy(zi * 4 + where, piece, r.a_send.at[zi, piece], me).wait_recv()
            share_copy(zi * 4 + where, piece, r.sh_send.at[zi, piece, k]).start()

    def gather_shared(i):
        zi, piece = i // cuts, i % cuts
        for k, where in ((0, q), (1, q_a), (2, q_b), (3, q_ab)):
            share_copy(zi * 4 + where, piece, r.sh_send.at[zi, piece, k], sibling).wait_recv()

    def gather_drain(i):
        zi, piece = i // cuts, i % cuts
        place, order = zi % half, 0
        for b in range(bits - 1):
            order = order + 2**b * ((bit_of(place, b) + bit_of(z, b)) % 2)
        for need, copy in line_sends(order, zi, piece):
            pl.when(need)(copy.wait_send)
        for copy in plane_sends(zi, piece):
            copy.wait_send()
        for k, where in ((0, q), (1, q_a), (2, q_b), (3, q_ab)):
            share_copy(zi * 4 + where, piece, r.sh_send.at[zi, piece, k]).wait_send()

    lag_a, lag_b = LAG_A, LAG_B
    all_chunks = 2 * chunks
    ticks = all_chunks + lag_b
    first_ticks = chunks + lag_b + jnp.where(z < half, 0, ahead)

    def gather_tick(k):
        pl.when(k < all_chunks)(lambda: gather_line(k))
        pl.when((k >= lag_a) & (k < all_chunks + lag_a))(lambda: gather_a(k - lag_a))
        pl.when((k >= lag_b) & (k < all_chunks + lag_b))(lambda: gather_b(k - lag_b))

    each(0, cuts, lambda piece: far_copy(piece).start())
    early = min(2, START_TICKS, chunks)
    each(0, early, gather_tick)

    hot, hot_t, act_hot = r.hot, r.hot_t, r.act_hot
    for t in range(horizon):
        r.latent_row[:, t * cap : (t + 1) * cap] = r.latent[t].astype(F32)
        r.action_row[:, t * cap : (t + 1) * cap] = r.action[t : t + 1].astype(F32)
    latent_row = r.latent_row[...].astype(BF16)
    spread_rows = (iota((LATENTS, STOCH), 1) // CLASSES == iota((LATENTS, STOCH), 0)).astype(F32).astype(BF16)
    class_row = (iota((1, STOCH), 1) % CLASSES).astype(F32)
    latent_col = latent_row.T
    for k in range(total // 128):
        seen = dot(latent_col[128 * k : 128 * (k + 1)], spread_rows)
        hot[128 * k : 128 * (k + 1)] = jnp.where(seen == class_row, 1.0, 0.0).astype(BF16)

    def hot_t_block(k):
        block = pl.ds(mult(k * 128, 128), 128)
        first = k * 128
        spread = ((iota((128, LATENTS), 0) + first) // CLASSES == iota((128, LATENTS), 1)).astype(F32).astype(BF16)
        seen = dot(spread, latent_row)
        class_col = ((iota((128, 1), 0) + first) % CLASSES).astype(F32)
        hot_t[block] = jnp.where(seen == class_col, 1.0, 0.0).astype(BF16)

    each(0, STOCH // 128, hot_t_block)
    act_hot[...] = jnp.where(r.action_row[...] == iota((128, total), 0).astype(F32), 1.0, 0.0).T.astype(BF16)

    r.embed_pad[...] = jnp.zeros((32, DET), BF16)
    r.embed_pad[0:ACTIONS] = r.act_embed[...]
    r.head_pad[...] = jnp.zeros((128, DET), BF16)
    r.head_pad[0:ACTIONS] = r.actor_head[...]
    r.small[...] = jnp.zeros(r.small.shape, F32)

    middle_ticks = min(START_TICKS, chunks + lag_b)
    each(early, middle_ticks, gather_tick)
    out_begin()
    each(middle_ticks, first_ticks, gather_tick)

    each(0, chunks, gather_shared)

    shuffle = r.shuffle
    row_i = iota((TALL, TALL), 0)
    shuffle[...] = jnp.where(
        iota((TALL, TALL), 1) == 3 * (row_i % 128) + row_i // 128, 1.0, 0.0
    ).astype(BF16)
    w_gru = r.w_gru
    for j in range(8):
        block = full[ROW_GRU + TALL * j : ROW_GRU + TALL * (j + 1)]
        sorted_rows = dot(shuffle[...], block).astype(BF16)
        for k in range(3):
            w_gru[128 * j : 128 * (j + 1), DET * k : DET * (k + 1)] = sorted_rows[128 * k : 128 * (k + 1)]
    w_back = full.at[ROW_GRU : ROW_GRU + GATES]
    pre, inputs, raw = r.pre, r.inputs, r.raw
    low, work = r.low, r.work
    a_one_at, a_two_at, g_one, g_two = 0, 2 * DET, 4 * DET, 6 * DET
    p_low = GATES
    inputs[steps_rows:total] = jnp.zeros((total - steps_rows, DET), BF16)
    pre_block = 5 * cap

    def pre_step(k):
        block = pl.ds(mult(k * pre_block, 16), pre_block)
        value = dot(hot[block], full[ROW_WIN : ROW_WIN + STOCH])
        value = value + dot(act_hot[block][:, 0:32], r.embed_pad[...])
        pre[block] = value
        active = elu(value).astype(BF16)
        inputs[block] = active
        raw[block] = dot(active, w_gru[0:DET])
        pl.when(z < half)(lambda: gather_tick(first_ticks + k))

    pre_blocks = (horizon - 1) // 5
    each(0, pre_blocks, pre_step)

    out_finish()
    r.start[...] = jnp.zeros((128, DET + META), F32)

    def from_lanes(k):
        block = pl.ds(mult(k * tall, 16), tall)
        got = r.got[block]
        put = jnp.where(got[:, DET : DET + 1].astype(F32) == (iota((tall, 128), 1) + 1).astype(F32), 1.0, 0.0).astype(BF16)
        r.placing[block] = put
        r.start[...] += dot_t(put, got)

    each(0, lanes // tall, from_lanes)
    start = r.start
    states_ref = r.states
    states_ref[0:cap] = start[0:cap, 0:DET]
    mask = start[0:cap, DET + 1 : DET + 2]
    eye = iota((cap, cap), 0) == iota((cap, cap), 1)
    mask_row = jnp.sum(jnp.where(eye, mask, 0.0), axis=0, keepdims=True)
    adv = r.adv
    running = jnp.zeros((1, cap), F32)
    sum_one = jnp.zeros((1, cap), F32)
    sum_two = jnp.zeros((1, cap), F32)
    for t in range(horizon - 1, -1, -1):
        running = r.rewards[t : t + 1] + discount * running
        sum_one = sum_one + mask_row * running
        sum_two = sum_two + mask_row * running * running
        r.returns[:, t * cap : (t + 1) * cap] = running
        r.weight_row[:, t * cap : (t + 1) * cap] = mask_row * (1.0 / horizon)
    tile_lane = iota((8, 128), 1)

    def total_of(value):
        return jnp.sum(value, axis=1, keepdims=True)

    sums = jnp.where(
        tile_lane == 0,
        total_of(sum_one),
        jnp.where(tile_lane == 1, total_of(sum_two), jnp.where(tile_lane == 2, horizon * total_of(mask_row), 0.0)),
    )
    moments, pair = r.moments, r.pair
    pair[0] = sums
    swap = remote(pair.at[0], pair.at[1], r.pair_sem.at[0], r.pair_sem.at[1], me, sibling)
    swap.start()
    swap.wait()
    moments[me] = pair[0] + pair[1]

    def moments_copy(k):
        peer = (me + k) % n
        return remote(moments.at[me], moments.at[me], r.mo_send.at[k], r.mo_recv.at[k], peer)

    def moments_landing(k):
        peer = (me + n - k) % n
        return remote(moments.at[peer], moments.at[peer], r.mo_send.at[k], r.mo_recv.at[k], peer)

    each(1, n, lambda k: moments_copy(k).start())

    def as_row(ref):
        value = ref[...].astype(F32)
        return jnp.concatenate([value[k : k + 1] for k in range(ref.shape[0])], axis=-1)

    gain = as_row(r.gain)
    bias = as_row(r.bias)
    update_ref, inv_ref = r.update, r.inv

    each(0, chunks, gather_drain)
    each(0, cuts, lambda piece: pl.when(z < half)(far_copy(piece).wait_send))
    scan_first = first_ticks + jnp.where(z < half, pre_blocks, 0)

    def forward_step(t):
        block = pl.ds(mult(t * cap, 16), cap)
        state = states_ref[block]
        state_low = state.astype(BF16)
        low[block] = state_low
        gru_raw = raw[block] + dot(state_low, w_gru[DET:])
        centred = gru_raw - jnp.mean(gru_raw, axis=-1, keepdims=True)
        inv_std = lax.rsqrt(jnp.mean(centred * centred, axis=-1, keepdims=True) + norm_eps)
        normed = centred * inv_std
        raw[block] = normed
        inv_ref[block] = jnp.broadcast_to(inv_std, (cap, 128))
        mixed = normed * gain + bias
        reset = jax.nn.sigmoid(mixed[:, :DET])
        candidate = jnp.tanh(reset * mixed[:, DET : 2 * DET])
        update = jax.nn.sigmoid(mixed[:, 2 * DET :] - 1.0)
        update_ref[block] = update
        states_ref[pl.ds(mult(t * cap + cap, 16), cap)] = update * candidate + (1.0 - update) * state
        j, k = t % 12 // 3, t % 3
        w_back[pl.ds(mult(DET * k, DET), DET), pl.ds(mult(128 * j, 128), 128)] = w_gru[
            pl.ds(mult(DET + 128 * j, 128), 128), pl.ds(mult(DET * k, DET), DET)
        ].T

    group = 3 if (horizon - 1) % 3 == 0 else 1
    rounds = (horizon - 1) // group

    def forward_round(m):
        for k in range(group):
            forward_step(m * group + k)
        gather_tick(scan_first + m)

    each(0, rounds, forward_round)
    done_ticks = scan_first + rounds
    each(done_ticks, jnp.maximum(ticks, done_ticks), gather_tick)
    low[steps_rows:total] = states_ref[steps_rows:total].astype(BF16)
    each(chunks, 2 * chunks, gather_shared)

    each(1, n, lambda k: moments_landing(k).wait_recv())
    sums = moments[0]
    for k in range(1, n):
        sums = sums + moments[k]
    centre = sums[0:1, 0:1] / sums[0:1, 2:3]
    spread = jnp.sqrt(sums[0:1, 1:2] / sums[0:1, 2:3] - centre * centre + norm_eps)
    per_row = jnp.concatenate(
        [(r.returns[...] - centre) / spread, r.weight_row[...], jnp.zeros((126, total), F32)], axis=0
    ).T
    adv[...] = per_row

    grads = r.grads

    def keep_grads(first, value):
        for c in range(4):
            grads[c, pl.ds(first, value.shape[0])] = value[:, 128 * c : 128 * (c + 1)]

    def load_grads(block):
        return jnp.concatenate([grads[c, block] for c in range(4)], axis=-1)

    def grad_rows(local, part, piece):
        return pl.ds(mult(local * rows + part * (rows // 2) + piece * prow, 16), prow)

    def store_grads(block, value):
        for c in range(4):
            grads[c, block] = value[:, 128 * c : 128 * (c + 1)]

    pair_in, b_in, a_in, z_in = r.pair_in, r.b_in, r.a_in, r.z_in

    class Reducer:
        def __init__(self, group):
            self.group = group
            self.turn = half // 2 if group == 0 else 0

        def target(self, i):
            return (i // parts + self.turn) % half, i % parts

        def sem(self, array, *at):
            return array.at[(self.group,) + at]

        def out_rows(self, t, offset, piece, count):
            return pl.ds(mult(ROW_A1 + t * 4 * rows + offset + piece * count * prow, 16), count * prow)

        def in_rows(self, t, piece, count):
            return pl.ds(mult((t * parts + piece) * count * prow, 16), count * prow)

        def pair_copy(self, t, piece):
            return remote(
                full.at[self.out_rows(t, 0, piece, 4)],
                pair_in.at[self.in_rows(t, piece, 4)],
                self.sem(r.pair_s, t, piece),
                self.sem(r.pair_r, t, piece),
                me,
                sibling,
            )

        def b_copy(self, t, piece):
            return remote(
                full.at[self.out_rows(t, 2 * rows, piece, 2)],
                b_in.at[self.group, self.in_rows(t, piece, 2)],
                self.sem(r.b_s, t, piece),
                self.sem(r.b_r, t, piece),
                b_dev,
            )

        def a_copy(self, t, piece):
            return remote(
                full.at[self.out_rows(t, 3 * rows, piece, 1)],
                a_in.at[self.group, self.in_rows(t, piece, 1)],
                self.sem(r.a_s, t, piece),
                self.sem(r.a_r, t, piece),
                a_dev,
            )

        def z_slot(self, b, t):
            return sum(half // 2 ** (k + 1) for k in range(b)) + t // 2 ** (b + 1)

        def z_copy(self, b, t, piece):
            slot = self.z_slot(b, t)
            return remote(
                full.at[self.out_rows(t, 3 * rows + rows // 2, piece, 1)],
                z_in.at[self.group, self.in_rows(slot, piece, 1)],
                self.sem(r.z_s, t, piece),
                self.sem(r.z_r, slot, piece),
                across(b),
            )

        def holds(self, b, t):
            return (z - t - self.group * half) % 2**b == 0

        def differs(self, b, t):
            return bit_of(z, b) != bit_of(t + self.group * half, b)

        def fin_rows(self, piece, part):
            return pl.ds(mult((part * (rows // 2) + piece * prow) * 4, 16), prow * 4)

        def fin_copy(self, piece, part=None):
            block = self.fin_rows(piece, core if part is None else part)
            return remote(
                r.weights_grad.at[block], r.weights_grad.at[block], r.fin_s.at[piece], r.fin_r.at[piece], me, sibling
            )

        def load(self, t, piece, a):
            if self.group == 0:
                return load_grads(grad_rows(t * 4 + a * a_step + b_bit * b_step, core, piece))
            return r.kept[(t * parts + piece) * 2 + a]

        def store(self, t, piece, a, value):
            if self.group == 0:
                store_grads(grad_rows(t * 4 + a * a_step + b_bit * b_step, core, piece), value)
            else:
                r.kept[(t * parts + piece) * 2 + a] = value

        def to_pair(self, i):
            t, piece = self.target(i)
            for k in range(4):
                block = pl.ds(mult(ROW_A1 + t * 4 * rows + (piece * 4 + k) * prow, 16), prow)
                full[block] = load_grads(grad_rows(t * 4 + k, sibling, piece)).astype(BF16)
            self.pair_copy(t, piece).start()

        def to_b(self, i):
            t, piece = self.target(i)
            self.pair_copy(t, piece).wait_recv()

            def both_cores(where):
                spot = pl.ds(mult(((t * parts + piece) * 4 + where) * prow, 16), prow)
                return load_grads(grad_rows(t * 4 + where, core, piece)) + pair_in[spot].astype(F32)

            for a in range(2):
                block = pl.ds(mult(ROW_A1 + t * 4 * rows + 2 * rows + (piece * 2 + a) * prow, 16), prow)
                full[block] = both_cores(a * a_step + (1 - b_bit) * b_step).astype(BF16)
            self.b_copy(t, piece).start()
            for a in range(2):
                self.store(t, piece, a, both_cores(a * a_step + b_bit * b_step))

        def b_part(self, t, piece, a):
            spot = pl.ds(mult(((t * parts + piece) * 2 + a) * prow, 16), prow)
            return b_in[self.group, spot].astype(F32)

        def to_a(self, i):
            t, piece = self.target(i)
            self.b_copy(t, piece).wait_recv()
            other = 1 - a_bit
            if self.group == 0:
                heads_rs.a_copy(t, piece).wait_send()
            full[self.out_rows(t, 3 * rows, piece, 1)] = (
                self.load(t, piece, other) + self.b_part(t, piece, other)
            ).astype(BF16)
            self.a_copy(t, piece).start()
            self.store(t, piece, a_bit, self.load(t, piece, a_bit) + self.b_part(t, piece, a_bit))

        def to_plane(self, b, i):
            t, piece = self.target(i)

            @pl.when(self.holds(b, t))
            def _():
                if b == 0:
                    self.a_copy(t, piece).wait_recv()
                    came = a_in[self.group, self.in_rows(t, piece, 1)]
                else:
                    self.z_copy(b - 1, t, piece).wait_recv()
                    came = z_in[self.group, self.in_rows(self.z_slot(b - 1, t), piece, 1)]
                value = self.load(t, piece, a_bit) + came.astype(F32)
                if b == bits:
                    first = mult((core * (rows // 2) + piece * prow) * 4, 16)
                    for c in range(4):
                        r.weights_grad[pl.ds(first + c, prow, stride=4), :] = value[:, 128 * c : 128 * (c + 1)]
                    self.fin_copy(piece).start()
                else:

                    @pl.when(self.differs(b, t))
                    def _():
                        if self.group == 0:
                            heads_rs.plane_gone(t, piece)
                        full[self.out_rows(t, 3 * rows + rows // 2, piece, 1)] = value.astype(BF16)
                        self.z_copy(b, t, piece).start()

                    pl.when(~self.differs(b, t))(lambda: self.store(t, piece, a_bit, value))

        def drain_early(self, i):
            t, piece = self.target(i)
            self.pair_copy(t, piece).wait_send()
            self.b_copy(t, piece).wait_send()

        def plane_gone(self, t, piece):
            for b in range(bits):
                pl.when(self.holds(b, t) & self.differs(b, t))(self.z_copy(b, t, piece).wait_send)

        def drain(self, i):
            t, piece = self.target(i)
            if self.group == 0:
                self.a_copy(t, piece).wait_send()
                self.plane_gone(t, piece)
            else:
                for b in range(bits):
                    waited = False
                    for c in range(bits):
                        waited = waited | (gru_rs.holds(c, t) & gru_rs.differs(c, t))
                    pl.when(self.holds(b, t) & self.differs(b, t) & ~waited)(self.z_copy(b, t, piece).wait_send)

            @pl.when(self.holds(bits, t))
            def _():
                self.fin_copy(piece).wait_send()
                self.fin_copy(piece, sibling).wait_recv()

    heads_rs, gru_rs = Reducer(1), Reducer(0)
    net_items = items // 2

    def of_item(k, stage):
        pl.when((k >= 0) & (k < items))(lambda: stage(heads_rs, k))
        pl.when((k >= items) & (k < 2 * items))(lambda: stage(gru_rs, k - items))

    def rs_tick(k):
        of_item(k, lambda rs, i: rs.to_a(i))
        for b in range(bits + 1):
            of_item(k - LAG_Z * (b + 1), lambda rs, i, b=b: rs.to_plane(b, i))

    rs_ticks = 2 * items + LAG_Z * (bits + 1)

    out_grads, state_grads = r.out_grads, r.state_grads
    r.loss_acc[...] = jnp.zeros((plan.block, 128), F32)
    critic_row = as_row(r.critic_head)
    lane_id = iota((plan.block, 128), 1)

    def net_rows(side):
        return (ROW_A1, ROW_A2) if side == 0 else (ROW_C1, ROW_C2)

    def net_cols(base, side):
        return slice(base + side * DET, base + (side + 1) * DET)

    def net_step(k, side):
        first, second = net_rows(side)
        block = pl.ds(mult(k * plan.block, 64), plan.block)
        one = dot(low[block], full[first : first + DET]) + dot(hot[block], full[first + DET : first + DET + STOCH])
        one_low = elu(one).astype(BF16)
        work[block, net_cols(a_one_at, side)] = one_low
        two = dot(one_low, full[second : second + DET])
        two_low = elu(two).astype(BF16)
        work[block, net_cols(a_two_at, side)] = two_low
        advantage = adv[block][:, 0:1]
        weight = adv[block][:, 1:2]
        if side == 0:
            real = lane_id < ACTIONS
            logits = jnp.where(real, dot_nt(two_low, r.head_pad[...]), -1e30)
            shifted = logits - jnp.max(logits, axis=-1, keepdims=True)
            powers = jnp.where(real, jnp.exp(shifted), 0.0)
            norm = jnp.sum(powers, axis=-1, keepdims=True)
            log_probs = jnp.where(real, shifted - jnp.log(norm), 0.0)
            probs = powers / norm
            taken = act_hot[block].astype(F32)
            chosen = jnp.sum(taken * log_probs, axis=-1, keepdims=True)
            entropy = -jnp.sum(probs * log_probs, axis=-1, keepdims=True)
            r.loss_acc[...] += weight * (-advantage * chosen - entropy_weight * entropy)
            grad_logits = weight * (
                -advantage * (taken - probs) + entropy_weight * probs * (log_probs + entropy)
            )
            both = grad_logits.astype(BF16)
            out_grads[block] = both
            back = dot(both, r.head_pad[...])
        else:
            value = jnp.sum(two_low.astype(F32) * critic_row, axis=-1, keepdims=True)
            gap = value - advantage
            r.loss_acc[...] += weight * (0.5 * gap * gap)
            value_low = (weight * gap).astype(BF16).astype(F32)
            out_grads[block] = jnp.where(lane_id == ACTIONS, value_low, out_grads[block].astype(F32)).astype(BF16)
            back = value_low * critic_row
        back_low = (back * elu_grad(two)).astype(BF16)
        work[block, net_cols(g_two, side)] = back_low
        low_one = (dot_nt(back_low, full[second : second + DET]) * elu_grad(one)).astype(BF16)
        work[block, net_cols(g_one, side)] = low_one
        state_part = dot_nt(low_one, full[first : first + DET])
        if side == 0:
            state_grads[block] = state_part
        else:
            state_grads[block] += state_part

    def net_grads(side):
        base = side * 2048
        for j in range(2):
            part = slice(j * WIDE, (j + 1) * WIDE)
            keep_grads(base + j * WIDE, dot_t(low[:, part], work[:, net_cols(g_one, side)]))
            at = a_one_at + side * DET + j * WIDE
            keep_grads(base + GATES + j * WIDE, dot_t(work[:, at : at + WIDE], work[:, net_cols(g_two, side)]))

        def latent_part(k):
            part = pl.ds(mult(k * WIDE, WIDE), WIDE)
            keep_grads(mult(base + DET + k * WIDE, WIDE), dot(hot_t[part], work[:, net_cols(g_one, side)]))

        each(0, STOCH // WIDE, latent_part)

    blocks = total // plan.block
    each(0, blocks, lambda k: net_step(k, 0))
    net_grads(0)
    each(chunks, 2 * chunks, gather_drain)
    each(0, cuts, lambda piece: pl.when(z >= half)(far_copy(piece).wait_send))
    each(0, net_items, heads_rs.to_pair)
    net_step(0, 1)
    each(0, net_items, heads_rs.to_b)
    each(1, blocks, lambda k: net_step(k, 1))
    each(0, net_items // 2, rs_tick)
    net_grads(1)
    each(net_items, items, heads_rs.to_pair)
    each(net_items // 2, net_items, rs_tick)

    small = r.small
    head_grad = dot_t(out_grads[...], work[:, a_two_at : a_two_at + 2 * DET])
    small[SM_ACTOR : SM_ACTOR + 24] = head_grad[0:24, 0:WIDE]
    small[SM_ACTOR + 24 : SM_ACTOR + 48] = head_grad[0:24, WIDE:DET]
    small[SM_CRITIC : SM_CRITIC + 1] = head_grad[ACTIONS : ACTIONS + 1, DET : DET + WIDE]
    small[SM_CRITIC + 1 : SM_CRITIC + 2] = head_grad[ACTIONS : ACTIONS + 1, DET + WIDE :]
    small[SM_LOSS : SM_LOSS + 1, 0:128] = jnp.sum(r.loss_acc[...], axis=0, keepdims=True)

    scan_ticks = net_items + rounds - 1

    gain_acc, bias_acc = r.gain_acc, r.bias_acc
    gain_acc[...] = jnp.zeros((8, GATES), F32)
    bias_acc[...] = jnp.zeros((8, GATES), F32)
    carry_ref = r.carry
    carry_ref[...] = state_grads[steps_rows:total]
    work[steps_rows:total, 0 : 4 * DET] = jnp.zeros((total - steps_rows, 4 * DET), BF16)
    gain_mid, bias_mid = gain[:, DET : 2 * DET], bias[:, DET : 2 * DET]

    def fold(value):
        out = value[0:8]
        for k in range(1, cap // 8):
            out = out + value[8 * k : 8 * (k + 1)]
        return out

    def backward_step(index):
        t = horizon - 2 - index
        block = pl.ds(mult(t * cap, 16), cap)
        carry = carry_ref[...]
        normed = raw[block]
        inv_std = inv_ref[block][:, 0:1]
        reset = jax.nn.sigmoid(normed[:, :DET] * gain[:, :DET] + bias[:, :DET])
        update = update_ref[block]
        state = states_ref[block]
        middle = normed[:, DET : 2 * DET] * gain_mid + bias_mid
        candidate = jnp.tanh(reset * middle)
        inner = carry * update * (1.0 - candidate * candidate)
        part = jnp.concatenate(
            [
                inner * middle * reset * (1.0 - reset),
                inner * reset,
                carry * (candidate - state) * update * (1.0 - update),
            ],
            axis=-1,
        )
        gain_acc[...] += fold(part * normed)
        bias_acc[...] += fold(part)
        normed_grad = part * gain
        raw_grad = inv_std * (
            normed_grad
            - jnp.mean(normed_grad, axis=-1, keepdims=True)
            - normed * jnp.mean(normed_grad * normed, axis=-1, keepdims=True)
        )
        grad_low = raw_grad.astype(BF16)
        work[block, 0:GATES] = grad_low
        carry_ref[...] = carry * (1.0 - update) + dot(grad_low, w_back[...]) + state_grads[block]

    def backward_round(m):
        pl.when(m == 0)(lambda: each(net_items, items, heads_rs.to_b))
        for k in range(group):
            backward_step(m * group + k)
        pl.when(m > 0)(lambda: rs_tick(net_items + m - 1))

    each(0, rounds, backward_round)

    back_begin, back_finish, back_drain = exchange(DET, r.bk_send, r.bk_recv)
    out_drain()
    start_grads = carry_ref[...].astype(BF16)

    def back_lanes(k):
        block = pl.ds(mult(k * tall, 16), tall)
        r.sent[block, :DET] = dot(r.placing[block][:, 0:cap], start_grads).astype(BF16)

    each(0, lanes // tall, back_lanes)
    back_begin()

    each(0, items, heads_rs.drain_early)
    pl.semaphore_signal(r.credit, inc=1, device_id=(me, sibling), device_id_type=MESH)
    def gru_part(j):
        source = inputs if j < 2 else low
        part = slice((j % 2) * WIDE, (j % 2 + 1) * WIDE)
        for k in range(3):
            value = dot_t(source[:, part], work[:, DET * k : DET * (k + 1)])
            for c in range(4):
                grads[c, pl.ds(ROW_GRU + k + 768 * j, WIDE, stride=3), :] = value[:, 128 * c : 128 * (c + 1)]

    for j in (3, 2, 1):
        gru_part(j)
    pl.semaphore_wait(r.credit, 1)
    each(0, net_items, gru_rs.to_pair)

    def pre_back(k):
        block = pl.ds(mult(k * pre_block, 16), pre_block)
        value = dot_nt(work[block, 0:GATES], w_gru[0:DET])
        work[block, p_low : p_low + DET] = (value * elu_grad(pre[block])).astype(BF16)

    each(0, pre_blocks, pre_back)
    ready = min(scan_ticks, items)
    each(ready, items, rs_tick)
    ready = max(ready, items)
    each(0, net_items, gru_rs.to_b)
    gru_part(0)

    def win_part(k):
        part = pl.ds(mult(k * WIDE, WIDE), WIDE)
        keep_grads(mult(k * WIDE, WIDE), dot(hot_t[part], work[:, p_low : p_low + DET]))

    each(0, STOCH // WIDE, win_part)
    each(net_items, items, gru_rs.to_pair)
    step_ticks = max(net_items // 4, 1)
    each(ready, ready + step_ticks, rs_tick)
    each(net_items, items, gru_rs.to_b)
    each(ready + step_ticks, ready + 2 * step_ticks, rs_tick)
    ready += 2 * step_ticks
    embed_grad = dot_t(act_hot[...], work[:, p_low : p_low + DET])
    small[SM_EMBED : SM_EMBED + 24] = embed_grad[0:24, 0:WIDE]
    small[SM_EMBED + 24 : SM_EMBED + 48] = embed_grad[0:24, WIDE:DET]
    gain_sum = jnp.sum(gain_acc[...], axis=0, keepdims=True)
    bias_sum = jnp.sum(bias_acc[...], axis=0, keepdims=True)
    for k in range(GATES // WIDE):
        small[SM_GAIN + k : SM_GAIN + k + 1] = gain_sum[:, k * WIDE : (k + 1) * WIDE]
        small[SM_BIAS + k : SM_BIAS + k + 1] = bias_sum[:, k * WIDE : (k + 1) * WIDE]

    small_in, scattered = r.small_in, r.scattered
    summed = small_in
    swap_small = remote(small, small_in, r.pair_sem.at[2], r.pair_sem.at[3], me, sibling)
    small_sum = small

    def eight(k):
        return pl.ds(mult(k * 8, 8), 8)

    def scatter_copy(k):
        peer = (me + k) % n
        return remote(small_sum.at[eight(peer)], scattered.at[me], r.sc_send.at[k], r.sc_recv.at[k], peer)

    def scatter_landing(k):
        peer = (me + n - k) % n
        return remote(small_sum.at[eight(me)], scattered.at[peer], r.sc_send.at[k], r.sc_recv.at[k], peer)

    def summed_copy(k):
        peer = (me + k) % n
        return remote(summed.at[eight(me)], summed.at[eight(me)], r.sm_send.at[k], r.sm_recv.at[k], peer)

    def summed_landing(k):
        peer = (me + n - k) % n
        return remote(summed.at[eight(peer)], summed.at[eight(peer)], r.sm_send.at[k], r.sm_recv.at[k], peer)

    def scatter_small():
        swap_small.wait()
        small_sum[...] = small[...] + small_in[...]
        scattered[me] = small_sum[eight(me)]
        each(1, n, lambda k: scatter_copy(k).start())

    def spread_small():
        each(1, n, lambda k: scatter_landing(k).wait_recv())
        block_sum = scattered[0]
        for k in range(1, n):
            block_sum = block_sum + scattered[k]
        summed[eight(me)] = block_sum
        each(1, n, lambda k: summed_copy(k).start())

    swap_small.start()
    between = (SCATTER_TICKS, scatter_small), (SPREAD_TICKS, spread_small)
    for before_end, run in between:
        until = max(ready, rs_ticks - before_end)
        each(ready, until, rs_tick)
        ready = until
        run()
    each(ready, rs_ticks, rs_tick)
    each(0, items, heads_rs.drain)

    back_finish()
    r.start_grad[...] = jnp.zeros((slots, DET), F32)

    def frames(k):
        block = pl.ds(mult(k * tall, 16), tall)
        r.start_grad[...] += dot_t(r.to_lane[block], r.got[block][:, 0:DET])

    each(0, lanes // tall, frames)
    each(1, n, lambda k: summed_landing(k).wait_recv())
    r.loss[...] = summed[SM_LOSS : SM_LOSS + 1, 0:1]
    r.embed_grad[:, 0:WIDE] = summed[SM_EMBED : SM_EMBED + ACTIONS]
    r.embed_grad[:, WIDE:DET] = summed[SM_EMBED + 24 : SM_EMBED + 24 + ACTIONS]
    for k in range(GATES // WIDE):
        for h in range(2):
            lanes_of = slice(h * 128, (h + 1) * 128)
            r.gain_grad[2 * k + h : 2 * k + h + 1] = summed[SM_GAIN + k : SM_GAIN + k + 1, lanes_of]
            r.bias_grad[2 * k + h : 2 * k + h + 1] = summed[SM_BIAS + k : SM_BIAS + k + 1, lanes_of]
    for k in range(2):
        for h in range(2):
            lanes_of = slice(h * 128, (h + 1) * 128)
            r.critic_grad[2 * k + h : 2 * k + h + 1] = summed[SM_CRITIC + k : SM_CRITIC + k + 1, lanes_of]
    r.actor_grad[:, 0:WIDE] = summed[SM_ACTOR : SM_ACTOR + ACTIONS]
    r.actor_grad[:, WIDE:DET] = summed[SM_ACTOR + 24 : SM_ACTOR + 24 + ACTIONS]
    each(0, items, gru_rs.drain_early)
    each(0, items, gru_rs.drain)

    back_drain()
    each(1, n, lambda k: moments_copy(k).wait_send())
    each(1, n, lambda k: scatter_copy(k).wait_send())
    each(1, n, lambda k: summed_copy(k).wait_send())


def hand_over(*refs):
    count = len(refs) // 2
    for k in range(count):
        refs[count + k][...] = refs[k][...]


def on_device(
    start_deter,
    frame_mask,
    counts,
    route,
    weights_flat,
    act_embed,
    gru_gain,
    gru_bias,
    actor_head,
    critic_head,
    latent_idx,
    action_idx,
    rewards,
):
    n = lax.axis_size("dp")
    slots = start_deter.shape[0]
    cap, horizon = action_idx.shape
    shard = weights_flat.shape[0]
    plan = Plan(n, slots, cap, horizon, shard * n // DET)
    total, steps_rows, lanes = plan.all_rows, plan.step_rows, n * plan.lane
    line, half, parts, prow, items = plan.line, plan.half, plan.parts, plan.part_rows, plan.items
    inputs = dict(
        start_deter=start_deter,
        frame_mask=frame_mask.reshape(1, slots),
        counts=counts.reshape(1, 1),
        route=route.reshape(1, slots),
        weights=weights_flat.reshape(plan.rows * 4, 128),
        act_embed=act_embed,
        gain=gru_gain.reshape(GATES // 128, 128),
        bias=gru_bias.reshape(GATES // 128, 128),
        actor_head=actor_head.T,
        critic_head=critic_head.reshape(DET // 128, 128),
        latent=jnp.transpose(latent_idx, (1, 2, 0)),
        action=action_idx.T,
        rewards=rewards.T,
    )
    outputs = dict(
        loss=(1, 1),
        start_grad=(slots, DET),
        weights_grad=(plan.rows * 4, 128),
        embed_grad=(ACTIONS, DET),
        gain_grad=(GATES // 128, 128),
        bias_grad=(GATES // 128, 128),
        actor_grad=(ACTIONS, DET),
        critic_grad=(DET // 128, 128),
    )
    group_rows = half * 4 * plan.rows
    half_rows = group_rows // 2
    scratch = dict(
        narrow=((plan.rows * 2, 128), F32),
        latent_row=((LATENTS, total), F32),
        action_row=((1, total), F32),
        returns=((1, total), F32),
        weight_row=((1, total), F32),
        kept=((2 * items, prow, DET), F32),
        full=((n * plan.rows, DET), BF16),
        start=((128, DET + META), F32),
        to_lane=((lanes, slots), BF16),
        sent=((lanes, DET + META), BF16),
        got=((lanes, DET + META), BF16),
        placing=((lanes, 128), BF16),
        hot=((total, STOCH), BF16),
        hot_t=((STOCH, total), BF16),
        act_hot=((total, 128), BF16),
        embed_pad=((32, DET), BF16),
        head_pad=((128, DET), BF16),
        small=((plan.small, WIDE), F32),
        small_in=((plan.small, WIDE), F32),
        scattered=((n, 8, WIDE), F32),
        states=((total, DET), F32),
        adv=((total, 128), F32),
        pair=((2, 8, 128), F32),
        moments=((n, 8, 128), F32),
        shuffle=((TALL, TALL), BF16),
        w_gru=((STOCH, GATES), BF16),
        pre=((steps_rows, DET), F32),
        inputs=((total, DET), BF16),
        work=((total, 8 * DET), BF16),
        raw=((steps_rows, GATES), F32),
        low=((total, DET), BF16),
        update=((steps_rows, DET), F32),
        inv=((steps_rows, 128), F32),
        out_grads=((total, 128), BF16),
        state_grads=((total, DET), F32),
        loss_acc=((plan.block, 128), F32),
        grads=((4, group_rows, 128), F32),
        pair_in=((half_rows, DET), BF16),
        b_in=((2, half_rows // 2, DET), BF16),
        a_in=((2, half_rows // 4, DET), BF16),
        z_in=((2, half_rows // 4, DET), BF16),
        gain_acc=((8, GATES), F32),
        bias_acc=((8, GATES), F32),
        carry=((cap, DET), F32),
    )
    semaphores = dict(
        ex_send=(n,),
        ex_recv=(n,),
        bk_send=(n,),
        bk_recv=(n,),
        mo_send=(n,),
        mo_recv=(n,),
        sc_send=(n,),
        sc_recv=(n,),
        sm_send=(n,),
        sm_recv=(n,),
        pair_sem=(4,),
        ag_recv=(n, plan.cuts),
        sh_recv=(n, plan.cuts),
        far_send=(plan.cuts,),
        line_send=(line, plan.cuts, max(plan.bits - 1, 1)),
        a_send=(line, plan.cuts),
        b_send=(line, plan.cuts, 2),
        sh_send=(line, plan.cuts, 4),
        pair_s=(2, half, parts),
        pair_r=(2, half, parts),
        b_s=(2, half, parts),
        b_r=(2, half, parts),
        a_s=(2, half, parts),
        a_r=(2, half, parts),
        z_s=(2, half, parts),
        z_r=(2, half, parts),
        fin_s=(parts,),
        fin_r=(parts,),
    )
    names = list(inputs) + list(outputs) + list(scratch) + list(semaphores) + list(dict(credit=0))
    vmem = pl.BlockSpec(memory_space=pltpu.VMEM)
    found = pl.pallas_call(
        functools.partial(kernel_body, plan, names),
        out_shape=[jax.ShapeDtypeStruct(shape, F32) for shape in outputs.values()],
        in_specs=[vmem] * len(inputs),
        out_specs=[vmem] * len(outputs),
        scratch_shapes=[pltpu.VMEM(shape, dtype) for shape, dtype in scratch.values()]
        + [pltpu.SemaphoreType.DMA(shape) for shape in semaphores.values()]
        + [pltpu.SemaphoreType.REGULAR],
        compiler_params=pltpu.CompilerParams(
            collective_id=0, has_side_effects=True, vmem_limit_bytes=127 * 2**19
        ),
    )(*inputs.values())
    found = pl.pallas_call(
        hand_over,
        out_shape=[jax.ShapeDtypeStruct(shape, F32) for shape in outputs.values()],
        in_specs=[vmem] * len(outputs),
        out_specs=[vmem] * len(outputs),
    )(*found)
    loss, start_grad, weights_grad, embed_grad, gain_grad, bias_grad, actor_grad, critic_grad = found
    return (
        loss.reshape(()),
        start_grad,
        weights_grad.reshape(shard),
        embed_grad,
        gain_grad.reshape(GATES),
        bias_grad.reshape(GATES),
        actor_grad.T,
        critic_grad.reshape(DET),
    )


def solution(mesh):
    return jax.shard_map(
        on_device,
        mesh=mesh,
        in_specs=(
            P(("dp", "rep"), None),
            P(("dp", "rep")),
            P(("dp", "rep")),
            P(("dp", "rep")),
            P("dp"),
            P(),
            P(),
            P(),
            P(),
            P(),
            P(("dp", "rep"), None, None),
            P(("dp", "rep"), None),
            P(("dp", "rep"), None),
        ),
        out_specs=(P(), P(("dp", "rep"), None), P("dp"), P(), P(), P(), P(), P()),
        check_vma=False,
    )
```

```python
import functools
from types import SimpleNamespace

import jax
import jax.numpy as jnp
from jax import lax
from jax.experimental import pallas as pl
from jax.experimental.pallas import tpu as pltpu
from jax.sharding import PartitionSpec as P

DET = 512
CLASSES = 32
LATENTS = 32
ACTIONS = 18
STOCH = 1024
GATES = 1536
WIDE = 256
META = 128
TALL = 384
LAG_A, LAG_B, LAG_Z = 2, 4, 2
GATHER_PARTS = 4
AHEAD = 4
SCATTER_TICKS, SPREAD_TICKS = 11, 4
START_TICKS = 3

discount = 0.99
entropy_weight = 0.1
norm_eps = 1e-05

F32 = jnp.float32
BF16 = jnp.bfloat16
MESH = pl.DeviceIdType.MESH

ROW_WIN, ROW_GRU, ROW_A1, ROW_A2, ROW_C1, ROW_C2 = 0, 1024, 4096, 5632, 6144, 7680
SM_EMBED, SM_GAIN, SM_BIAS, SM_ACTOR, SM_CRITIC, SM_LOSS = 0, 48, 54, 64, 112, 114


def dot(left, right):
    return jnp.dot(left, right, preferred_element_type=F32)


def dot_t(left, right):
    return lax.dot_general(left, right, (((0,), (0,)), ((), ())), preferred_element_type=F32)


def dot_nt(left, right):
    return lax.dot_general(left, right, (((1,), (1,)), ((), ())), preferred_element_type=F32)


def elu(value):
    near = value + 0.5 * value * value
    below = jnp.where(value > -0.00390625, near, jnp.exp(jnp.minimum(value, 0.0)) - 1.0)
    return jnp.where(value > 0, value, below)


def elu_grad(value):
    return jnp.where(value > 0, 1.0, jnp.exp(jnp.minimum(value, 0.0)))


def iota(shape, dim):
    return lax.broadcasted_iota(jnp.int32, shape, dim)


def mult(value, step):
    return pl.multiple_of(value, step)


class Plan:
    def __init__(self, devices, slots, cap, horizon, flat_rows):
        self.n = devices
        self.line = devices // 4
        self.half = self.line // 2
        self.rows = flat_rows // devices
        self.slots = slots
        self.cap = cap
        self.horizon = horizon
        self.all_rows = cap * horizon
        self.step_rows = cap * (horizon - 1)
        self.lane = -(-max(2, 2 * slots // devices) // 16) * 16
        self.parts = max(1, min(4, self.rows // 2 // 32))
        self.part_rows = self.rows // 2 // self.parts
        self.items = self.half * self.parts
        self.cuts = max(1, min(GATHER_PARTS, self.rows // 2 // 16))
        self.bits = self.line.bit_length() - 1
        self.small = 8 * devices
        self.block = 256 if self.line <= 4 else 192


def kernel_body(plan, names, *refs):
    r = SimpleNamespace(**dict(zip(names, refs)))
    n, line, half, rows = plan.n, plan.line, plan.half, plan.rows
    cap, horizon, parts, prow = plan.cap, plan.horizon, plan.parts, plan.part_rows
    total, steps_rows, lane = plan.all_rows, plan.step_rows, plan.lane
    items, bits = plan.items, plan.bits
    me = lax.axis_index("dp")
    core = lax.axis_index("rep")
    z = me // 4
    a_step = 1 + core
    b_step = 2 - core
    a_bit = (me // a_step) % 2
    b_bit = (me // b_step) % 2
    a_dev = me + a_step * (1 - 2 * a_bit)
    b_dev = me + b_step * (1 - 2 * b_bit)
    q = me % 4
    q_a = a_dev % 4
    q_b = b_dev % 4
    q_ab = 3 - q
    sibling = 1 - core

    def remote(src, dst, send, recv, dev, on_core=None):
        return pltpu.make_async_remote_copy(
            src_ref=src,
            dst_ref=dst,
            send_sem=send,
            recv_sem=recv,
            device_id=(dev, core if on_core is None else on_core),
            device_id_type=MESH,
        )

    barrier = pltpu.get_barrier_semaphore()

    def greet(k, carry):
        pl.semaphore_signal(barrier, inc=1, device_id=((me + k) % n, core), device_id_type=MESH)
        return carry

    lax.fori_loop(1, n, greet, 0)
    pl.semaphore_signal(barrier, inc=1, device_id=(me, sibling), device_id_type=MESH)

    full = r.full
    own_rows = pl.ds(mult(me * rows + core * (rows // 2), 16), rows // 2)
    r.narrow[...] = r.weights[pl.ds(mult(core * rows * 2, 16), rows * 2)].astype(F32)
    for c in range(4):
        full[own_rows, 128 * c : 128 * (c + 1)] = r.narrow[pl.ds(c, rows // 2, stride=4), :].astype(BF16)

    slots = plan.slots
    lanes = n * lane
    tall = min(lanes, 256)

    def each(low, high, body):
        def step(k, carry):
            body(k)
            return carry

        lax.fori_loop(low, high, step, 0)

    pl.semaphore_wait(barrier, n)

    def lane_rows(k):
        return pl.ds(mult(k * lane, 16), lane)

    def exchange(width, sends, recvs):
        src, dst = r.sent, r.got

        def copy(k, to, into):
            return remote(
                src.at[lane_rows(to), 0:width], dst.at[lane_rows(into), 0:width], sends.at[k], recvs.at[k], to
            )

        def begin():
            dst[lane_rows(me), 0:width] = src[lane_rows(me), 0:width]
            each(1, n, lambda k: copy(k, (me + k) % n, me).start())

        def finish():
            each(1, n, lambda k: copy(k, me, (me + n - k) % n).wait_recv())

        def drain():
            each(1, n, lambda k: copy(k, (me + k) % n, me).wait_send())

        return begin, finish, drain

    out_begin, out_finish, out_drain = exchange(DET + META, r.ex_send, r.ex_recv)
    cuts = plan.cuts
    chunks = half * cuts
    crow = rows // 2 // cuts
    def bit_of(value, b):
        return (value // 2**b) % 2

    def across(b):
        return me + 4 * 2**b * (1 - 2 * bit_of(z, b))

    ahead = min(AHEAD, cuts)

    def item_at(i):
        i = jnp.where(z < half, i, jnp.where(i < ahead, chunks + i, jnp.where(i < ahead + chunks, i - ahead, i)))
        late = i // cuts
        group = late // half
        order = late % half
        place = z % half
        for b in range(bits - 1):
            place = place + bit_of(order, b) * 2**b * (1 - 2 * bit_of(z, b))
        return order, group * half + place, i % cuts

    def full_at(shard, piece, part):
        return full.at[pl.ds(mult(shard * rows + part * (rows // 2) + piece * crow, 16), crow)]

    def gather_copy(shard, piece, send, dev):
        view = full_at(shard, piece, core)
        return remote(view, view, send, r.ag_recv.at[shard, piece], dev)

    def share_copy(shard, piece, send, part=None):
        view = full_at(shard, piece, core if part is None else part)
        return remote(view, view, send, r.sh_recv.at[shard, piece], me, sibling)

    def far_copy(piece):
        return gather_copy(me, piece, r.far_send.at[piece], across(bits - 1))

    def plane_sends(zi, piece):
        mine = zi * 4 + q
        other = zi * 4 + q_a
        return (
            gather_copy(mine, piece, r.a_send.at[zi, piece], a_dev),
            gather_copy(mine, piece, r.b_send.at[zi, piece, 0], b_dev),
            gather_copy(other, piece, r.b_send.at[zi, piece, 1], b_dev),
        )

    def line_sends(order, zi, piece):
        return [
            (order < 2**b, gather_copy(zi * 4 + q, piece, r.line_send.at[zi, piece, b], across(b)))
            for b in range(bits - 1)
        ]

    def gather_line(i):
        order, zi, piece = item_at(i)

        @pl.when(zi != z)
        def _():
            gather_copy(zi * 4 + q, piece, r.a_send.at[zi, piece], me).wait_recv()

        for need, copy in line_sends(order, zi, piece):
            pl.when(need)(copy.start)
        to_a, to_b, _ = plane_sends(zi, piece)
        to_a.start()
        to_b.start()
        share_copy(zi * 4 + q, piece, r.sh_send.at[zi, piece, 0]).start()

    def gather_a(i):
        _, zi, piece = item_at(i)
        gather_copy(zi * 4 + q_a, piece, r.a_send.at[zi, piece], me).wait_recv()
        plane_sends(zi, piece)[2].start()
        share_copy(zi * 4 + q_a, piece, r.sh_send.at[zi, piece, 1]).start()

    def gather_b(i):
        _, zi, piece = item_at(i)
        for k, where in ((2, q_b), (3, q_ab)):
            gather_copy(zi * 4 + where, piece, r.a_send.at[zi, piece], me).wait_recv()
            share_copy(zi * 4 + where, piece, r.sh_send.at[zi, piece, k]).start()

    def gather_shared(i):
        zi, piece = i // cuts, i % cuts
        for k, where in ((0, q), (1, q_a), (2, q_b), (3, q_ab)):
            share_copy(zi * 4 + where, piece, r.sh_send.at[zi, piece, k], sibling).wait_recv()

    def gather_drain(i):
        zi, piece = i // cuts, i % cuts
        place, order = zi % half, 0
        for b in range(bits - 1):
            order = order + 2**b * ((bit_of(place, b) + bit_of(z, b)) % 2)
        for need, copy in line_sends(order, zi, piece):
            pl.when(need)(copy.wait_send)
        for copy in plane_sends(zi, piece):
            copy.wait_send()
        for k, where in ((0, q), (1, q_a), (2, q_b), (3, q_ab)):
            share_copy(zi * 4 + where, piece, r.sh_send.at[zi, piece, k]).wait_send()

    lag_a, lag_b = LAG_A, LAG_B
    all_chunks = 2 * chunks
    ticks = all_chunks + lag_b
    first_ticks = chunks + lag_b + jnp.where(z < half, 0, ahead)

    def gather_tick(k):
        pl.when(k < all_chunks)(lambda: gather_line(k))
        pl.when((k >= lag_a) & (k < all_chunks + lag_a))(lambda: gather_a(k - lag_a))
        pl.when((k >= lag_b) & (k < all_chunks + lag_b))(lambda: gather_b(k - lag_b))

    each(0, cuts, lambda piece: far_copy(piece).start())
    early = min(2, START_TICKS, chunks)
    each(0, early, gather_tick)

    route = r.route[...].astype(F32)
    used_row = (iota((1, slots), 1) < r.counts[...]).astype(F32)
    target_row = jnp.floor((route + 0.5) * (1.0 / cap))
    within_row = route - cap * target_row
    eye = iota((slots, slots), 0) == iota((slots, slots), 1)
    target_col = jnp.sum(jnp.where(eye, target_row, 0.0), axis=1, keepdims=True)
    used_col = jnp.sum(jnp.where(eye, used_row, 0.0), axis=1, keepdims=True)
    earlier = iota((slots, slots), 0) < iota((slots, slots), 1)
    same = jnp.where(earlier & (target_col == target_row), used_col, 0.0)
    rank_row = jnp.sum(same, axis=0, keepdims=True)
    column_row = jnp.where(used_row > 0, target_row * lane + rank_row, -1.0)

    def to_lanes(k):
        block = pl.ds(mult(k * tall, 16), tall)
        chosen_slot = column_row == (iota((tall, slots), 0) + k * tall).astype(F32)
        picked = jnp.where(chosen_slot, 1.0, 0.0).astype(BF16)
        r.to_lane[block] = picked
        place = jnp.sum(jnp.where(chosen_slot, within_row + 1.0, 0.0), axis=1, keepdims=True)
        marked = jnp.sum(
            jnp.where(chosen_slot, r.frame_mask[...].astype(F32), 0.0), axis=1, keepdims=True
        )
        meta_lane = iota((tall, META), 1)
        meta = jnp.where(meta_lane == 0, place, jnp.where(meta_lane == 1, marked, 0.0))
        r.sent[block, :DET] = dot(picked, r.start_deter[...]).astype(BF16)
        r.sent[block, DET:] = meta.astype(BF16)

    each(0, lanes // tall, to_lanes)


    hot, hot_t, act_hot = r.hot, r.hot_t, r.act_hot
    for t in range(horizon):
        r.latent_row[:, t * cap : (t + 1) * cap] = r.latent[t].astype(F32)
        r.action_row[:, t * cap : (t + 1) * cap] = r.action[t : t + 1].astype(F32)
    latent_row = r.latent_row[...].astype(BF16)
    spread_rows = (iota((LATENTS, STOCH), 1) // CLASSES == iota((LATENTS, STOCH), 0)).astype(F32).astype(BF16)
    class_row = (iota((1, STOCH), 1) % CLASSES).astype(F32)
    latent_col = latent_row.T
    for k in range(total // 128):
        seen = dot(latent_col[128 * k : 128 * (k + 1)], spread_rows)
        hot[128 * k : 128 * (k + 1)] = jnp.where(seen == class_row, 1.0, 0.0).astype(BF16)

    def hot_t_block(k):
        block = pl.ds(mult(k * 128, 128), 128)
        first = k * 128
        spread = ((iota((128, LATENTS), 0) + first) // CLASSES == iota((128, LATENTS), 1)).astype(F32).astype(BF16)
        seen = dot(spread, latent_row)
        class_col = ((iota((128, 1), 0) + first) % CLASSES).astype(F32)
        hot_t[block] = jnp.where(seen == class_col, 1.0, 0.0).astype(BF16)

    each(0, STOCH // 128, hot_t_block)
    act_hot[...] = jnp.where(r.action_row[...] == iota((128, total), 0).astype(F32), 1.0, 0.0).T.astype(BF16)

    r.embed_pad[...] = jnp.zeros((32, DET), BF16)
    r.embed_pad[0:ACTIONS] = r.act_embed[...]
    r.head_pad[...] = jnp.zeros((128, DET), BF16)
    r.head_pad[0:ACTIONS] = r.actor_head[...]
    r.small[...] = jnp.zeros(r.small.shape, F32)

    middle_ticks = min(START_TICKS, chunks + lag_b)
    each(early, middle_ticks, gather_tick)
    out_begin()
    each(middle_ticks, first_ticks, gather_tick)

    each(0, chunks, gather_shared)

    shuffle = r.shuffle
    row_i = iota((TALL, TALL), 0)
    shuffle[...] = jnp.where(
        iota((TALL, TALL), 1) == 3 * (row_i % 128) + row_i // 128, 1.0, 0.0
    ).astype(BF16)
    w_gru = r.w_gru
    for j in range(8):
        block = full[ROW_GRU + TALL * j : ROW_GRU + TALL * (j + 1)]
        sorted_rows = dot(shuffle[...], block).astype(BF16)
        for k in range(3):
            w_gru[128 * j : 128 * (j + 1), DET * k : DET * (k + 1)] = sorted_rows[128 * k : 128 * (k + 1)]
    w_back = full.at[ROW_GRU : ROW_GRU + GATES]
    pre, inputs, raw = r.pre, r.inputs, r.raw
    low, work = r.low, r.work
    a_one_at, a_two_at, g_one, g_two = 0, 2 * DET, 4 * DET, 6 * DET
    p_low = GATES
    inputs[steps_rows:total] = jnp.zeros((total - steps_rows, DET), BF16)
    pre_block = 5 * cap

    def pre_step(k):
        block = pl.ds(mult(k * pre_block, 16), pre_block)
        value = dot(hot[block], full[ROW_WIN : ROW_WIN + STOCH])
        value = value + dot(act_hot[block][:, 0:32], r.embed_pad[...])
        pre[block] = value
        active = elu(value).astype(BF16)
        inputs[block] = active
        raw[block] = dot(active, w_gru[0:DET])
        pl.when(z < half)(lambda: gather_tick(first_ticks + k))

    pre_blocks = (horizon - 1) // 5
    each(0, pre_blocks, pre_step)

    out_finish()
    r.start[...] = jnp.zeros((128, DET + META), F32)

    def from_lanes(k):
        block = pl.ds(mult(k * tall, 16), tall)
        got = r.got[block]
        put = jnp.where(got[:, DET : DET + 1].astype(F32) == (iota((tall, 128), 1) + 1).astype(F32), 1.0, 0.0).astype(BF16)
        r.placing[block] = put
        r.start[...] += dot_t(put, got)

    each(0, lanes // tall, from_lanes)
    start = r.start
    states_ref = r.states
    states_ref[0:cap] = start[0:cap, 0:DET]
    mask = start[0:cap, DET + 1 : DET + 2]
    eye = iota((cap, cap), 0) == iota((cap, cap), 1)
    mask_row = jnp.sum(jnp.where(eye, mask, 0.0), axis=0, keepdims=True)
    adv = r.adv
    running = jnp.zeros((1, cap), F32)
    sum_one = jnp.zeros((1, cap), F32)
    sum_two = jnp.zeros((1, cap), F32)
    for t in range(horizon - 1, -1, -1):
        running = r.rewards[t : t + 1] + discount * running
        sum_one = sum_one + mask_row * running
        sum_two = sum_two + mask_row * running * running
        r.returns[:, t * cap : (t + 1) * cap] = running
        r.weight_row[:, t * cap : (t + 1) * cap] = mask_row * (1.0 / horizon)
    tile_lane = iota((8, 128), 1)

    def total_of(value):
        return jnp.sum(value, axis=1, keepdims=True)

    sums = jnp.where(
        tile_lane == 0,
        total_of(sum_one),
        jnp.where(tile_lane == 1, total_of(sum_two), jnp.where(tile_lane == 2, horizon * total_of(mask_row), 0.0)),
    )
    moments, pair = r.moments, r.pair
    pair[0] = sums
    swap = remote(pair.at[0], pair.at[1], r.pair_sem.at[0], r.pair_sem.at[1], me, sibling)
    swap.start()

    def moments_copy(k):
        peer = (me + k) % n
        return remote(moments.at[me], moments.at[me], r.mo_send.at[k], r.mo_recv.at[k], peer)

    def moments_landing(k):
        peer = (me + n - k) % n
        return remote(moments.at[peer], moments.at[peer], r.mo_send.at[k], r.mo_recv.at[k], peer)


    def as_row(ref):
        value = ref[...].astype(F32)
        return jnp.concatenate([value[k : k + 1] for k in range(ref.shape[0])], axis=-1)

    gain = as_row(r.gain)
    bias = as_row(r.bias)
    update_ref, inv_ref = r.update, r.inv

    each(0, chunks, gather_drain)
    each(0, cuts, lambda piece: pl.when(z < half)(far_copy(piece).wait_send))
    scan_first = first_ticks + jnp.where(z < half, pre_blocks, 0)

    def forward_step(t):
        block = pl.ds(mult(t * cap, 16), cap)
        state = states_ref[block]
        state_low = state.astype(BF16)
        low[block] = state_low
        gru_raw = raw[block] + dot(state_low, w_gru[DET:])
        centred = gru_raw - jnp.mean(gru_raw, axis=-1, keepdims=True)
        inv_std = lax.rsqrt(jnp.mean(centred * centred, axis=-1, keepdims=True) + norm_eps)
        normed = centred * inv_std
        raw[block] = normed
        inv_ref[block] = jnp.broadcast_to(inv_std, (cap, 128))
        mixed = normed * gain + bias
        reset = jax.nn.sigmoid(mixed[:, :DET])
        candidate = jnp.tanh(reset * mixed[:, DET : 2 * DET])
        update = jax.nn.sigmoid(mixed[:, 2 * DET :] - 1.0)
        update_ref[block] = update
        states_ref[pl.ds(mult(t * cap + cap, 16), cap)] = update * candidate + (1.0 - update) * state
        j, k = t % 12 // 3, t % 3
        w_back[pl.ds(mult(DET * k, DET), DET), pl.ds(mult(128 * j, 128), 128)] = w_gru[
            pl.ds(mult(DET + 128 * j, 128), 128), pl.ds(mult(DET * k, DET), DET)
        ].T

    group = 3 if (horizon - 1) % 3 == 0 else 1
    rounds = (horizon - 1) // group

    def forward_round(m):
        for k in range(group):
            forward_step(m * group + k)
        gather_tick(scan_first + m)

    each(0, 1, forward_round)
    swap.wait()
    moments[me] = pair[0] + pair[1]
    each(1, n, lambda k: moments_copy(k).start())
    each(1, rounds, forward_round)
    each(1, n, lambda k: moments_landing(k).wait_recv())
    sums = moments[0]
    for k in range(1, n):
        sums = sums + moments[k]
    centre = sums[0:1, 0:1] / sums[0:1, 2:3]
    spread = jnp.sqrt(sums[0:1, 1:2] / sums[0:1, 2:3] - centre * centre + norm_eps)
    per_row = jnp.concatenate(
        [(r.returns[...] - centre) / spread, r.weight_row[...], jnp.zeros((126, total), F32)], axis=0
    ).T
    adv[...] = per_row

    done_ticks = scan_first + rounds
    each(done_ticks, jnp.maximum(ticks, done_ticks), gather_tick)
    low[steps_rows:total] = states_ref[steps_rows:total].astype(BF16)
    each(chunks, 2 * chunks, gather_shared)

    grads = r.grads

    def keep_grads(first, value):
        for c in range(4):
            grads[c, pl.ds(first, value.shape[0])] = value[:, 128 * c : 128 * (c + 1)]

    def load_grads(block):
        return jnp.concatenate([grads[c, block] for c in range(4)], axis=-1)

    def grad_rows(local, part, piece):
        return pl.ds(mult(local * rows + part * (rows // 2) + piece * prow, 16), prow)

    def store_grads(block, value):
        for c in range(4):
            grads[c, block] = value[:, 128 * c : 128 * (c + 1)]

    pair_in, b_in, a_in, z_in = r.pair_in, r.b_in, r.a_in, r.z_in

    class Reducer:
        def __init__(self, group):
            self.group = group
            self.turn = half // 2 if group == 0 else 0

        def target(self, i):
            return (i // parts + self.turn) % half, i % parts

        def sem(self, array, *at):
            return array.at[(self.group,) + at]

        def out_rows(self, t, offset, piece, count):
            return pl.ds(mult(ROW_A1 + t * 4 * rows + offset + piece * count * prow, 16), count * prow)

        def in_rows(self, t, piece, count):
            return pl.ds(mult((t * parts + piece) * count * prow, 16), count * prow)

        def pair_copy(self, t, piece):
            return remote(
                full.at[self.out_rows(t, 0, piece, 4)],
                pair_in.at[self.in_rows(t, piece, 4)],
                self.sem(r.pair_s, t, piece),
                self.sem(r.pair_r, t, piece),
                me,
                sibling,
            )

        def b_copy(self, t, piece):
            return remote(
                full.at[self.out_rows(t, 2 * rows, piece, 2)],
                b_in.at[self.group, self.in_rows(t, piece, 2)],
                self.sem(r.b_s, t, piece),
                self.sem(r.b_r, t, piece),
                b_dev,
            )

        def a_copy(self, t, piece):
            return remote(
                full.at[self.out_rows(t, 3 * rows, piece, 1)],
                a_in.at[self.group, self.in_rows(t, piece, 1)],
                self.sem(r.a_s, t, piece),
                self.sem(r.a_r, t, piece),
                a_dev,
            )

        def z_slot(self, b, t):
            return sum(half // 2 ** (k + 1) for k in range(b)) + t // 2 ** (b + 1)

        def z_copy(self, b, t, piece):
            slot = self.z_slot(b, t)
            return remote(
                full.at[self.out_rows(t, 3 * rows + rows // 2, piece, 1)],
                z_in.at[self.group, self.in_rows(slot, piece, 1)],
                self.sem(r.z_s, t, piece),
                self.sem(r.z_r, slot, piece),
                across(b),
            )

        def holds(self, b, t):
            return (z - t - self.group * half) % 2**b == 0

        def differs(self, b, t):
            return bit_of(z, b) != bit_of(t + self.group * half, b)

        def fin_rows(self, piece, part):
            return pl.ds(mult((part * (rows // 2) + piece * prow) * 4, 16), prow * 4)

        def fin_copy(self, piece, part=None):
            block = self.fin_rows(piece, core if part is None else part)
            return remote(
                r.weights_grad.at[block], r.weights_grad.at[block], r.fin_s.at[piece], r.fin_r.at[piece], me, sibling
            )

        def load(self, t, piece, a):
            if self.group == 0:
                return load_grads(grad_rows(t * 4 + a * a_step + b_bit * b_step, core, piece))
            return r.kept[(t * parts + piece) * 2 + a]

        def store(self, t, piece, a, value):
            if self.group == 0:
                store_grads(grad_rows(t * 4 + a * a_step + b_bit * b_step, core, piece), value)
            else:
                r.kept[(t * parts + piece) * 2 + a] = value

        def to_pair(self, i):
            t, piece = self.target(i)
            for k in range(4):
                block = pl.ds(mult(ROW_A1 + t * 4 * rows + (piece * 4 + k) * prow, 16), prow)
                full[block] = load_grads(grad_rows(t * 4 + k, sibling, piece)).astype(BF16)
            self.pair_copy(t, piece).start()

        def to_b(self, i):
            t, piece = self.target(i)
            self.pair_copy(t, piece).wait_recv()

            def both_cores(where):
                spot = pl.ds(mult(((t * parts + piece) * 4 + where) * prow, 16), prow)
                return load_grads(grad_rows(t * 4 + where, core, piece)) + pair_in[spot].astype(F32)

            for a in range(2):
                block = pl.ds(mult(ROW_A1 + t * 4 * rows + 2 * rows + (piece * 2 + a) * prow, 16), prow)
                full[block] = both_cores(a * a_step + (1 - b_bit) * b_step).astype(BF16)
            self.b_copy(t, piece).start()
            for a in range(2):
                self.store(t, piece, a, both_cores(a * a_step + b_bit * b_step))

        def b_part(self, t, piece, a):
            spot = pl.ds(mult(((t * parts + piece) * 2 + a) * prow, 16), prow)
            return b_in[self.group, spot].astype(F32)

        def to_a(self, i):
            t, piece = self.target(i)
            self.b_copy(t, piece).wait_recv()
            other = 1 - a_bit
            if self.group == 0:
                heads_rs.a_copy(t, piece).wait_send()
            full[self.out_rows(t, 3 * rows, piece, 1)] = (
                self.load(t, piece, other) + self.b_part(t, piece, other)
            ).astype(BF16)
            self.a_copy(t, piece).start()
            self.store(t, piece, a_bit, self.load(t, piece, a_bit) + self.b_part(t, piece, a_bit))

        def to_plane(self, b, i):
            t, piece = self.target(i)

            @pl.when(self.holds(b, t))
            def _():
                if b == 0:
                    self.a_copy(t, piece).wait_recv()
                    came = a_in[self.group, self.in_rows(t, piece, 1)]
                else:
                    self.z_copy(b - 1, t, piece).wait_recv()
                    came = z_in[self.group, self.in_rows(self.z_slot(b - 1, t), piece, 1)]
                value = self.load(t, piece, a_bit) + came.astype(F32)
                if b == bits:
                    first = mult((core * (rows // 2) + piece * prow) * 4, 16)
                    for c in range(4):
                        r.weights_grad[pl.ds(first + c, prow, stride=4), :] = value[:, 128 * c : 128 * (c + 1)]
                    self.fin_copy(piece).start()
                else:

                    @pl.when(self.differs(b, t))
                    def _():
                        if self.group == 0:
                            heads_rs.plane_gone(t, piece)
                        full[self.out_rows(t, 3 * rows + rows // 2, piece, 1)] = value.astype(BF16)
                        self.z_copy(b, t, piece).start()

                    pl.when(~self.differs(b, t))(lambda: self.store(t, piece, a_bit, value))

        def drain_early(self, i):
            t, piece = self.target(i)
            self.pair_copy(t, piece).wait_send()
            self.b_copy(t, piece).wait_send()

        def plane_gone(self, t, piece):
            for b in range(bits):
                pl.when(self.holds(b, t) & self.differs(b, t))(self.z_copy(b, t, piece).wait_send)

        def drain(self, i):
            t, piece = self.target(i)
            if self.group == 0:
                self.a_copy(t, piece).wait_send()
                self.plane_gone(t, piece)
            else:
                for b in range(bits):
                    waited = False
                    for c in range(bits):
                        waited = waited | (gru_rs.holds(c, t) & gru_rs.differs(c, t))
                    pl.when(self.holds(b, t) & self.differs(b, t) & ~waited)(self.z_copy(b, t, piece).wait_send)

            @pl.when(self.holds(bits, t))
            def _():
                self.fin_copy(piece).wait_send()
                self.fin_copy(piece, sibling).wait_recv()

    heads_rs, gru_rs = Reducer(1), Reducer(0)
    net_items = items // 2

    def of_item(k, stage):
        pl.when((k >= 0) & (k < items))(lambda: stage(heads_rs, k))
        pl.when((k >= items) & (k < 2 * items))(lambda: stage(gru_rs, k - items))

    def rs_tick(k):
        of_item(k, lambda rs, i: rs.to_a(i))
        for b in range(bits + 1):
            of_item(k - LAG_Z * (b + 1), lambda rs, i, b=b: rs.to_plane(b, i))

    rs_ticks = 2 * items + LAG_Z * (bits + 1)

    out_grads, state_grads = r.out_grads, r.state_grads
    r.loss_acc[...] = jnp.zeros((plan.block, 128), F32)
    critic_row = as_row(r.critic_head)
    lane_id = iota((plan.block, 128), 1)

    def net_rows(side):
        return (ROW_A1, ROW_A2) if side == 0 else (ROW_C1, ROW_C2)

    def net_cols(base, side):
        return slice(base + side * DET, base + (side + 1) * DET)

    def net_step(k, side):
        first, second = net_rows(side)
        block = pl.ds(mult(k * plan.block, 64), plan.block)
        one = dot(low[block], full[first : first + DET]) + dot(hot[block], full[first + DET : first + DET + STOCH])
        one_low = elu(one).astype(BF16)
        work[block, net_cols(a_one_at, side)] = one_low
        two = dot(one_low, full[second : second + DET])
        two_low = elu(two).astype(BF16)
        work[block, net_cols(a_two_at, side)] = two_low
        advantage = adv[block][:, 0:1]
        weight = adv[block][:, 1:2]
        if side == 0:
            real = lane_id < ACTIONS
            logits = jnp.where(real, dot_nt(two_low, r.head_pad[...]), -1e30)
            shifted = logits - jnp.max(logits, axis=-1, keepdims=True)
            powers = jnp.where(real, jnp.exp(shifted), 0.0)
            norm = jnp.sum(powers, axis=-1, keepdims=True)
            log_probs = jnp.where(real, shifted - jnp.log(norm), 0.0)
            probs = powers / norm
            taken = act_hot[block].astype(F32)
            chosen = jnp.sum(taken * log_probs, axis=-1, keepdims=True)
            entropy = -jnp.sum(probs * log_probs, axis=-1, keepdims=True)
            r.loss_acc[...] += weight * (-advantage * chosen - entropy_weight * entropy)
            grad_logits = weight * (
                -advantage * (taken - probs) + entropy_weight * probs * (log_probs + entropy)
            )
            both = grad_logits.astype(BF16)
            out_grads[block] = both
            back = dot(both, r.head_pad[...])
        else:
            value = jnp.sum(two_low.astype(F32) * critic_row, axis=-1, keepdims=True)
            gap = value - advantage
            r.loss_acc[...] += weight * (0.5 * gap * gap)
            value_low = (weight * gap).astype(BF16).astype(F32)
            out_grads[block] = jnp.where(lane_id == ACTIONS, value_low, out_grads[block].astype(F32)).astype(BF16)
            back = value_low * critic_row
        back_low = (back * elu_grad(two)).astype(BF16)
        work[block, net_cols(g_two, side)] = back_low
        low_one = (dot_nt(back_low, full[second : second + DET]) * elu_grad(one)).astype(BF16)
        work[block, net_cols(g_one, side)] = low_one
        state_part = dot_nt(low_one, full[first : first + DET])
        if side == 0:
            state_grads[block] = state_part
        else:
            state_grads[block] += state_part

    def net_grads(side):
        base = side * 2048
        for j in range(2):
            part = slice(j * WIDE, (j + 1) * WIDE)
            keep_grads(base + j * WIDE, dot_t(low[:, part], work[:, net_cols(g_one, side)]))
            at = a_one_at + side * DET + j * WIDE
            keep_grads(base + GATES + j * WIDE, dot_t(work[:, at : at + WIDE], work[:, net_cols(g_two, side)]))

        def latent_part(k):
            part = pl.ds(mult(k * WIDE, WIDE), WIDE)
            keep_grads(mult(base + DET + k * WIDE, WIDE), dot(hot_t[part], work[:, net_cols(g_one, side)]))

        each(0, STOCH // WIDE, latent_part)

    blocks = total // plan.block
    each(0, blocks, lambda k: net_step(k, 0))
    net_grads(0)
    each(chunks, 2 * chunks, gather_drain)
    each(0, cuts, lambda piece: pl.when(z >= half)(far_copy(piece).wait_send))
    each(0, net_items, heads_rs.to_pair)
    net_step(0, 1)
    each(0, net_items, heads_rs.to_b)
    each(1, blocks, lambda k: net_step(k, 1))
    each(0, net_items // 2, rs_tick)
    net_grads(1)
    each(net_items, items, heads_rs.to_pair)
    each(net_items // 2, net_items, rs_tick)

    small = r.small
    head_grad = dot_t(out_grads[...], work[:, a_two_at : a_two_at + 2 * DET])
    small[SM_ACTOR : SM_ACTOR + 24] = head_grad[0:24, 0:WIDE]
    small[SM_ACTOR + 24 : SM_ACTOR + 48] = head_grad[0:24, WIDE:DET]
    small[SM_CRITIC : SM_CRITIC + 1] = head_grad[ACTIONS : ACTIONS + 1, DET : DET + WIDE]
    small[SM_CRITIC + 1 : SM_CRITIC + 2] = head_grad[ACTIONS : ACTIONS + 1, DET + WIDE :]
    small[SM_LOSS : SM_LOSS + 1, 0:128] = jnp.sum(r.loss_acc[...], axis=0, keepdims=True)

    scan_ticks = net_items + rounds - 1

    gain_acc, bias_acc = r.gain_acc, r.bias_acc
    gain_acc[...] = jnp.zeros((8, GATES), F32)
    bias_acc[...] = jnp.zeros((8, GATES), F32)
    carry_ref = r.carry
    carry_ref[...] = state_grads[steps_rows:total]
    work[steps_rows:total, 0 : 4 * DET] = jnp.zeros((total - steps_rows, 4 * DET), BF16)
    gain_mid, bias_mid = gain[:, DET : 2 * DET], bias[:, DET : 2 * DET]

    def fold(value):
        out = value[0:8]
        for k in range(1, cap // 8):
            out = out + value[8 * k : 8 * (k + 1)]
        return out

    def backward_step(index):
        t = horizon - 2 - index
        block = pl.ds(mult(t * cap, 16), cap)
        carry = carry_ref[...]
        normed = raw[block]
        inv_std = inv_ref[block][:, 0:1]
        reset = jax.nn.sigmoid(normed[:, :DET] * gain[:, :DET] + bias[:, :DET])
        update = update_ref[block]
        state = states_ref[block]
        middle = normed[:, DET : 2 * DET] * gain_mid + bias_mid
        candidate = jnp.tanh(reset * middle)
        inner = carry * update * (1.0 - candidate * candidate)
        part = jnp.concatenate(
            [
                inner * middle * reset * (1.0 - reset),
                inner * reset,
                carry * (candidate - state) * update * (1.0 - update),
            ],
            axis=-1,
        )
        gain_acc[...] += fold(part * normed)
        bias_acc[...] += fold(part)
        normed_grad = part * gain
        raw_grad = inv_std * (
            normed_grad
            - jnp.mean(normed_grad, axis=-1, keepdims=True)
            - normed * jnp.mean(normed_grad * normed, axis=-1, keepdims=True)
        )
        grad_low = raw_grad.astype(BF16)
        work[block, 0:GATES] = grad_low
        carry_ref[...] = carry * (1.0 - update) + dot(grad_low, w_back[...]) + state_grads[block]

    def backward_round(m):
        pl.when(m == 0)(lambda: each(net_items, items, heads_rs.to_b))
        for k in range(group):
            backward_step(m * group + k)
        pl.when(m > 0)(lambda: rs_tick(net_items + m - 1))

    each(0, rounds, backward_round)

    back_begin, back_finish, back_drain = exchange(DET, r.bk_send, r.bk_recv)
    out_drain()
    start_grads = carry_ref[...].astype(BF16)

    def back_lanes(k):
        block = pl.ds(mult(k * tall, 16), tall)
        r.sent[block, :DET] = dot(r.placing[block][:, 0:cap], start_grads).astype(BF16)

    each(0, lanes // tall, back_lanes)
    back_begin()

    each(0, items, heads_rs.drain_early)
    pl.semaphore_signal(r.credit, inc=1, device_id=(me, sibling), device_id_type=MESH)
    def gru_part(j):
        source = inputs if j < 2 else low
        part = slice((j % 2) * WIDE, (j % 2 + 1) * WIDE)
        for k in range(3):
            value = dot_t(source[:, part], work[:, DET * k : DET * (k + 1)])
            for c in range(4):
                grads[c, pl.ds(ROW_GRU + k + 768 * j, WIDE, stride=3), :] = value[:, 128 * c : 128 * (c + 1)]

    for j in (3, 2, 1):
        gru_part(j)
    pl.semaphore_wait(r.credit, 1)
    each(0, net_items, gru_rs.to_pair)

    def pre_back(k):
        block = pl.ds(mult(k * pre_block, 16), pre_block)
        value = dot_nt(work[block, 0:GATES], w_gru[0:DET])
        work[block, p_low : p_low + DET] = (value * elu_grad(pre[block])).astype(BF16)

    each(0, pre_blocks, pre_back)
    ready = min(scan_ticks, items)
    each(ready, items, rs_tick)
    ready = max(ready, items)
    each(0, net_items, gru_rs.to_b)
    gru_part(0)

    def win_part(k):
        part = pl.ds(mult(k * WIDE, WIDE), WIDE)
        keep_grads(mult(k * WIDE, WIDE), dot(hot_t[part], work[:, p_low : p_low + DET]))

    each(0, STOCH // WIDE, win_part)
    each(net_items, items, gru_rs.to_pair)
    step_ticks = max(net_items // 4, 1)
    each(ready, ready + step_ticks, rs_tick)
    each(net_items, items, gru_rs.to_b)
    each(ready + step_ticks, ready + 2 * step_ticks, rs_tick)
    ready += 2 * step_ticks
    embed_grad = dot_t(act_hot[...], work[:, p_low : p_low + DET])
    small[SM_EMBED : SM_EMBED + 24] = embed_grad[0:24, 0:WIDE]
    small[SM_EMBED + 24 : SM_EMBED + 48] = embed_grad[0:24, WIDE:DET]
    gain_sum = jnp.sum(gain_acc[...], axis=0, keepdims=True)
    bias_sum = jnp.sum(bias_acc[...], axis=0, keepdims=True)
    for k in range(GATES // WIDE):
        small[SM_GAIN + k : SM_GAIN + k + 1] = gain_sum[:, k * WIDE : (k + 1) * WIDE]
        small[SM_BIAS + k : SM_BIAS + k + 1] = bias_sum[:, k * WIDE : (k + 1) * WIDE]

    small_in, scattered = r.small_in, r.scattered
    summed = small_in
    swap_small = remote(small, small_in, r.pair_sem.at[2], r.pair_sem.at[3], me, sibling)
    small_sum = small

    def eight(k):
        return pl.ds(mult(k * 8, 8), 8)

    def scatter_copy(k):
        peer = (me + k) % n
        return remote(small_sum.at[eight(peer)], scattered.at[me], r.sc_send.at[k], r.sc_recv.at[k], peer)

    def scatter_landing(k):
        peer = (me + n - k) % n
        return remote(small_sum.at[eight(me)], scattered.at[peer], r.sc_send.at[k], r.sc_recv.at[k], peer)

    def summed_copy(k):
        peer = (me + k) % n
        return remote(summed.at[eight(me)], summed.at[eight(me)], r.sm_send.at[k], r.sm_recv.at[k], peer)

    def summed_landing(k):
        peer = (me + n - k) % n
        return remote(summed.at[eight(peer)], summed.at[eight(peer)], r.sm_send.at[k], r.sm_recv.at[k], peer)

    def scatter_small():
        swap_small.wait()
        small_sum[...] = small[...] + small_in[...]
        scattered[me] = small_sum[eight(me)]
        each(1, n, lambda k: scatter_copy(k).start())

    def spread_small():
        each(1, n, lambda k: scatter_landing(k).wait_recv())
        block_sum = scattered[0]
        for k in range(1, n):
            block_sum = block_sum + scattered[k]
        summed[eight(me)] = block_sum
        each(1, n, lambda k: summed_copy(k).start())

    swap_small.start()
    between = (SCATTER_TICKS, scatter_small), (SPREAD_TICKS, spread_small)
    for before_end, run in between:
        until = max(ready, rs_ticks - before_end)
        each(ready, until, rs_tick)
        ready = until
        run()
    each(ready, rs_ticks, rs_tick)
    each(0, items, heads_rs.drain)

    back_finish()
    r.start_grad[...] = jnp.zeros((slots, DET), F32)

    def frames(k):
        block = pl.ds(mult(k * tall, 16), tall)
        r.start_grad[...] += dot_t(r.to_lane[block], r.got[block][:, 0:DET])

    each(0, lanes // tall, frames)
    each(1, n, lambda k: summed_landing(k).wait_recv())
    r.loss[...] = summed[SM_LOSS : SM_LOSS + 1, 0:1]
    r.embed_grad[:, 0:WIDE] = summed[SM_EMBED : SM_EMBED + ACTIONS]
    r.embed_grad[:, WIDE:DET] = summed[SM_EMBED + 24 : SM_EMBED + 24 + ACTIONS]
    for k in range(GATES // WIDE):
        for h in range(2):
            lanes_of = slice(h * 128, (h + 1) * 128)
            r.gain_grad[2 * k + h : 2 * k + h + 1] = summed[SM_GAIN + k : SM_GAIN + k + 1, lanes_of]
            r.bias_grad[2 * k + h : 2 * k + h + 1] = summed[SM_BIAS + k : SM_BIAS + k + 1, lanes_of]
    for k in range(2):
        for h in range(2):
            lanes_of = slice(h * 128, (h + 1) * 128)
            r.critic_grad[2 * k + h : 2 * k + h + 1] = summed[SM_CRITIC + k : SM_CRITIC + k + 1, lanes_of]
    r.actor_grad[:, 0:WIDE] = summed[SM_ACTOR : SM_ACTOR + ACTIONS]
    r.actor_grad[:, WIDE:DET] = summed[SM_ACTOR + 24 : SM_ACTOR + 24 + ACTIONS]
    each(0, items, gru_rs.drain_early)
    each(0, items, gru_rs.drain)

    back_drain()
    each(1, n, lambda k: moments_copy(k).wait_send())
    each(1, n, lambda k: scatter_copy(k).wait_send())
    each(1, n, lambda k: summed_copy(k).wait_send())


def hand_over(*refs):
    count = len(refs) // 2
    for k in range(count):
        refs[count + k][...] = refs[k][...]


def on_device(
    start_deter,
    frame_mask,
    counts,
    route,
    weights_flat,
    act_embed,
    gru_gain,
    gru_bias,
    actor_head,
    critic_head,
    latent_idx,
    action_idx,
    rewards,
):
    n = lax.axis_size("dp")
    slots = start_deter.shape[0]
    cap, horizon = action_idx.shape
    shard = weights_flat.shape[0]
    plan = Plan(n, slots, cap, horizon, shard * n // DET)
    total, steps_rows, lanes = plan.all_rows, plan.step_rows, n * plan.lane
    line, half, parts, prow, items = plan.line, plan.half, plan.parts, plan.part_rows, plan.items
    inputs = dict(
        start_deter=start_deter,
        frame_mask=frame_mask.reshape(1, slots),
        counts=counts.reshape(1, 1),
        route=route.reshape(1, slots),
        weights=weights_flat.reshape(plan.rows * 4, 128),
        act_embed=act_embed,
        gain=gru_gain.reshape(GATES // 128, 128),
        bias=gru_bias.reshape(GATES // 128, 128),
        actor_head=actor_head.T,
        critic_head=critic_head.reshape(DET // 128, 128),
        latent=jnp.transpose(latent_idx, (1, 2, 0)),
        action=action_idx.T,
        rewards=rewards.T,
    )
    outputs = dict(
        loss=(1, 1),
        start_grad=(slots, DET),
        weights_grad=(plan.rows * 4, 128),
        embed_grad=(ACTIONS, DET),
        gain_grad=(GATES // 128, 128),
        bias_grad=(GATES // 128, 128),
        actor_grad=(ACTIONS, DET),
        critic_grad=(DET // 128, 128),
    )
    group_rows = half * 4 * plan.rows
    half_rows = group_rows // 2
    scratch = dict(
        narrow=((plan.rows * 2, 128), F32),
        latent_row=((LATENTS, total), F32),
        action_row=((1, total), F32),
        returns=((1, total), F32),
        weight_row=((1, total), F32),
        kept=((2 * items, prow, DET), F32),
        full=((n * plan.rows, DET), BF16),
        start=((128, DET + META), F32),
        to_lane=((lanes, slots), BF16),
        sent=((lanes, DET + META), BF16),
        got=((lanes, DET + META), BF16),
        placing=((lanes, 128), BF16),
        hot=((total, STOCH), BF16),
        hot_t=((STOCH, total), BF16),
        act_hot=((total, 128), BF16),
        embed_pad=((32, DET), BF16),
        head_pad=((128, DET), BF16),
        small=((plan.small, WIDE), F32),
        small_in=((plan.small, WIDE), F32),
        scattered=((n, 8, WIDE), F32),
        states=((total, DET), F32),
        adv=((total, 128), F32),
        pair=((2, 8, 128), F32),
        moments=((n, 8, 128), F32),
        shuffle=((TALL, TALL), BF16),
        w_gru=((STOCH, GATES), BF16),
        pre=((steps_rows, DET), F32),
        inputs=((total, DET), BF16),
        work=((total, 8 * DET), BF16),
        raw=((steps_rows, GATES), F32),
        low=((total, DET), BF16),
        update=((steps_rows, DET), F32),
        inv=((steps_rows, 128), F32),
        out_grads=((total, 128), BF16),
        state_grads=((total, DET), F32),
        loss_acc=((plan.block, 128), F32),
        grads=((4, group_rows, 128), F32),
        pair_in=((half_rows, DET), BF16),
        b_in=((2, half_rows // 2, DET), BF16),
        a_in=((2, half_rows // 4, DET), BF16),
        z_in=((2, half_rows // 4, DET), BF16),
        gain_acc=((8, GATES), F32),
        bias_acc=((8, GATES), F32),
        carry=((cap, DET), F32),
    )
    semaphores = dict(
        ex_send=(n,),
        ex_recv=(n,),
        bk_send=(n,),
        bk_recv=(n,),
        mo_send=(n,),
        mo_recv=(n,),
        sc_send=(n,),
        sc_recv=(n,),
        sm_send=(n,),
        sm_recv=(n,),
        pair_sem=(4,),
        ag_recv=(n, plan.cuts),
        sh_recv=(n, plan.cuts),
        far_send=(plan.cuts,),
        line_send=(line, plan.cuts, max(plan.bits - 1, 1)),
        a_send=(line, plan.cuts),
        b_send=(line, plan.cuts, 2),
        sh_send=(line, plan.cuts, 4),
        pair_s=(2, half, parts),
        pair_r=(2, half, parts),
        b_s=(2, half, parts),
        b_r=(2, half, parts),
        a_s=(2, half, parts),
        a_r=(2, half, parts),
        z_s=(2, half, parts),
        z_r=(2, half, parts),
        fin_s=(parts,),
        fin_r=(parts,),
    )
    names = list(inputs) + list(outputs) + list(scratch) + list(semaphores) + list(dict(credit=0))
    vmem = pl.BlockSpec(memory_space=pltpu.VMEM)
    found = pl.pallas_call(
        functools.partial(kernel_body, plan, names),
        out_shape=[jax.ShapeDtypeStruct(shape, F32) for shape in outputs.values()],
        in_specs=[vmem] * len(inputs),
        out_specs=[vmem] * len(outputs),
        scratch_shapes=[pltpu.VMEM(shape, dtype) for shape, dtype in scratch.values()]
        + [pltpu.SemaphoreType.DMA(shape) for shape in semaphores.values()]
        + [pltpu.SemaphoreType.REGULAR],
        compiler_params=pltpu.CompilerParams(
            collective_id=0, has_side_effects=True, vmem_limit_bytes=127 * 2**19
        ),
    )(*inputs.values())
    found = pl.pallas_call(
        hand_over,
        out_shape=[jax.ShapeDtypeStruct(shape, F32) for shape in outputs.values()],
        in_specs=[vmem] * len(outputs),
        out_specs=[vmem] * len(outputs),
    )(*found)
    loss, start_grad, weights_grad, embed_grad, gain_grad, bias_grad, actor_grad, critic_grad = found
    return (
        loss.reshape(()),
        start_grad,
        weights_grad.reshape(shard),
        embed_grad,
        gain_grad.reshape(GATES),
        bias_grad.reshape(GATES),
        actor_grad.T,
        critic_grad.reshape(DET),
    )


def solution(mesh):
    return jax.shard_map(
        on_device,
        mesh=mesh,
        in_specs=(
            P(("dp", "rep"), None),
            P(("dp", "rep")),
            P(("dp", "rep")),
            P(("dp", "rep")),
            P("dp"),
            P(),
            P(),
            P(),
            P(),
            P(),
            P(("dp", "rep"), None, None),
            P(("dp", "rep"), None),
            P(("dp", "rep"), None),
        ),
        out_specs=(P(), P(("dp", "rep"), None), P("dp"), P(), P(), P(), P(), P()),
        check_vma=False,
    )
```
